32 devices in a mesh: section: 2 (over y), dp: 16 (over z, x, core).
Axes of the slice: x: 2, y: 2, z: 4, core: 2. Of those that a mesh axis runs over, the one named last changes fastest.
Arguments:
- acts: bfloat16 [32, 256, 768], P('dp'), may hold values from -6 to 6
- counts: int32 [32], P('dp'), may hold values from 38 to 256, as said below
- cotangent: bfloat16 [32, 256, 768], P('dp'), may hold values from -6 to 6
- norm_gains: float32 [2, 2, 768], P('section'), may hold values from 0.5 to 1.5
- w_qkv: bfloat16 [2, 768, 2304], P('section'), may hold values from -0.3125 to 0.3125
- w_out: bfloat16 [2, 768, 768], P('section'), may hold values from -0.625 to 0.625
- w_up: bfloat16 [2, 768, 3072], P('section'), may hold values from -0.21875 to 0.21875
- w_down: bfloat16 [2, 3072, 768], P('section'), may hold values from -0.109375 to 0.109375
Outputs:
- ends: float32 [2, 32, 256, 768], P('section', 'dp')
- grad_gains: float32 [2, 2, 768], P('section', None, 'dp')
- grad_qkv: float32 [2, 768, 2304], P('section', 'dp')
- grad_out: float32 [2, 768, 768], P('section', 'dp')
- grad_up: float32 [2, 768, 3072], P('section', 'dp')
- grad_down: float32 [2, 3072, 768], P('section', 'dp')
The draws below stay inside these ranges and needn't reach their ends.
Inputs may be any that keep to these rules, and one draw needn't show every extreme that they name: In every draw one cell holds all 256 genes; the other counts are drawn independently.
All inputs are finite; a program needn't handle non-finite values.
Results may differ from the reference program's by a relative error of at most 0.03.
The reference program's roundings to bfloat16 on the way count: a program that leaves them out, or rounds other values in their place, can miss the bound.
Values may be sent and summed in bfloat16 or wider, within the bound.
A program may use at most 192 MiB of HBM per device.

```python
import jax
import jax.numpy as jnp
from jax import lax

D = 768
HEADS = 12
HD = 64
FF = 3072
LEN = 256
CELLS = 32
N_SECTION = 2


def draw_counts(key, part):
    key = jax.random.fold_in(key, 11)
    lengths_key, full_key = jax.random.split(key)
    lowest = LEN * 75 // 512 + 1
    lengths = jax.random.randint(lengths_key, (CELLS,), lowest, LEN + 1)
    full_cell = jax.random.randint(full_key, (), 0, CELLS)
    return jnp.where(jnp.arange(CELLS) == full_cell, LEN, lengths).astype(jnp.int32)


def steps_of(own_key, dims, cuts, least, largest):
    factor_of, own = 1.0, jax.random.fold_in(own_key, 6)
    for axis_at, shards_of in cuts:
        steps = jnp.exp(jax.random.uniform(jax.random.fold_in(own, axis_at), (shards_of,), jnp.float32, least / len(cuts), largest / len(cuts)))
        factor_of = factor_of * jnp.repeat(steps, dims[axis_at] // shards_of).reshape([-1 if axis == axis_at else 1 for axis in range(len(dims))])
    return factor_of


def gaussian(key, dims, scale, reach, cuts=(), dtype=jnp.bfloat16):
    level = steps_of(key, dims, cuts, -0.22, 0.18) if cuts else 1.0
    array = jax.random.normal(key, dims, jnp.float32) * scale * level
    return jnp.minimum(jnp.maximum(array, -reach), reach).astype(dtype)


def setup_inputs(seed: int = 0) -> dict:
    keys = jax.random.split(jax.random.key(seed), 9)
    return {
        "acts": gaussian(keys[0], (CELLS, LEN, D), 1.0, 6.0, ((0, 16),)),
        "counts": draw_counts(jax.random.fold_in(keys[8], 71), 0),
        "cotangent": gaussian(keys[2], (CELLS, LEN, D), 1.0, 6.0, ((0, 16),)),
        "norm_gains": jnp.clip(1.0 + 0.1 * jax.random.normal(keys[3], (N_SECTION, 2, D), jnp.float32), 0.5, 1.5),
        "w_qkv": gaussian(keys[4], (N_SECTION, D, 3 * D), (D // 2) ** -0.5, 0.3125, ((0, 2),)),
        "w_out": gaussian(keys[5], (N_SECTION, D, D), (D // 8) ** -0.5, 0.625, ((0, 2),)),
        "w_up": gaussian(keys[6], (N_SECTION, D, FF), D ** -0.5, 0.21875, ((0, 2),)),
        "w_down": gaussian(keys[7], (N_SECTION, FF, D), FF ** -0.5, 0.109375, ((0, 2),)),
    }


EPSILON = 1e-05
HIGH = lax.Precision.HIGHEST

@jax.custom_vjp
def low(v):
    return lax.optimization_barrier(v.astype(jnp.bfloat16)).astype(jnp.float32)

@jax.custom_vjp
def low_back(v):
    return v

def low_keep(v):
    return (low(v), None)

def low_pass(kept, grad):
    return (grad,)

def back_keep(v):
    return (v, None)

def back_low(kept, grad):
    return (low(grad),)
low.defvjp(low_keep, low_pass)
low_back.defvjp(back_keep, back_low)

def product(left, right):
    return jnp.dot(left, right, precision=HIGH)

def normalize(hidden, gain):
    centred = hidden - lax.optimization_barrier(jnp.mean(hidden, axis=-1, keepdims=True))
    spread = lax.optimization_barrier(jnp.mean(centred * centred, axis=-1, keepdims=True))
    return centred * lax.rsqrt(spread + EPSILON) * gain

def gelu_exact(values):
    return jax.nn.gelu(values, approximate=False)

def attend(qkv_rows, key_valid):
    length = qkv_rows.shape[0]
    split_parts = qkv_rows.reshape(length, 3, HEADS, HD)
    scores = jnp.einsum('qhe,khe->hqk', split_parts[:, 0], split_parts[:, 1], precision=HIGH) * HD ** (-0.5)
    scores = low_back(scores)
    scores = jnp.where(key_valid[None, None, :], scores, -1e+30)
    weights_soft = low(jax.nn.softmax(scores, axis=-1))
    mixed_heads = jnp.einsum('hqk,khe->qhe', weights_soft, split_parts[:, 2], precision=HIGH)
    return low_back(low(mixed_heads.reshape(length, HEADS * HD)))

def layer(hidden, gene_count, gains, w_qkv, w_out, w_up, w_down):
    key_valid = jnp.arange(hidden.shape[0]) < gene_count
    normed_a = low(normalize(hidden, gains[0]))
    qkv_rows = low_back(low(product(normed_a, w_qkv)))
    mid_stream = hidden + low_back(product(attend(qkv_rows, key_valid), w_out))
    normed_b = low(normalize(mid_stream, gains[1]))
    up_value = low_back(product(normed_b, w_up))
    activated = low(gelu_exact(up_value))
    return mid_stream + low_back(product(activated, w_down))

def reference(acts, counts, cotangent, norm_gains, w_qkv, w_out, w_up, w_down):

    def whole(inputs, gains, weight_qkv, weight_out, weight_up, weight_down):

        def one_cell(cell_item):
            hidden, gene_count = cell_item
            first_out = layer(hidden, gene_count, gains[0], weight_qkv[0], weight_out[0], weight_up[0], weight_down[0])
            first_out = low_back(low(first_out))
            return layer(first_out, gene_count, gains[1], weight_qkv[1], weight_out[1], weight_up[1], weight_down[1])
        return lax.map(jax.checkpoint(one_cell), (inputs, counts))
    primal = (acts.astype(jnp.float32), norm_gains.astype(jnp.float32), w_qkv.astype(jnp.float32), w_out.astype(jnp.float32), w_up.astype(jnp.float32), w_down.astype(jnp.float32))
    output, pullback = jax.vjp(whole, *primal)
    d_acts, d_gains, d_qkv, d_out, d_up, d_down = pullback(cotangent.astype(jnp.float32))
    ends = jnp.stack([d_acts, output])
    return (ends, d_gains, d_qkv, d_out, d_up, d_down)
```

```python
import functools

import jax
import jax.numpy as jnp
from jax import lax
from jax.experimental import pallas as pl
from jax.experimental.pallas import tpu as pltpu
from jax.sharding import PartitionSpec as P

HEADS = 12
HD = 64
EPSILON = 1e-05
MESH = pl.DeviceIdType.MESH
F32 = jnp.float32
BF16 = jnp.bfloat16

UNITS = 36
LAG_CORE = 2
LAG_X = 6
LAG_Z = 9
KEEP = 8


def passed_along(block, axis, distance):
    devices = range(lax.axis_size(axis))
    route = [(i - distance, i) for i in devices if i - distance in devices]
    return lax.ppermute(block, axis, route)


def normalize(hidden, gain):
    centred = hidden - jnp.mean(hidden, axis=-1, keepdims=True)
    spread = jnp.mean(centred * centred, axis=-1, keepdims=True)
    return centred * lax.rsqrt(spread + EPSILON) * gain


def gelu_exact(values):
    return jax.nn.gelu(values, approximate=False)


def split_heads(qkv_rows):
    length = qkv_rows.shape[0]
    split_parts = qkv_rows.reshape(length, 3, HEADS, HD)
    return (split_parts[:, 0], split_parts[:, 1], split_parts[:, 2])


def masked_scores(queries, key_rows, key_valid):
    scores = jnp.einsum(
        "qhe,khe->hqk", queries, key_rows, preferred_element_type=jnp.float32
    ) * HD ** (-0.5)
    return jnp.where(key_valid[None, None, :], scores, -1e30)


def layer_forward(source, gene_count, gains, weights):
    weight_qkv, weight_out, weight_up, weight_down = weights
    length = source.shape[0]
    key_valid = jnp.arange(length) < gene_count
    normed_a = normalize(source, gains[0]).astype(jnp.bfloat16)
    qkv_rows = jnp.dot(normed_a, weight_qkv, preferred_element_type=jnp.float32).astype(
        jnp.bfloat16
    )
    queries, key_rows, value_rows = split_heads(qkv_rows)
    scores = masked_scores(queries, key_rows, key_valid)
    largest = jnp.max(scores, axis=-1, keepdims=True)
    raised = jnp.exp(scores - largest)
    summed = jnp.sum(raised, axis=-1, keepdims=True)
    log_total = largest + jnp.log(summed)
    weights_soft = (raised / summed).astype(jnp.bfloat16)
    mixed_heads = jnp.einsum(
        "hqk,khe->qhe", weights_soft, value_rows, preferred_element_type=jnp.float32
    )
    mixed_heads = mixed_heads.reshape(length, HEADS * HD).astype(jnp.bfloat16)
    mid_stream = source + jnp.dot(mixed_heads, weight_out, preferred_element_type=jnp.float32)
    normed_b = normalize(mid_stream, gains[1]).astype(jnp.bfloat16)
    up_value = jnp.dot(normed_b, weight_up, preferred_element_type=jnp.float32)
    activated = gelu_exact(up_value).astype(jnp.bfloat16)
    result = mid_stream + jnp.dot(activated, weight_down, preferred_element_type=jnp.float32)
    return (
        result,
        (normed_a, qkv_rows, log_total, mixed_heads, mid_stream, normed_b, up_value, activated),
    )


def attend_backward(qkv_rows, log_total, d_mixed, key_valid):
    length = qkv_rows.shape[0]
    queries, key_rows, value_rows = split_heads(qkv_rows)
    scores = masked_scores(queries, key_rows, key_valid)
    weights_soft = jnp.exp(scores - log_total)
    d_heads = d_mixed.reshape(length, HEADS, HD)
    d_values = jnp.einsum(
        "hqk,qhe->khe",
        weights_soft.astype(jnp.bfloat16),
        d_heads,
        preferred_element_type=jnp.float32,
    )
    d_weights = jnp.einsum("qhe,khe->hqk", d_heads, value_rows, preferred_element_type=jnp.float32)
    inner = jnp.sum(weights_soft * d_weights, axis=-1, keepdims=True)
    d_scores = (weights_soft * (d_weights - inner)).astype(jnp.bfloat16)
    d_queries = jnp.einsum(
        "hqk,khe->qhe", d_scores, key_rows, preferred_element_type=jnp.float32
    ) * HD ** (-0.5)
    d_keys = jnp.einsum(
        "hqk,qhe->khe", d_scores, queries, preferred_element_type=jnp.float32
    ) * HD ** (-0.5)
    stacked = jnp.stack([d_queries, d_keys, d_values], axis=1)
    return stacked.reshape(length, 3 * HEADS * HD).astype(jnp.bfloat16)


def backward_inputs(grad_in, source, stored, gene_count, gains, weights):
    normed_a, qkv_rows, log_total, mixed_heads, mid_stream, normed_b, up_value, activated = stored
    weight_qkv, weight_out, weight_up, weight_down = weights
    key_valid = jnp.arange(source.shape[0]) < gene_count
    d_low = grad_in.astype(jnp.bfloat16)
    d_activated = jnp.einsum("ld,fd->lf", d_low, weight_down, preferred_element_type=jnp.float32)
    unused, gelu_back = jax.vjp(gelu_exact, up_value)
    d_up = gelu_back(d_activated)[0].astype(jnp.bfloat16)
    d_normed_b = jnp.einsum("lf,df->ld", d_up, weight_up, preferred_element_type=jnp.float32)
    unused, norm_back_b = jax.vjp(normalize, mid_stream, gains[1])
    d_mid_part, d_gain_b = norm_back_b(d_normed_b)
    d_mid = grad_in + d_mid_part
    d_branch = d_mid.astype(jnp.bfloat16)
    d_mixed = jnp.einsum(
        "le,de->ld", d_branch, weight_out, preferred_element_type=jnp.float32
    ).astype(jnp.bfloat16)
    d_qkv = attend_backward(qkv_rows, log_total, d_mixed, key_valid)
    d_normed_a = jnp.einsum("le,de->ld", d_qkv, weight_qkv, preferred_element_type=jnp.float32)
    unused, norm_back_a = jax.vjp(normalize, source, gains[0])
    d_source_part, d_gain_a = norm_back_a(d_normed_a)
    d_source = d_mid + d_source_part
    return (d_source, jnp.stack([d_gain_a, d_gain_b]), (d_low, d_up, d_branch, d_qkv))


def scatter_kernel(
    a_ref, o_ref, b_ref, f_ref, deltas_ref, gain_ref,
    gq_ref, go_ref, gu_ref, gd_ref, gg_ref,
    turned, core_out, core_in, x_out, x_in, z_out, z_in,
    keep_core, keep_x, keep_z, gain_held, gain_in,
    core_send, core_recv, x_send, x_recv, z_send, z_recv, gain_send, gain_recv,
):
    section = lax.axis_index("section")
    place = lax.axis_index("dp")
    z = place // 4
    x = (place // 2) % 2
    core = place % 2
    far_z = (z + 1 - 2 * (z % 2), (z + 2) % 4, 3 - z)
    core_device = (section, z * 4 + x * 2 + 1 - core)
    x_device = (section, z * 4 + (1 - x) * 2 + core)
    z_devices = [(section, other * 4 + x * 2 + core) for other in far_z]

    barrier = pltpu.get_barrier_semaphore()
    for device in [core_device, x_device] + z_devices:
        pl.semaphore_signal(barrier, inc=1, device_id=device, device_id_type=MESH)
    pl.semaphore_wait(barrier, 5)

    def gain_copy(step, device):
        return pltpu.make_async_remote_copy(
            src_ref=gain_held.at[min(step, 2)],
            dst_ref=gain_in.at[step],
            send_sem=gain_send.at[step],
            recv_sem=gain_recv.at[step],
            device_id=device,
            device_id_type=MESH,
        )

    def turn(source, column, rows_to):
        block = source[:, column:column + 384].T
        for at, row in enumerate(rows_to):
            lhs, start = row
            turned[lhs, start:start + 48, :] = block[at * 48:(at + 1) * 48]

    def place_of(share):
        return (share % 2) * 384 + ((share // 2) % 2) * 192 + (share // 4) * 48

    gain_held[0] = gain_ref[...]
    first = gain_copy(0, core_device)
    first.start()
    for part in range(8):
        turn(f_ref, part * 384, [(j, place_of(part * 2 + k)) for k in range(2) for j in range(4)])
        if part == 2:
            first.wait()
            gain_held[1] = gain_held[0] + gain_in[0]
            second = gain_copy(1, x_device)
            second.start()
        if part == 7:
            second.wait()
            gain_held[2] = gain_held[1] + gain_in[1]
            thirds = [gain_copy(2 + j, z_devices[j]) for j in range(3)]
            for copy in thirds:
                copy.start()
    for lhs, source in ((4, b_ref), (5, o_ref), (6, a_ref)):
        for part in range(2):
            turn(source, part * 384, [(lhs, place_of(part * 8 + k)) for k in range(8)])
    for copy in thirds:
        copy.wait()
    gg_ref[...] = gain_held[2] + gain_in[2] + gain_in[3] + gain_in[4]

    def core_copy(k):
        return pltpu.make_async_remote_copy(
            src_ref=core_out.at[k], dst_ref=core_in.at[k],
            send_sem=core_send.at[k], recv_sem=core_recv.at[k],
            device_id=core_device, device_id_type=MESH,
        )

    def x_copy(k):
        return pltpu.make_async_remote_copy(
            src_ref=x_out.at[k], dst_ref=x_in.at[k],
            send_sem=x_send.at[k], recv_sem=x_recv.at[k],
            device_id=x_device, device_id_type=MESH,
        )

    def z_copy(k, j):
        return pltpu.make_async_remote_copy(
            src_ref=z_out.at[k, j], dst_ref=z_in.at[k, j],
            send_sem=z_send.at[k, j], recv_sem=z_recv.at[k, j],
            device_id=z_devices[j], device_id_type=MESH,
        )

    def form(k):
        down = (k < 12).astype(jnp.int32)
        left = down * (k // 3) + (1 - down) * (
            4 + (k >= 24).astype(jnp.int32) + (k >= 27).astype(jnp.int32)
        )
        right = down * (k % 3) + (1 - down) * (k - 9)
        delta = deltas_ref[:, pl.ds(pl.multiple_of(right * 256, 256), 256)]
        away = turned[left, pl.ds(pl.multiple_of((1 - core) * 384, 16), 384), :]
        core_out[k] = jnp.dot(away, delta, preferred_element_type=F32).astype(BF16)
        core_copy(k).start()
        own = turned[left, pl.ds(pl.multiple_of(core * 384, 16), 384), :]
        keep_core[k % KEEP] = jnp.dot(own, delta, preferred_element_type=F32)

    def over_core(k):
        core_copy(k).wait_recv()
        rows = pl.ds(pl.multiple_of((1 - x) * 192, 16), 192)
        x_out[k] = (keep_core[k % KEEP, rows, :] + core_in[k, rows, :].astype(F32)).astype(BF16)
        x_copy(k).start()
        rows = pl.ds(pl.multiple_of(x * 192, 16), 192)
        keep_x[k % KEEP] = keep_core[k % KEEP, rows, :] + core_in[k, rows, :].astype(F32)

    def over_x(k):
        x_copy(k).wait_recv()
        for j in range(3):
            rows = pl.ds(pl.multiple_of(far_z[j] * 48, 16), 48)
            z_out[k, j] = (keep_x[k % KEEP, rows, :] + x_in[k, rows, :].astype(F32)).astype(BF16)
            z_copy(k, j).start()
        rows = pl.ds(pl.multiple_of(z * 48, 16), 48)
        keep_z[k % KEEP] = keep_x[k % KEEP, rows, :] + x_in[k, rows, :].astype(F32)

    def over_z(k):
        for j in range(3):
            z_copy(k, j).wait_recv()
        total = keep_z[k % KEEP]
        for j in range(3):
            total = total + z_in[k, j].astype(F32)

        @pl.when(k < 12)
        def _():
            gd_ref[
                pl.ds(pl.multiple_of((k // 3) * 48, 8), 48),
                pl.ds(pl.multiple_of((k % 3) * 256, 256), 256),
            ] = total

        @pl.when(jnp.logical_and(k >= 12, k < 24))
        def _():
            gu_ref[:, pl.ds(pl.multiple_of((k - 12) * 256, 256), 256)] = total

        @pl.when(jnp.logical_and(k >= 24, k < 27))
        def _():
            go_ref[:, pl.ds(pl.multiple_of((k - 24) * 256, 256), 256)] = total

        @pl.when(k >= 27)
        def _():
            gq_ref[:, pl.ds(pl.multiple_of((k - 27) * 256, 256), 256)] = total

    def step(t, carry):
        @pl.when(t < UNITS)
        def _():
            form(t)

        for lag, work in ((LAG_CORE, over_core), (LAG_X, over_x), (LAG_Z, over_z)):
            @pl.when(jnp.logical_and(t >= lag, t < UNITS + lag))
            def _():
                work(t - lag)

        return carry

    lax.fori_loop(0, UNITS + LAG_Z, step, 0)

    def finish(k, carry):
        core_copy(k).wait_send()
        x_copy(k).wait_send()
        for j in range(3):
            z_copy(k, j).wait_send()
        return carry

    lax.fori_loop(0, UNITS, finish, 0)


def scattered(normed_a, mixed, normed_b, activated, deltas, d_gains):
    gain_rows = jnp.pad(d_gains, ((0, 6), (0, 0)))
    vmem = pl.BlockSpec(memory_space=pltpu.VMEM)
    dma = pltpu.SemaphoreType.DMA
    outs = pl.pallas_call(
        scatter_kernel,
        out_shape=(
            jax.ShapeDtypeStruct((48, 2304), F32),
            jax.ShapeDtypeStruct((48, 768), F32),
            jax.ShapeDtypeStruct((48, 3072), F32),
            jax.ShapeDtypeStruct((192, 768), F32),
            jax.ShapeDtypeStruct((8, 768), F32),
        ),
        in_specs=[vmem] * 6,
        out_specs=(vmem,) * 5,
        scratch_shapes=[
            pltpu.VMEM((7, 768, 512), BF16),
            pltpu.VMEM((UNITS, 384, 256), BF16),
            pltpu.VMEM((UNITS, 384, 256), BF16),
            pltpu.VMEM((UNITS, 192, 256), BF16),
            pltpu.VMEM((UNITS, 192, 256), BF16),
            pltpu.VMEM((UNITS, 3, 48, 256), BF16),
            pltpu.VMEM((UNITS, 3, 48, 256), BF16),
            pltpu.VMEM((KEEP, 384, 256), F32),
            pltpu.VMEM((KEEP, 192, 256), F32),
            pltpu.VMEM((KEEP, 48, 256), F32),
            pltpu.VMEM((3, 8, 768), F32),
            pltpu.VMEM((5, 8, 768), F32),
            dma((UNITS,)), dma((UNITS,)),
            dma((UNITS,)), dma((UNITS,)),
            dma((UNITS, 3)), dma((UNITS, 3)),
            dma((5,)), dma((5,)),
        ],
        compiler_params=pltpu.CompilerParams(
            collective_id=1, has_side_effects=True, vmem_limit_bytes=60 << 20
        ),
        name="scatter_grads",
    )(normed_a, mixed, normed_b, activated, deltas, gain_rows)
    gq, go, gu, gd, gg = outs
    place = lax.axis_index("dp")
    return (lax.dynamic_slice_in_dim(gg[:2], place * 48, 48, axis=1), gq, go, gu, gd)


def plain_scattered(normed_a, mixed, normed_b, activated, deltas, d_gains):
    d_low, d_up = deltas[:, :768], deltas[:, 768:3840]
    d_branch, d_qkv = deltas[:, 3840:4608], deltas[:, 4608:]
    dot = functools.partial(jnp.einsum, "ld,le->de", preferred_element_type=F32)
    scatter = functools.partial(
        lax.psum_scatter, axis_name="dp", scatter_dimension=0, tiled=True
    )
    return (
        lax.psum_scatter(d_gains, "dp", scatter_dimension=1, tiled=True),
        scatter(dot(normed_a, d_qkv)),
        scatter(dot(mixed, d_branch)),
        scatter(dot(normed_b, d_up)),
        scatter(dot(activated, d_low)),
    )


def body(acts, counts, cotangent, norm_gains, w_qkv, w_out, w_up, w_down):
    micro_count = acts.shape[0]
    section_index = lax.axis_index("section")
    on_first = section_index == 0
    gains = norm_gains[0]
    weights = (w_qkv[0], w_out[0], w_up[0], w_down[0])

    def cell_count(forward_tick):
        return counts[jnp.clip(forward_tick - section_index, 0, micro_count - 1)]

    arrived = jnp.zeros_like(acts[0])
    inputs, stores, results = ([], [], [])
    for forward_tick in range(micro_count + 1):
        source = jnp.where(on_first, acts[min(forward_tick, micro_count - 1)], arrived).astype(
            jnp.float32
        )
        result, stored = layer_forward(source, cell_count(forward_tick), gains, weights)
        inputs.append(source)
        stores.append(stored)
        results.append(result)
        if forward_tick < micro_count:
            arrived = passed_along(result.astype(jnp.bfloat16), "section", 1)
    returned = jnp.zeros_like(cotangent[0])
    source_grads = []
    total_gains = 0.0
    tick_deltas = []
    for backward_tick in range(micro_count + 1):
        forward_tick = micro_count - backward_tick
        if backward_tick < micro_count:
            upstream = cotangent[micro_count - 1 - backward_tick]
        else:
            upstream = jnp.zeros_like(cotangent[0])
        grad_in = jnp.where(on_first, returned, upstream).astype(jnp.float32)
        gene_count = cell_count(forward_tick)
        d_source, d_gains, deltas = backward_inputs(
            grad_in, inputs[forward_tick], stores[forward_tick], gene_count, gains, weights
        )
        if backward_tick < micro_count:
            returned = passed_along(d_source.astype(jnp.bfloat16), "section", -1)
        total_gains = total_gains + d_gains
        tick_deltas.append(jnp.concatenate(deltas, axis=1))
        if backward_tick > 0:
            source_grads.append(d_source)
    tick_deltas = tick_deltas[::-1]

    def held(per_tick):
        return jnp.concatenate([
            jnp.where(on_first, per_tick[cell], per_tick[cell + 1]) for cell in range(micro_count)
        ])

    left = [held([stored[at] for stored in stores]) for at in (0, 3, 5, 7)]
    right = held(tick_deltas)
    reduce = scattered if lax.axis_size("dp") == 16 and micro_count == 2 else plain_scattered
    grad_gains, grad_qkv, grad_out, grad_up, grad_down = reduce(*left, right, total_gains)
    input_grads = jnp.stack(source_grads[::-1])
    layer_outputs = jnp.stack(results[1:])
    ends = jnp.where(on_first, input_grads, layer_outputs)[None]
    return (ends, grad_gains[None], grad_qkv[None], grad_out[None], grad_up[None], grad_down[None])


def solution(mesh):
    placed = (
        P("dp", None, None),
        P("dp"),
        P("dp", None, None),
        P("section", None, None),
        P("section", None, None),
        P("section", None, None),
        P("section", None, None),
        P("section", None, None),
    )
    return jax.shard_map(
        body,
        mesh=mesh,
        in_specs=placed,
        out_specs=(
            P("section", "dp", None, None),
            P("section", None, "dp"),
            P("section", "dp", None),
            P("section", "dp", None),
            P("section", "dp", None),
            P("section", "dp", None),
        ),
        check_vma=False,
    )
```

```python
import functools

import jax
import jax.numpy as jnp
from jax import lax
from jax.experimental import pallas as pl
from jax.experimental.pallas import tpu as pltpu
from jax.sharding import PartitionSpec as P

HEADS = 12
HD = 64
EPSILON = 1e-05
MESH = pl.DeviceIdType.MESH
F32 = jnp.float32
BF16 = jnp.bfloat16

UNITS = 36
LAG_CORE = 2
LAG_X = 6
LAG_Z = 9
KEEP = 8


NT = (((1,), (1,)), ((), ()))
TN = (((0,), (0,)), ((), ()))


def dot(left, right):
    return jnp.dot(left, right, preferred_element_type=F32)


def dot_nt(left, right):
    return lax.dot_general(left, right, NT, preferred_element_type=F32)


def dot_tn(left, right):
    return lax.dot_general(left, right, TN, preferred_element_type=F32)


def gelu_and_slope(u):
    size = 1.0 + (0.3275911 * 0.5 ** 0.5) * jnp.abs(u)
    t = pl.reciprocal(size, approx=True)
    t = t * (2.0 - size * t)
    bell = jnp.exp(-0.5 * (u * u))
    tail = (0.5 * 1.061405429) * t + (0.5 * -1.453152027)
    tail = tail * t + (0.5 * 1.421413741)
    tail = tail * t + (0.5 * -0.284496736)
    tail = tail * t + (0.5 * 0.254829592)
    tail = tail * t * bell
    share = jnp.where(u >= 0.0, 1.0 - tail, tail)
    return u * share, share + u * (bell * 0.3989422804014327)


def layer_kernel(
    counts_ref, gains_ref, acts_ref, cotangent_ref, wq_hbm, wo_hbm, wu_hbm, wd_hbm,
    ends_ref, a_ref, o_ref, b_ref, f_ref, deltas_ref, gain_ref,
    wq, wo, wu, wd, source, upstream, relayed, qkv, probs, slope,
    normed_1, normed_2, scale_1, scale_2, mid, wide, d_mid, d_mixed,
    weight_sem, input_sem, send_sem, recv_sem,
):
    section = lax.axis_index("section")
    place = lax.axis_index("dp")
    partner = (1 - section, place)
    on_first = section == 0
    rows_in = source.shape[1]
    pairs = HEADS // 2

    loads = [
        pltpu.make_async_copy(hbm, vmem, weight_sem.at[at])
        for at, (hbm, vmem) in enumerate(((wq_hbm, wq), (wo_hbm, wo), (wu_hbm, wu), (wd_hbm, wd)))
    ]
    acts_in = pltpu.make_async_copy(acts_ref, source, input_sem)
    cotangent_in = pltpu.make_async_copy(cotangent_ref, upstream, input_sem)

    @pl.when(on_first)
    def _():
        acts_in.start()

    for load in loads:
        load.start()

    @pl.when(section == 1)
    def _():
        cotangent_in.start()

    barrier = pltpu.get_barrier_semaphore()
    pl.semaphore_signal(barrier, inc=1, device_id=partner, device_id_type=MESH)
    pl.semaphore_wait(barrier, 1)

    @pl.when(on_first)
    def _():
        acts_in.wait()

    @pl.when(section == 1)
    def _():
        cotangent_in.wait()

    gain_ref[...] = jnp.zeros_like(gain_ref)
    low_lanes = lax.broadcasted_iota(jnp.int32, (rows_in, 128), 1) < HD

    def relay_copy(cell, target):
        return pltpu.make_async_remote_copy(
            src_ref=relayed.at[cell],
            dst_ref=target.at[cell],
            send_sem=send_sem.at[cell],
            recv_sem=recv_sem.at[cell],
            device_id=partner,
            device_id_type=MESH,
        )

    def stacked(pair_block):
        none = jnp.zeros_like(pair_block)
        return jnp.concatenate(
            [jnp.where(low_lanes, pair_block, none), jnp.where(low_lanes, none, pair_block)], axis=0
        )

    def unstacked(block):
        return jnp.where(low_lanes, block[:rows_in], block[rows_in:])

    def columns(start, width=128):
        return pl.ds(pl.multiple_of(start, 128), width)

    def norm_rows(values, row_gain, at, rows, normed, scale):
        centred = values - jnp.mean(values, axis=-1, keepdims=True)
        spread = jnp.mean(centred * centred, axis=-1, keepdims=True)
        factor = lax.rsqrt(spread + EPSILON)
        unit = centred * factor
        normed[at, rows, :] = unit
        scale[at, rows, :] = jnp.broadcast_to(factor, (values.shape[0], 128))
        return (unit * row_gain).astype(BF16)

    def norm_back(d_normed, row_gain, at, rows, normed, scale, gain_row):
        unit = normed[at, rows, :]
        product = d_normed * unit
        gain_ref[gain_row:gain_row + 1, :] += jnp.sum(product, axis=0, keepdims=True)
        e = d_normed * row_gain
        mean_e = jnp.mean(e, axis=-1, keepdims=True)
        mean_en = jnp.mean(product * row_gain, axis=-1, keepdims=True)
        return scale[at, rows, :1] * (e - mean_e - unit * mean_en)

    def forward(t, cell):
        first_gain = gains_ref[0:1, :]
        second_gain = gains_ref[1:2, :]
        base = cell * rows_in
        all_rows = pl.ds(pl.multiple_of(base, 256), rows_in)

        @pl.when(section == 1)
        def _():
            relay_copy(cell, source).wait_recv()

        for part in range(4):
            rows = pl.ds(part * 64, 64)
            a_ref[pl.ds(pl.multiple_of(base + part * 64, 64), 64), :] = norm_rows(
                source[cell, rows, :].astype(F32), first_gain, cell, rows, normed_1, scale_1
            )

        @pl.when(t == 0)
        def _():
            loads[0].wait()

        a = a_ref[all_rows, :]
        for tile in range(9):
            cols = slice(tile * 256, tile * 256 + 256)
            block = dot(a, wq[:, cols])
            if tile < 3:
                block = block.astype(BF16).astype(F32) * HD ** -0.5
            qkv[cell, :, cols] = block.astype(BF16)

        valid = lax.broadcasted_iota(jnp.int32, (1, rows_in), 1) < counts_ref[cell]

        def attend(pair, carry):
            start = pair * 128
            queries = stacked(qkv[cell, :, columns(start)])
            scores = dot_nt(queries, qkv[cell, :, columns(start + 768)])
            scores = jnp.where(valid, scores, -1e30)
            raised = jnp.exp(scores - jnp.max(scores, axis=-1, keepdims=True))
            soft = raised * (1.0 / jnp.sum(raised, axis=-1, keepdims=True))
            soft = soft.astype(BF16)
            probs[cell, pair] = soft
            mixed = dot(soft, qkv[cell, :, columns(start + 1536)])
            o_ref[all_rows, columns(start)] = unstacked(mixed).astype(BF16)
            return carry

        lax.fori_loop(0, pairs, attend, 0)

        @pl.when(t == 0)
        def _():
            loads[1].wait()

        o = o_ref[all_rows, :]
        for tile in range(3):
            cols = slice(tile * 256, tile * 256 + 256)
            mid[:, cols] = source[cell, :, cols].astype(F32) + dot(o, wo[:, cols])
        for part in range(4):
            rows = pl.ds(part * 64, 64)
            b_ref[pl.ds(pl.multiple_of(base + part * 64, 64), 64), :] = norm_rows(
                mid[rows, :], second_gain, cell, rows, normed_2, scale_2
            )

        @pl.when(t == 0)
        def _():
            loads[2].wait()

        def rise(tile, carry):
            cols = columns(tile * 256, 256)
            u = dot(b_ref[all_rows, :], wu[:, cols])
            value, steep = gelu_and_slope(u)
            f_ref[all_rows, cols] = value.astype(BF16)
            slope[cell, :, cols] = steep.astype(BF16)
            return carry

        lax.fori_loop(0, 12, rise, 0)

        @pl.when(t == 0)
        def _():
            loads[3].wait()

        f = f_ref[all_rows, :]
        for tile in range(3):
            cols = slice(tile * 256, tile * 256 + 256)
            result = mid[:, cols] + dot(f, wd[:, cols])

            @pl.when(on_first)
            def _():
                relayed[cell, :, cols] = result.astype(BF16)

            @pl.when(section == 1)
            def _():
                ends_ref[cell, :, cols] = result

        @pl.when(on_first)
        def _():
            relay_copy(cell, source).start()

    def backward(cell):
        first_gain = gains_ref[0:1, :]
        second_gain = gains_ref[1:2, :]
        base = cell * rows_in
        all_rows = pl.ds(pl.multiple_of(base, 256), rows_in)

        @pl.when(on_first)
        def _():
            relay_copy(cell, source).wait_send()
            relay_copy(cell, upstream).wait_recv()

        deltas_ref[all_rows, 0:768] = upstream[cell]

        def fall(tile, carry):
            start = pl.multiple_of(tile * 256, 256)
            d_active = dot_nt(upstream[cell], wd[pl.ds(start, 256), :])
            d_up = d_active * slope[cell, :, pl.ds(start, 256)].astype(F32)
            deltas_ref[all_rows, columns(start + 768, 256)] = d_up.astype(BF16)
            return carry

        lax.fori_loop(0, 12, fall, 0)
        d_up = deltas_ref[all_rows, 768:3840]
        for tile in range(3):
            wide[:, tile * 256:tile * 256 + 256] = dot_nt(
                d_up, wu[tile * 256:tile * 256 + 256, :]
            )
        for part in range(4):
            rows = pl.ds(part * 64, 64)
            total = upstream[cell, rows, :].astype(F32) + norm_back(
                wide[rows, :], second_gain, cell, rows, normed_2, scale_2, 1
            )
            d_mid[rows, :] = total
            deltas_ref[pl.ds(pl.multiple_of(base + part * 64, 64), 64), 3840:4608] = total.astype(
                BF16
            )
        d_branch = deltas_ref[all_rows, 3840:4608]
        for tile in range(3):
            d_mixed[:, tile * 256:tile * 256 + 256] = dot_nt(
                d_branch, wo[tile * 256:tile * 256 + 256, :]
            ).astype(BF16)

        def attend_back(pair, carry):
            start = pair * 128
            queries = stacked(qkv[cell, :, columns(start)])
            key_rows = qkv[cell, :, columns(start + 768)]
            d_out = stacked(d_mixed[:, columns(start)])
            soft = probs[cell, pair]
            d_values = dot_tn(soft, d_out)
            d_soft = dot_nt(d_out, qkv[cell, :, columns(start + 1536)])
            soft = soft.astype(F32)
            inner = jnp.sum(soft * d_soft, axis=-1, keepdims=True)
            d_scores = (soft * (d_soft - inner)).astype(BF16)
            d_queries = unstacked(dot(d_scores, key_rows)) * HD ** -0.5
            d_keys = dot_tn(d_scores, queries)
            deltas_ref[all_rows, columns(start + 4608)] = d_queries.astype(BF16)
            deltas_ref[all_rows, columns(start + 5376)] = d_keys.astype(BF16)
            deltas_ref[all_rows, columns(start + 6144)] = d_values.astype(BF16)
            return carry

        lax.fori_loop(0, pairs, attend_back, 0)
        d_qkv = deltas_ref[all_rows, 4608:6912]
        for tile in range(3):
            wide[:, tile * 256:tile * 256 + 256] = dot_nt(
                d_qkv, wq[tile * 256:tile * 256 + 256, :]
            )
        for part in range(4):
            rows = pl.ds(part * 64, 64)
            total = d_mid[rows, :] + norm_back(
                wide[rows, :], first_gain, cell, rows, normed_1, scale_1, 0
            )

            @pl.when(on_first)
            def _():
                ends_ref[cell, rows, :] = total

            @pl.when(section == 1)
            def _():
                relayed[cell, rows, :] = total.astype(BF16)

        @pl.when(section == 1)
        def _():
            relay_copy(cell, upstream).start()

    def step(t, carry):
        backwards = (1 - section) * (t // 2) + section * (t % 2)
        cell = (1 - section) * (t % 2) + section * (t // 2)

        @pl.when(backwards == 0)
        def _():
            forward(t, cell)

        @pl.when(backwards == 1)
        def _():
            backward(cell)

        return carry

    lax.fori_loop(0, 4, step, 0)

    @pl.when(section == 1)
    def _():
        for cell in range(2):
            relay_copy(cell, upstream).wait_send()


def layers(acts, counts, cotangent, gains, w_qkv, w_out, w_up, w_down):
    rows = acts.shape[0] * acts.shape[1]
    length, width = acts.shape[1:]
    vmem = pl.BlockSpec(memory_space=pltpu.VMEM)
    anywhere = pl.BlockSpec(memory_space=pl.ANY)
    dma = pltpu.SemaphoreType.DMA
    return pl.pallas_call(
        layer_kernel,
        out_shape=(
            jax.ShapeDtypeStruct((2, length, width), F32),
            jax.ShapeDtypeStruct((rows, 768), BF16),
            jax.ShapeDtypeStruct((rows, 768), BF16),
            jax.ShapeDtypeStruct((rows, 768), BF16),
            jax.ShapeDtypeStruct((rows, 3072), BF16),
            jax.ShapeDtypeStruct((rows, 6912), BF16),
            jax.ShapeDtypeStruct((8, 768), F32),
        ),
        in_specs=[pl.BlockSpec(memory_space=pltpu.SMEM), vmem] + [anywhere] * 6,
        out_specs=(vmem,) * 7,
        scratch_shapes=[
            pltpu.VMEM((768, 2304), BF16),
            pltpu.VMEM((768, 768), BF16),
            pltpu.VMEM((768, 3072), BF16),
            pltpu.VMEM((3072, 768), BF16),
            pltpu.VMEM((2, length, width), BF16),
            pltpu.VMEM((2, length, width), BF16),
            pltpu.VMEM((2, length, width), BF16),
            pltpu.VMEM((2, length, 2304), BF16),
            pltpu.VMEM((2, HEADS // 2, 2 * length, length), BF16),
            pltpu.VMEM((2, length, 3072), BF16),
            pltpu.VMEM((2, length, width), F32),
            pltpu.VMEM((2, length, width), F32),
            pltpu.VMEM((2, length, 128), F32),
            pltpu.VMEM((2, length, 128), F32),
            pltpu.VMEM((length, width), F32),
            pltpu.VMEM((length, width), F32),
            pltpu.VMEM((length, width), F32),
            pltpu.VMEM((length, width), BF16),
            dma((4,)), dma(()), dma((2,)), dma((2,)),
        ],
        compiler_params=pltpu.CompilerParams(
            collective_id=2, has_side_effects=True, vmem_limit_bytes=62 << 20
        ),
        name="two_layers",
    )(counts, gains, acts, cotangent, w_qkv, w_out, w_up, w_down)


def scatter_kernel(
    a_ref, o_ref, b_ref, f_ref, deltas_ref, gain_ref,
    gq_ref, go_ref, gu_ref, gd_ref, gg_ref,
    turned, core_out, core_in, x_out, x_in, z_out, z_in,
    keep_core, keep_x, keep_z, gain_held, gain_in,
    core_send, core_recv, x_send, x_recv, z_send, z_recv, gain_send, gain_recv,
):
    section = lax.axis_index("section")
    place = lax.axis_index("dp")
    z = place // 4
    x = (place // 2) % 2
    core = place % 2
    far_z = (z + 1 - 2 * (z % 2), (z + 2) % 4, 3 - z)
    core_device = (section, z * 4 + x * 2 + 1 - core)
    x_device = (section, z * 4 + (1 - x) * 2 + core)
    z_devices = [(section, other * 4 + x * 2 + core) for other in far_z]

    barrier = pltpu.get_barrier_semaphore()
    for device in [core_device, x_device] + z_devices:
        pl.semaphore_signal(barrier, inc=1, device_id=device, device_id_type=MESH)
    pl.semaphore_wait(barrier, 5)

    def gain_copy(step, device):
        return pltpu.make_async_remote_copy(
            src_ref=gain_held.at[min(step, 2)],
            dst_ref=gain_in.at[step],
            send_sem=gain_send.at[step],
            recv_sem=gain_recv.at[step],
            device_id=device,
            device_id_type=MESH,
        )

    def turn(source, column, rows_to):
        block = source[:, column:column + 384].T
        for at, row in enumerate(rows_to):
            lhs, start = row
            turned[lhs, start:start + 48, :] = block[at * 48:(at + 1) * 48]

    def place_of(share):
        return (share % 2) * 384 + ((share // 2) % 2) * 192 + (share // 4) * 48

    gain_held[0] = gain_ref[...]
    first = gain_copy(0, core_device)
    first.start()
    for part in range(8):
        turn(f_ref, part * 384, [(j, place_of(part * 2 + k)) for k in range(2) for j in range(4)])
        if part == 2:
            first.wait()
            gain_held[1] = gain_held[0] + gain_in[0]
            second = gain_copy(1, x_device)
            second.start()
        if part == 7:
            second.wait()
            gain_held[2] = gain_held[1] + gain_in[1]
            thirds = [gain_copy(2 + j, z_devices[j]) for j in range(3)]
            for copy in thirds:
                copy.start()
    for lhs, source in ((4, b_ref), (5, o_ref), (6, a_ref)):
        for part in range(2):
            turn(source, part * 384, [(lhs, place_of(part * 8 + k)) for k in range(8)])
    for copy in thirds:
        copy.wait()
    gg_ref[...] = gain_held[2] + gain_in[2] + gain_in[3] + gain_in[4]

    def core_copy(k):
        return pltpu.make_async_remote_copy(
            src_ref=core_out.at[k], dst_ref=core_in.at[k],
            send_sem=core_send.at[k], recv_sem=core_recv.at[k],
            device_id=core_device, device_id_type=MESH,
        )

    def x_copy(k):
        return pltpu.make_async_remote_copy(
            src_ref=x_out.at[k], dst_ref=x_in.at[k],
            send_sem=x_send.at[k], recv_sem=x_recv.at[k],
            device_id=x_device, device_id_type=MESH,
        )

    def z_copy(k, j):
        return pltpu.make_async_remote_copy(
            src_ref=z_out.at[k, j], dst_ref=z_in.at[k, j],
            send_sem=z_send.at[k, j], recv_sem=z_recv.at[k, j],
            device_id=z_devices[j], device_id_type=MESH,
        )

    def form(k):
        down = (k < 12).astype(jnp.int32)
        left = down * (k // 3) + (1 - down) * (
            4 + (k >= 24).astype(jnp.int32) + (k >= 27).astype(jnp.int32)
        )
        right = down * (k % 3) + (1 - down) * (k - 9)
        delta = deltas_ref[:, pl.ds(pl.multiple_of(right * 256, 256), 256)]
        away = turned[left, pl.ds(pl.multiple_of((1 - core) * 384, 16), 384), :]
        core_out[k] = jnp.dot(away, delta, preferred_element_type=F32).astype(BF16)
        core_copy(k).start()
        own = turned[left, pl.ds(pl.multiple_of(core * 384, 16), 384), :]
        keep_core[k % KEEP] = jnp.dot(own, delta, preferred_element_type=F32)

    def over_core(k):
        core_copy(k).wait_recv()
        rows = pl.ds(pl.multiple_of((1 - x) * 192, 16), 192)
        x_out[k] = (keep_core[k % KEEP, rows, :] + core_in[k, rows, :].astype(F32)).astype(BF16)
        x_copy(k).start()
        rows = pl.ds(pl.multiple_of(x * 192, 16), 192)
        keep_x[k % KEEP] = keep_core[k % KEEP, rows, :] + core_in[k, rows, :].astype(F32)

    def over_x(k):
        x_copy(k).wait_recv()
        for j in range(3):
            rows = pl.ds(pl.multiple_of(far_z[j] * 48, 16), 48)
            z_out[k, j] = (keep_x[k % KEEP, rows, :] + x_in[k, rows, :].astype(F32)).astype(BF16)
            z_copy(k, j).start()
        rows = pl.ds(pl.multiple_of(z * 48, 16), 48)
        keep_z[k % KEEP] = keep_x[k % KEEP, rows, :] + x_in[k, rows, :].astype(F32)

    def over_z(k):
        for j in range(3):
            z_copy(k, j).wait_recv()
        total = keep_z[k % KEEP]
        for j in range(3):
            total = total + z_in[k, j].astype(F32)

        @pl.when(k < 12)
        def _():
            gd_ref[
                pl.ds(pl.multiple_of((k // 3) * 48, 8), 48),
                pl.ds(pl.multiple_of((k % 3) * 256, 256), 256),
            ] = total

        @pl.when(jnp.logical_and(k >= 12, k < 24))
        def _():
            gu_ref[:, pl.ds(pl.multiple_of((k - 12) * 256, 256), 256)] = total

        @pl.when(jnp.logical_and(k >= 24, k < 27))
        def _():
            go_ref[:, pl.ds(pl.multiple_of((k - 24) * 256, 256), 256)] = total

        @pl.when(k >= 27)
        def _():
            gq_ref[:, pl.ds(pl.multiple_of((k - 27) * 256, 256), 256)] = total

    def step(t, carry):
        @pl.when(t < UNITS)
        def _():
            form(t)

        for lag, work in ((LAG_CORE, over_core), (LAG_X, over_x), (LAG_Z, over_z)):
            @pl.when(jnp.logical_and(t >= lag, t < UNITS + lag))
            def _():
                work(t - lag)

        return carry

    lax.fori_loop(0, UNITS + LAG_Z, step, 0)

    def finish(k, carry):
        core_copy(k).wait_send()
        x_copy(k).wait_send()
        for j in range(3):
            z_copy(k, j).wait_send()
        return carry

    lax.fori_loop(0, UNITS, finish, 0)


def scattered(normed_a, mixed, normed_b, activated, deltas, d_gains):
    vmem = pl.BlockSpec(memory_space=pltpu.VMEM)
    dma = pltpu.SemaphoreType.DMA
    outs = pl.pallas_call(
        scatter_kernel,
        out_shape=(
            jax.ShapeDtypeStruct((48, 2304), F32),
            jax.ShapeDtypeStruct((48, 768), F32),
            jax.ShapeDtypeStruct((48, 3072), F32),
            jax.ShapeDtypeStruct((192, 768), F32),
            jax.ShapeDtypeStruct((8, 768), F32),
        ),
        in_specs=[vmem] * 6,
        out_specs=(vmem,) * 5,
        scratch_shapes=[
            pltpu.VMEM((7, 768, 512), BF16),
            pltpu.VMEM((UNITS, 384, 256), BF16),
            pltpu.VMEM((UNITS, 384, 256), BF16),
            pltpu.VMEM((UNITS, 192, 256), BF16),
            pltpu.VMEM((UNITS, 192, 256), BF16),
            pltpu.VMEM((UNITS, 3, 48, 256), BF16),
            pltpu.VMEM((UNITS, 3, 48, 256), BF16),
            pltpu.VMEM((KEEP, 384, 256), F32),
            pltpu.VMEM((KEEP, 192, 256), F32),
            pltpu.VMEM((KEEP, 48, 256), F32),
            pltpu.VMEM((3, 8, 768), F32),
            pltpu.VMEM((5, 8, 768), F32),
            dma((UNITS,)), dma((UNITS,)),
            dma((UNITS,)), dma((UNITS,)),
            dma((UNITS, 3)), dma((UNITS, 3)),
            dma((5,)), dma((5,)),
        ],
        compiler_params=pltpu.CompilerParams(
            collective_id=1, has_side_effects=True, vmem_limit_bytes=60 << 20
        ),
        name="scatter_grads",
    )(normed_a, mixed, normed_b, activated, deltas, d_gains)
    gq, go, gu, gd, gg = outs
    place = lax.axis_index("dp")
    return (lax.dynamic_slice_in_dim(gg[:2], place * 48, 48, axis=1), gq, go, gu, gd)


def plain_scattered(normed_a, mixed, normed_b, activated, deltas, d_gains):
    d_low, d_up = deltas[:, :768], deltas[:, 768:3840]
    d_branch, d_qkv = deltas[:, 3840:4608], deltas[:, 4608:]
    scatter = functools.partial(
        lax.psum_scatter, axis_name="dp", scatter_dimension=0, tiled=True
    )
    return (
        lax.psum_scatter(d_gains[:2], "dp", scatter_dimension=1, tiled=True),
        scatter(dot_tn(normed_a, d_qkv)),
        scatter(dot_tn(mixed, d_branch)),
        scatter(dot_tn(normed_b, d_up)),
        scatter(dot_tn(activated, d_low)),
    )


def body(acts, counts, cotangent, norm_gains, w_qkv, w_out, w_up, w_down):
    ends, normed_a, mixed, normed_b, activated, deltas, d_gains = layers(
        acts, counts, cotangent, norm_gains[0], w_qkv[0], w_out[0], w_up[0], w_down[0]
    )
    reduce = scattered if lax.axis_size("dp") == 16 else plain_scattered
    shares = reduce(normed_a, mixed, normed_b, activated, deltas, d_gains)
    return (ends[None],) + tuple(share[None] for share in shares)


def solution(mesh):
    placed = (
        P("dp", None, None),
        P("dp"),
        P("dp", None, None),
        P("section", None, None),
        P("section", None, None),
        P("section", None, None),
        P("section", None, None),
        P("section", None, None),
    )
    return jax.shard_map(
        body,
        mesh=mesh,
        in_specs=placed,
        out_specs=(
            P("section", "dp", None, None),
            P("section", None, "dp"),
            P("section", "dp", None),
            P("section", "dp", None),
            P("section", "dp", None),
            P("section", "dp", None),
        ),
        check_vma=False,
    )
```

```python
import functools

import jax
import jax.numpy as jnp
from jax import lax
from jax.experimental import pallas as pl
from jax.experimental.pallas import tpu as pltpu
from jax.sharding import PartitionSpec as P

HEADS = 12
HD = 64
EPSILON = 1e-05
MESH = pl.DeviceIdType.MESH
F32 = jnp.float32
BF16 = jnp.bfloat16

UNITS = 36
EARLY = 12
LAG_CORE = 2
LAG_X = 6
LAG_Z = 9
HELD = 4
VMEM_BYTES = 63 << 20


NT = (((1,), (1,)), ((), ()))
TN = (((0,), (0,)), ((), ()))


def dot(left, right):
    return jnp.dot(left, right, preferred_element_type=F32)


def dot_nt(left, right):
    return lax.dot_general(left, right, NT, preferred_element_type=F32)


def dot_tn(left, right):
    return lax.dot_general(left, right, TN, preferred_element_type=F32)


def gelu_and_slope(u):
    share = 0.5 + 0.5 * lax.erf(u * 0.5 ** 0.5)
    bell = jnp.exp(-0.5 * (u * u))
    return u * share, share + u * (bell * 0.3989422804014327)


def kernel(
    scattering, counts_ref, gains_ref, acts_ref, cotangent_ref, wq_hbm, wo_hbm, wu_hbm, wd_hbm,
    ends_ref, *rest,
):
    if scattering:
        gq_ref, go_ref, gu_ref, gd_ref, gg_ref, turned, deltas_ref, gain_ref = rest[:8]
        (core_out, keep_core, core_in, x_in, z_in, gain_held, gain_in,
         core_send, core_recv, x_send, x_recv, z_send, z_recv, gain_send, gain_recv) = rest[-15:]
        rest = rest[8:-15]
    else:
        turned, deltas_ref, gain_ref = rest[:3]
        rest = rest[3:]
    (wq, wo, wu, wd, source, upstream, relayed, a_ref, o_ref, b_ref, f_ref, probs,
     normed_1, normed_2, scale_1, scale_2, mid, wide, d_mid, d_mixed,
     weight_sem, input_sem, send_sem, recv_sem) = rest

    section = lax.axis_index("section")
    place = lax.axis_index("dp")
    partner = (1 - section, place)
    on_first = section == 0
    on_second = section == 1
    rows_in = source.shape[1]
    pairs = HEADS // 2

    z = place // 4
    x = (place // 2) % 2
    core = place % 2
    far_z = (z + 1 - 2 * (z % 2), (z + 2) % 4, 3 - z)
    core_device = (section, z * 4 + x * 2 + 1 - core)
    x_device = (section, z * 4 + (1 - x) * 2 + core)
    z_devices = [(section, other * 4 + x * 2 + core) for other in far_z]
    met = [partner] + ([core_device, x_device] + z_devices if scattering else [])

    barrier = pltpu.get_barrier_semaphore()
    for device in met:
        pl.semaphore_signal(barrier, inc=1, device_id=device, device_id_type=MESH)

    loads = [
        pltpu.make_async_copy(hbm, vmem, weight_sem.at[at])
        for at, (hbm, vmem) in enumerate(((wq_hbm, wq), (wo_hbm, wo), (wu_hbm, wu), (wd_hbm, wd)))
    ]
    acts_in = pltpu.make_async_copy(acts_ref, source, input_sem)
    cotangent_in = pltpu.make_async_copy(cotangent_ref, upstream, input_sem)

    @pl.when(on_first)
    def _():
        acts_in.start()

    for load in loads:
        load.start()

    @pl.when(on_second)
    def _():
        cotangent_in.start()

    gain_ref[...] = jnp.zeros_like(gain_ref)

    @pl.when(on_first)
    def _():
        acts_in.wait()

    @pl.when(on_second)
    def _():
        cotangent_in.wait()
        pl.semaphore_wait(barrier, len(met))

    low_lanes = lax.broadcasted_iota(jnp.int32, (rows_in, 128), 1) < HD

    def relay_copy(cell, target):
        return pltpu.make_async_remote_copy(
            src_ref=relayed.at[cell],
            dst_ref=target.at[cell],
            send_sem=send_sem.at[cell],
            recv_sem=recv_sem.at[cell],
            device_id=partner,
            device_id_type=MESH,
        )

    def place_of(share):
        return (share % 2) * 384 + ((share // 2) % 2) * 192 + (share // 4) * 48

    def turn(cell, ref, left):
        lanes = pl.ds(pl.multiple_of(cell * rows_in, 256), rows_in)
        for part in range(2):
            block = ref[:, part * 384:part * 384 + 384].T
            for at in range(8):
                start = place_of(part * 8 + at)
                turned[left, start:start + 48, lanes] = block[at * 48:at * 48 + 48]

    def turn_wide(cell):
        lanes = pl.ds(pl.multiple_of(cell * rows_in, 256), rows_in)
        for part in range(8):
            block = f_ref[:, part * 384:part * 384 + 384].T
            for at in range(8):
                start = place_of(part * 2 + at // 4)
                turned[at % 4, start:start + 48, lanes] = block[at * 48:at * 48 + 48]

    def stacked(pair_block):
        none = jnp.zeros_like(pair_block)
        return jnp.concatenate(
            [jnp.where(low_lanes, pair_block, none), jnp.where(low_lanes, none, pair_block)], axis=0
        )

    def unstacked(block):
        return jnp.where(low_lanes, block[:rows_in], block[rows_in:])

    def columns(start, width=128):
        return pl.ds(pl.multiple_of(start, 128), width)

    def norm_rows(values, row_gain, at, rows, normed, scale):
        centred = values - jnp.mean(values, axis=-1, keepdims=True)
        spread = jnp.mean(centred * centred, axis=-1, keepdims=True)
        factor = lax.rsqrt(spread + EPSILON)
        unit = centred * factor
        normed[at, rows, :] = unit
        scale[at, rows, :] = jnp.broadcast_to(factor, (values.shape[0], 128))
        return (unit * row_gain).astype(BF16)

    def norm_back(d_normed, row_gain, at, rows, normed, scale, gain_row):
        unit = normed[at, rows, :]
        product = d_normed * unit
        gain_ref[gain_row:gain_row + 1, :] += jnp.sum(product, axis=0, keepdims=True)
        e = d_normed * row_gain
        mean_e = jnp.mean(e, axis=-1, keepdims=True)
        mean_en = jnp.mean(product * row_gain, axis=-1, keepdims=True)
        return scale[at, rows, :1] * (e - mean_e - unit * mean_en)

    def whole(cell):
        return pl.ds(pl.multiple_of(cell * rows_in, 256), rows_in)

    def some(cell, part):
        return pl.ds(pl.multiple_of(cell * rows_in + part * 64, 64), 64)

    def norm_source(cell):
        for part in range(4):
            a_ref[part * 64:part * 64 + 64, :] = norm_rows(
                source[cell, pl.ds(part * 64, 64), :].astype(F32),
                gains_ref[0:1, :], cell, pl.ds(part * 64, 64), normed_1, scale_1,
            )

    def project_qkv(cell):
        a = a_ref[...]
        turn(cell, a_ref, 6)
        for tile in range(9):
            cols = slice(tile * 256, tile * 256 + 256)
            block = dot(a, wq[:, cols])
            if tile < 3:
                block = block.astype(BF16).astype(F32) * HD ** -0.5
            deltas_ref[whole(cell), tile * 256 + 4608:tile * 256 + 4864] = block.astype(BF16)

    def attention(cell):
        valid = lax.broadcasted_iota(jnp.int32, (1, rows_in), 1) < counts_ref[cell]

        def attend(pair, carry):
            start = pair * 128
            queries = stacked(deltas_ref[whole(cell), columns(start + 4608)])
            scores = dot_nt(queries, deltas_ref[whole(cell), columns(start + 5376)])
            scores = jnp.where(valid, scores, -1e30)
            raised = jnp.exp(scores - jnp.max(scores, axis=-1, keepdims=True))
            soft = raised * (1.0 / jnp.sum(raised, axis=-1, keepdims=True))
            soft = soft.astype(BF16)
            probs[cell, pair] = soft
            mixed = dot(soft, deltas_ref[whole(cell), columns(start + 6144)])
            o_ref[:, columns(start)] = unstacked(mixed).astype(BF16)
            return carry

        lax.fori_loop(0, pairs, attend, 0, unroll=True)

    def project_out(cell):
        o = o_ref[...]
        turn(cell, o_ref, 5)
        for tile in range(3):
            cols = slice(tile * 256, tile * 256 + 256)
            mid[:, cols] = source[cell, :, cols].astype(F32) + dot(o, wo[:, cols])

    def norm_mid(cell):
        for part in range(4):
            rows = pl.ds(part * 64, 64)
            b_ref[rows, :] = norm_rows(
                mid[rows, :], gains_ref[1:2, :], cell, rows, normed_2, scale_2
            )

    def go_up(cell):
        turn(cell, b_ref, 4)

        def rise(tile, carry):
            cols = columns(tile * 256, 256)
            u = dot(b_ref[...], wu[:, cols])
            value, steep = gelu_and_slope(u)
            f_ref[:, cols] = value.astype(BF16)
            deltas_ref[whole(cell), columns(tile * 256 + 768, 256)] = steep.astype(BF16)
            return carry

        lax.fori_loop(0, 12, rise, 0, unroll=True)

    def go_down(cell):
        f = f_ref[...]
        turn_wide(cell)
        for tile in range(3):
            cols = slice(tile * 256, tile * 256 + 256)
            result = mid[:, cols] + dot(f, wd[:, cols])
            ends_ref[cell, :, cols] = result
            relayed[cell, :, cols] = result.astype(BF16)

    def back_down(cell):
        deltas_ref[whole(cell), 0:768] = upstream[cell]

        def fall(tile, carry):
            start = pl.multiple_of(tile * 256, 256)
            d_active = dot_nt(upstream[cell], wd[pl.ds(start, 256), :])
            d_up = d_active * deltas_ref[whole(cell), columns(start + 768, 256)].astype(F32)
            deltas_ref[whole(cell), columns(start + 768, 256)] = d_up.astype(BF16)
            return carry

        lax.fori_loop(0, 12, fall, 0, unroll=True)

    def back_up(cell):
        d_up = deltas_ref[whole(cell), 768:3840]
        for tile in range(3):
            wide[:, tile * 256:tile * 256 + 256] = dot_nt(
                d_up, wu[tile * 256:tile * 256 + 256, :]
            )

    def norm_mid_back(cell):
        for part in range(4):
            rows = pl.ds(part * 64, 64)
            total = upstream[cell, rows, :].astype(F32) + norm_back(
                wide[rows, :], gains_ref[1:2, :], cell, rows, normed_2, scale_2, 1
            )
            d_mid[rows, :] = total
            deltas_ref[some(cell, part), 3840:4608] = total.astype(BF16)

    def back_out(cell):
        d_branch = deltas_ref[whole(cell), 3840:4608]
        for tile in range(3):
            d_mixed[:, tile * 256:tile * 256 + 256] = dot_nt(
                d_branch, wo[tile * 256:tile * 256 + 256, :]
            ).astype(BF16)

    def attention_back(cell):
        def attend_back(pair, carry):
            start = pair * 128
            queries = stacked(deltas_ref[whole(cell), columns(start + 4608)])
            key_rows = deltas_ref[whole(cell), columns(start + 5376)]
            d_out = stacked(d_mixed[:, columns(start)])
            soft = probs[cell, pair]
            d_values = dot_tn(soft, d_out)
            d_soft = dot_nt(d_out, deltas_ref[whole(cell), columns(start + 6144)])
            soft = soft.astype(F32)
            inner = jnp.sum(soft * d_soft, axis=-1, keepdims=True)
            d_scores = (soft * (d_soft - inner)).astype(BF16)
            d_queries = unstacked(dot(d_scores, key_rows)) * HD ** -0.5
            d_keys = dot_tn(d_scores, queries)
            deltas_ref[whole(cell), columns(start + 4608)] = d_queries.astype(BF16)
            deltas_ref[whole(cell), columns(start + 5376)] = d_keys.astype(BF16)
            deltas_ref[whole(cell), columns(start + 6144)] = d_values.astype(BF16)
            return carry

        lax.fori_loop(0, pairs, attend_back, 0, unroll=True)

    def back_qkv(cell):
        d_qkv = deltas_ref[whole(cell), 4608:6912]
        for tile in range(3):
            wide[:, tile * 256:tile * 256 + 256] = dot_nt(
                d_qkv, wq[tile * 256:tile * 256 + 256, :]
            )

    def norm_source_back(cell):
        for part in range(4):
            rows = pl.ds(part * 64, 64)
            total = d_mid[rows, :] + norm_back(
                wide[rows, :], gains_ref[0:1, :], cell, rows, normed_1, scale_1, 0
            )

            relayed[cell, rows, :] = total.astype(BF16)

            @pl.when(on_first)
            def _():
                ends_ref[cell, rows, :] = total

    def weights_here(t, at):
        @pl.when(t == 0)
        def _():
            loads[at].wait()

    def forward(t, cell):
        @pl.when(on_second)
        def _():
            relay_copy(cell, source).wait_recv()

        norm_source(cell)
        weights_here(t, 0)
        project_qkv(cell)
        attention(cell)
        weights_here(t, 1)
        project_out(cell)
        norm_mid(cell)
        weights_here(t, 2)
        go_up(cell)
        weights_here(t, 3)
        go_down(cell)

        @pl.when(on_first)
        def _():
            @pl.when(t == 0)
            def _():
                pl.semaphore_wait(barrier, len(met))

            relay_copy(cell, source).start()

    def nothing(at):
        del at

    def backward(cell, between=nothing):
        back_down(cell)
        between(0)
        back_up(cell)
        between(1)
        norm_mid_back(cell)
        back_out(cell)
        between(2)
        attention_back(cell)
        between(3)
        back_qkv(cell)
        norm_source_back(cell)

        @pl.when(on_second)
        def _():
            relay_copy(cell, upstream).start()

        between(4)

    def receive_gradient(cell):
        @pl.when(on_first)
        def _():
            relay_copy(cell, source).wait_send()
            relay_copy(cell, upstream).wait_recv()

        deltas_ref[whole(cell), 0:768] = upstream[cell]

    def step(t, carry):
        backwards = (1 - section) * (t // 2) + section * (t % 2)
        cell = (1 - section) * (t % 2) + section * (t // 2)

        @pl.when(backwards == 0)
        def _():
            forward(t, cell)

        @pl.when(backwards == 1)
        def _():
            receive_gradient(cell)
            backward(cell)

        return carry

    lax.fori_loop(0, 3 if scattering else 4, step, 0)

    if scattering:
        def gain_copy(at, device):
            return pltpu.make_async_remote_copy(
                src_ref=gain_held.at[min(at, 2)],
                dst_ref=gain_in.at[at],
                send_sem=gain_send.at[at],
                recv_sem=gain_recv.at[at],
                device_id=device,
                device_id_type=MESH,
            )

        def core_copy(k):
            return pltpu.make_async_remote_copy(
                src_ref=core_out.at[k % HELD], dst_ref=core_in.at[k],
                send_sem=core_send.at[k], recv_sem=core_recv.at[k],
                device_id=core_device, device_id_type=MESH,
            )

        def x_copy(k):
            rows = pl.ds(pl.multiple_of((1 - x) * 192, 16), 192)
            return pltpu.make_async_remote_copy(
                src_ref=core_in.at[k, rows], dst_ref=x_in.at[k],
                send_sem=x_send.at[k], recv_sem=x_recv.at[k],
                device_id=x_device, device_id_type=MESH,
            )

        def z_copy(k, j):
            rows = pl.ds(pl.multiple_of(far_z[j] * 48, 16), 48)
            return pltpu.make_async_remote_copy(
                src_ref=x_in.at[k, rows], dst_ref=z_in.at[k, j],
                send_sem=z_send.at[k, j], recv_sem=z_recv.at[k, j],
                device_id=z_devices[j], device_id_type=MESH,
            )

        def form(k):
            down = (k < 12).astype(jnp.int32)
            left = down * (k // 3) + (1 - down) * (
                4 + (k >= 24).astype(jnp.int32) + (k >= 27).astype(jnp.int32)
            )
            right = down * (k % 3) + (1 - down) * (k - 9)
            delta = deltas_ref[:, columns(right * 256, 256)]

            @pl.when(k >= HELD)
            def _():
                core_copy(k - HELD).wait_send()

            away = turned[left, pl.ds(pl.multiple_of((1 - core) * 384, 16), 384), :]
            core_out[k % HELD] = dot(away, delta).astype(BF16)
            core_copy(k).start()
            own = turned[left, pl.ds(pl.multiple_of(core * 384, 16), 384), :]
            keep_core[k % HELD] = dot(own, delta)

        def over_core(k):
            core_copy(k).wait_recv()
            total = keep_core[k % HELD] + core_in[k].astype(F32)
            core_in[k] = total.astype(BF16)
            x_copy(k).start()

        def over_x(k):
            x_copy(k).wait_recv()
            own = pl.ds(pl.multiple_of(x * 192, 16), 192)
            total = core_in[k, own, :].astype(F32) + x_in[k].astype(F32)
            x_in[k] = total.astype(BF16)
            for j in range(3):
                z_copy(k, j).start()

        def over_z(k):
            for j in range(3):
                z_copy(k, j).wait_recv()
            total = x_in[k, pl.ds(pl.multiple_of(z * 48, 16), 48), :].astype(F32)
            for j in range(3):
                total = total + z_in[k, j].astype(F32)

            @pl.when(k < 12)
            def _():
                rows = pl.ds(pl.multiple_of((k // 3) * 48, 8), 48)
                gd_ref[rows, columns((k % 3) * 256, 256)] = total

            @pl.when(jnp.logical_and(k >= 12, k < 24))
            def _():
                gu_ref[:, columns((k - 12) * 256, 256)] = total

            @pl.when(jnp.logical_and(k >= 24, k < 27))
            def _():
                go_ref[:, columns((k - 24) * 256, 256)] = total

            @pl.when(k >= 27)
            def _():
                gq_ref[:, columns((k - 27) * 256, 256)] = total

        receive_gradient(1)

        @pl.when(on_first)
        def _():
            def early(t, carry):
                @pl.when(t < EARLY)
                def _():
                    form(t)

                @pl.when(t >= LAG_CORE)
                def _():
                    over_core(t - LAG_CORE)

                return carry

            lax.fori_loop(0, EARLY + LAG_CORE, early, 0)

        x_turns = ((0,), (1,), (2,), (3, 4), (5,))
        z_turns = ((), (), (), (0,), (1, 2))

        def between(at):
            @pl.when(on_first)
            def _():
                for k in x_turns[at]:
                    over_x(k)
                for k in z_turns[at]:
                    over_z(k)

        backward(1, between)

        gain_held[0] = gain_ref[...]
        gain_copy(0, core_device).start()

        def later(t, carry):
            @pl.when(t < UNITS)
            def _():
                form(t)

            fresh = jnp.logical_or(on_second, t >= EARLY + LAG_CORE)

            @pl.when(jnp.logical_and(fresh, jnp.logical_and(t >= LAG_CORE, t < UNITS + LAG_CORE)))
            def _():
                over_core(t - LAG_CORE)

            @pl.when(jnp.logical_and(t >= LAG_X, t < UNITS + LAG_X))
            def _():
                over_x(t - LAG_X)

            @pl.when(t >= LAG_Z)
            def _():
                over_z(t - LAG_Z)

            @pl.when(t == 16)
            def _():
                gain_copy(0, core_device).wait()
                gain_held[1] = gain_held[0] + gain_in[0]
                gain_copy(1, x_device).start()

            @pl.when(t == 22)
            def _():
                gain_copy(1, x_device).wait()
                gain_held[2] = gain_held[1] + gain_in[1]
                for j in range(3):
                    gain_copy(2 + j, z_devices[j]).start()

            return carry

        lax.fori_loop((1 - section) * EARLY, UNITS + LAG_Z, later, 0)

        for j in range(3):
            gain_copy(2 + j, z_devices[j]).wait()
        total_gains = gain_held[2] + gain_in[2] + gain_in[3] + gain_in[4]
        chosen = (
            lax.broadcasted_iota(jnp.int32, (768, 48), 0)
            == lax.broadcasted_iota(jnp.int32, (768, 48), 1) + place * 48
        ).astype(F32)
        own_gains = jnp.dot(
            total_gains, chosen, precision=lax.Precision.HIGHEST, preferred_element_type=F32
        )
        gg_ref[...] = own_gains[:2]

        def finish(k, carry):
            @pl.when(k >= UNITS - HELD)
            def _():
                core_copy(k).wait_send()

            x_copy(k).wait_send()
            for j in range(3):
                z_copy(k, j).wait_send()
            return carry

        lax.fori_loop(0, UNITS, finish, 0)

    @pl.when(on_second)
    def _():
        for cell in range(2):
            relay_copy(cell, upstream).wait_send()


def run_kernel(scattering, acts, counts, cotangent, gains, weights):
    cells, length, width = acts.shape
    vmem = pl.BlockSpec(memory_space=pltpu.VMEM)
    anywhere = pl.BlockSpec(memory_space=pl.ANY)
    dma = pltpu.SemaphoreType.DMA
    held = (
        ((7, 768, cells * length), BF16),
        ((cells * length, 6912), BF16),
        ((8, 768), F32),
    )
    shares = (((48, 2304), F32), ((48, 768), F32), ((48, 3072), F32), ((192, 768), F32), ((2, 48), F32))
    outs = (((cells, length, width), F32),) + (shares if scattering else held)
    scratch = (held if scattering else ()) + (
        ((768, 2304), BF16),
        ((768, 768), BF16),
        ((768, 3072), BF16),
        ((3072, 768), BF16),
        ((cells, length, width), BF16),
        ((cells, length, width), BF16),
        ((cells, length, width), BF16),
        ((length, width), BF16),
        ((length, width), BF16),
        ((length, width), BF16),
        ((length, 3072), BF16),
        ((cells, HEADS // 2, 2 * length, length), BF16),
        ((cells, length, width), F32),
        ((cells, length, width), F32),
        ((cells, length, 128), F32),
        ((cells, length, 128), F32),
        ((length, width), F32),
        ((length, width), F32),
        ((length, width), F32),
        ((length, width), BF16),
    )
    semaphores = [dma((4,)), dma(()), dma((2,)), dma((2,))]
    travel = ()
    if scattering:
        travel = (
            ((HELD, 384, 256), BF16),
            ((HELD, 384, 256), F32),
            ((UNITS, 384, 256), BF16),
            ((UNITS, 192, 256), BF16),
            ((UNITS, 3, 48, 256), BF16),
            ((3, 8, 768), F32),
            ((5, 8, 768), F32),
        )
    travel_semaphores = [
        dma((UNITS,)), dma((UNITS,)), dma((UNITS,)), dma((UNITS,)),
        dma((UNITS, 3)), dma((UNITS, 3)), dma((5,)), dma((5,)),
    ] if scattering else []
    return pl.pallas_call(
        functools.partial(kernel, scattering),
        out_shape=tuple(jax.ShapeDtypeStruct(shape, kind) for shape, kind in outs),
        in_specs=[pl.BlockSpec(memory_space=pltpu.SMEM), vmem] + [anywhere] * 6,
        out_specs=(vmem,) * len(outs),
        scratch_shapes=[pltpu.VMEM(shape, kind) for shape, kind in scratch]
        + semaphores
        + [pltpu.VMEM(shape, kind) for shape, kind in travel]
        + travel_semaphores,
        compiler_params=pltpu.CompilerParams(
            collective_id=1 if scattering else 2,
            has_side_effects=True,
            vmem_limit_bytes=VMEM_BYTES,
        ),
        name="relay_layers",
    )(counts, gains, acts, cotangent, *weights)


def plain_scattered(turned, deltas, d_gains):
    d_low, d_up = deltas[:, :768], deltas[:, 768:3840]
    d_branch, d_qkv = deltas[:, 3840:4608], deltas[:, 4608:]
    rows = turned.shape[2]
    shares = turned.reshape(7, 2, 2, 4, 48, rows).transpose(3, 2, 1, 0, 4, 5).reshape(16, 7, 48, rows)
    scatter = functools.partial(lax.psum_scatter, axis_name="dp", scatter_dimension=0, tiled=True)
    return (
        lax.psum_scatter(d_gains[:2], "dp", scatter_dimension=1, tiled=True),
        scatter(dot(shares[:, 6].reshape(768, rows), d_qkv)),
        scatter(dot(shares[:, 5].reshape(768, rows), d_branch)),
        scatter(dot(shares[:, 4].reshape(768, rows), d_up)),
        scatter(dot(shares[:, :4].reshape(3072, rows), d_low)),
    )


def body(acts, counts, cotangent, norm_gains, w_qkv, w_out, w_up, w_down):
    weights = (w_qkv[0], w_out[0], w_up[0], w_down[0])
    if lax.axis_size("dp") == 16:
        ends, *shares, d_gains = run_kernel(True, acts, counts, cotangent, norm_gains[0], weights)
        shares = [d_gains] + shares
    else:
        ends, *held = run_kernel(False, acts, counts, cotangent, norm_gains[0], weights)
        shares = plain_scattered(*held)
    return (ends[None],) + tuple(share[None] for share in shares)


def solution(mesh):
    placed = (
        P("dp", None, None),
        P("dp"),
        P("dp", None, None),
        P("section", None, None),
        P("section", None, None),
        P("section", None, None),
        P("section", None, None),
        P("section", None, None),
    )
    return jax.shard_map(
        body,
        mesh=mesh,
        in_specs=placed,
        out_specs=(
            P("section", "dp", None, None),
            P("section", None, "dp"),
            P("section", "dp", None),
            P("section", "dp", None),
            P("section", "dp", None),
            P("section", "dp", None),
        ),
        check_vma=False,
    )
```

```python
import functools

import jax
import jax.numpy as jnp
from jax import lax
from jax.experimental import pallas as pl
from jax.experimental.pallas import tpu as pltpu
from jax.sharding import PartitionSpec as P

HEADS = 12
HD = 64
EPSILON = 1e-05
MESH = pl.DeviceIdType.MESH
F32 = jnp.float32
BF16 = jnp.bfloat16

UNITS = 36
Z_FIRST = 6
X_FIRST = UNITS - Z_FIRST
EVERY = 5
EARLY = 10
LAG_CORE = 2
LAG_X = 4
LAG_NEAR = 7
LAG_FAR = 10
LAG_Z_NEAR = 6
LAG_Z_FAR = 9
LAG_Z_X = 12
HELD = 3
SHARE_ENDS = (20, 30, 33)
LINES = X_FIRST + 2 * Z_FIRST
VMEM_BYTES = 63 << 20


NT = (((1,), (1,)), ((), ()))
TN = (((0,), (0,)), ((), ()))


def dot(left, right):
    return jnp.dot(left, right, preferred_element_type=F32)


def dot_nt(left, right):
    return lax.dot_general(left, right, NT, preferred_element_type=F32)


def dot_tn(left, right):
    return lax.dot_general(left, right, TN, preferred_element_type=F32)


def gelu_and_slope(u):
    share = 0.5 + 0.5 * lax.erf(u * 0.5 ** 0.5)
    bell = jnp.exp(-0.5 * (u * u))
    return u * share, share + u * (bell * 0.3989422804014327)


def kernel(
    scattering, counts_ref, gains_ref, acts_ref, cotangent_ref, wq_hbm, wo_hbm, wu_hbm, wd_hbm,
    ends_ref, *rest,
):
    if scattering:
        gq_ref, go_ref, gu_ref, gd_ref, gg_ref, turned, deltas_ref, gain_ref = rest[:8]
        gq_out, go_out, gu_out, gd_out, out_sem = rest[8:13]
        (core_out, keep_core, core_in, x_in, last_in, near_in, far_in, gain_held, gain_in,
         core_send, core_recv, x_send, x_recv, near_send, near_recv, far_send, far_recv,
         gain_send, gain_recv) = rest[-19:]
        rest = rest[13:-19]
    else:
        turned, deltas_ref, gain_ref = rest[:3]
        rest = rest[3:]
    (wq, wo, wu, wd, source, upstream, relayed, a_ref, o_ref, b_ref, f_ref, probs,
     normed_1, normed_2, scale_1, scale_2, mid, wide, ends_out,
     weight_sem, input_sem, send_sem, recv_sem, ends_sem) = rest
    d_mid, d_mixed = mid, a_ref

    section = lax.axis_index("section")
    place = lax.axis_index("dp")
    partner = (1 - section, place)
    on_first = section == 0
    on_second = section == 1
    rows_in = source.shape[1]
    pairs = HEADS // 2

    z = place // 4
    x = (place // 2) % 2
    core = place % 2
    far_z = (z + 1 - 2 * (z % 2), (z + 2) % 4, 3 - z)
    core_device = (section, z * 4 + x * 2 + 1 - core)
    x_device = (section, z * 4 + (1 - x) * 2 + core)
    z_devices = [(section, other * 4 + x * 2 + core) for other in far_z]
    met = [partner] + ([core_device, x_device] + z_devices if scattering else [])

    barrier = pltpu.get_barrier_semaphore()
    for device in met:
        pl.semaphore_signal(barrier, inc=1, device_id=device, device_id_type=MESH)

    loads = [
        pltpu.make_async_copy(hbm, vmem, weight_sem.at[at])
        for at, (hbm, vmem) in enumerate(((wq_hbm, wq), (wo_hbm, wo), (wu_hbm, wu), (wd_hbm, wd)))
    ]
    acts_in = pltpu.make_async_copy(acts_ref, source, input_sem)
    cotangent_in = pltpu.make_async_copy(cotangent_ref, upstream, input_sem)

    @pl.when(on_first)
    def _():
        acts_in.start()

    loads[0].start()

    @pl.when(on_second)
    def _():
        cotangent_in.start()

    gain_ref[...] = jnp.zeros_like(gain_ref)

    @pl.when(on_first)
    def _():
        acts_in.wait()

    @pl.when(on_second)
    def _():
        cotangent_in.wait()
        pl.semaphore_wait(barrier, len(met))

    low_lanes = lax.broadcasted_iota(jnp.int32, (rows_in, 128), 1) < HD

    def relay_copy(cell, target):
        return pltpu.make_async_remote_copy(
            src_ref=relayed.at[cell],
            dst_ref=target.at[cell],
            send_sem=send_sem.at[cell],
            recv_sem=recv_sem.at[cell],
            device_id=partner,
            device_id_type=MESH,
        )

    def ends_copy(cell):
        return pltpu.make_async_copy(ends_out.at[cell], ends_ref.at[cell], ends_sem.at[cell])

    def place_of(share):
        return (share % 2) * 384 + ((share // 2) % 2) * 192 + (share // 4) * 48

    def turn(cell, ref, left):
        lanes = pl.ds(pl.multiple_of(cell * rows_in, 256), rows_in)
        for part in range(2):
            block = ref[:, part * 384:part * 384 + 384].T
            for at in range(8):
                start = place_of(part * 8 + at)
                turned[left, start:start + 48, lanes] = block[at * 48:at * 48 + 48]

    def turn_wide(cell):
        lanes = pl.ds(pl.multiple_of(cell * rows_in, 256), rows_in)
        for part in range(8):
            block = f_ref[:, part * 384:part * 384 + 384].T
            for at in range(8):
                start = place_of(part * 2 + at // 4)
                turned[at % 4, start:start + 48, lanes] = block[at * 48:at * 48 + 48]

    def stacked(pair_block):
        none = jnp.zeros_like(pair_block)
        return jnp.concatenate(
            [jnp.where(low_lanes, pair_block, none), jnp.where(low_lanes, none, pair_block)], axis=0
        )

    def unstacked(block):
        return jnp.where(low_lanes, block[:rows_in], block[rows_in:])

    def columns(start, width=128):
        return pl.ds(pl.multiple_of(start, 128), width)

    def norm_rows(values, row_gain, at, rows, normed, scale):
        centred = values - jnp.mean(values, axis=-1, keepdims=True)
        spread = jnp.mean(centred * centred, axis=-1, keepdims=True)
        factor = lax.rsqrt(spread + EPSILON)
        unit = centred * factor
        normed[at, rows, :] = unit
        scale[at, rows, :] = jnp.broadcast_to(factor, (values.shape[0], 128))
        return (unit * row_gain).astype(BF16)

    def norm_back(d_normed, row_gain, at, rows, normed, scale, gain_row):
        unit = normed[at, rows, :]
        product = d_normed * unit
        gain_ref[gain_row:gain_row + 1, :] += jnp.sum(product, axis=0, keepdims=True)
        e = d_normed * row_gain
        mean_e = jnp.mean(e, axis=-1, keepdims=True)
        mean_en = jnp.mean(product * row_gain, axis=-1, keepdims=True)
        return scale[at, rows, :1] * (e - mean_e - unit * mean_en)

    def whole(cell):
        return pl.ds(pl.multiple_of(cell * rows_in, 256), rows_in)

    def some(cell, part):
        return pl.ds(pl.multiple_of(cell * rows_in + part * 64, 64), 64)

    def norm_source(cell):
        for part in range(4):
            a_ref[part * 64:part * 64 + 64, :] = norm_rows(
                source[cell, pl.ds(part * 64, 64), :].astype(F32),
                gains_ref[0:1, :], cell, pl.ds(part * 64, 64), normed_1, scale_1,
            )

    def project_qkv(cell):
        a = a_ref[...]
        turn(cell, a_ref, 6)
        for tile in range(9):
            cols = slice(tile * 256, tile * 256 + 256)
            block = dot(a, wq[:, cols])
            if tile < 3:
                block = block.astype(BF16).astype(F32) * HD ** -0.5
            deltas_ref[whole(cell), tile * 256 + 4608:tile * 256 + 4864] = block.astype(BF16)

    def attention(cell):
        valid = lax.broadcasted_iota(jnp.int32, (1, rows_in), 1) < counts_ref[cell]

        def attend(pair, carry):
            start = pair * 128
            queries = stacked(deltas_ref[whole(cell), columns(start + 4608)])
            scores = dot_nt(queries, deltas_ref[whole(cell), columns(start + 5376)])
            scores = jnp.where(valid, scores, -1e30)
            raised = jnp.exp(scores - jnp.max(scores, axis=-1, keepdims=True))
            soft = raised * (1.0 / jnp.sum(raised, axis=-1, keepdims=True))
            soft = soft.astype(BF16)
            probs[cell, pair] = soft
            mixed = dot(soft, deltas_ref[whole(cell), columns(start + 6144)])
            o_ref[:, columns(start)] = unstacked(mixed).astype(BF16)
            return carry

        lax.fori_loop(0, pairs, attend, 0, unroll=True)

    def project_out(cell):
        o = o_ref[...]
        turn(cell, o_ref, 5)
        for tile in range(3):
            cols = slice(tile * 256, tile * 256 + 256)
            mid[:, cols] = source[cell, :, cols].astype(F32) + dot(o, wo[:, cols])

    def norm_mid(cell):
        for part in range(4):
            rows = pl.ds(part * 64, 64)
            b_ref[rows, :] = norm_rows(
                mid[rows, :], gains_ref[1:2, :], cell, rows, normed_2, scale_2
            )

    def go_up(cell):
        turn(cell, b_ref, 4)

        def rise(tile, carry):
            cols = columns(tile * 256, 256)
            u = dot(b_ref[...], wu[:, cols])
            value, steep = gelu_and_slope(u)
            f_ref[:, cols] = value.astype(BF16)
            deltas_ref[whole(cell), columns(tile * 256 + 768, 256)] = steep.astype(BF16)
            return carry

        lax.fori_loop(0, 12, rise, 0, unroll=True)

    def go_down(cell):
        f = f_ref[...]
        turn_wide(cell)
        for tile in range(3):
            cols = slice(tile * 256, tile * 256 + 256)
            result = mid[:, cols] + dot(f, wd[:, cols])
            ends_out[cell, :, cols] = result
            relayed[cell, :, cols] = result.astype(BF16)

    def back_down(cell):
        deltas_ref[whole(cell), 0:768] = upstream[cell]

        def fall(tile, carry):
            start = pl.multiple_of(tile * 256, 256)
            d_active = dot_nt(upstream[cell], wd[pl.ds(start, 256), :])
            d_up = d_active * deltas_ref[whole(cell), columns(start + 768, 256)].astype(F32)
            deltas_ref[whole(cell), columns(start + 768, 256)] = d_up.astype(BF16)
            return carry

        lax.fori_loop(0, 12, fall, 0, unroll=True)

    def back_up(cell):
        d_up = deltas_ref[whole(cell), 768:3840]
        for tile in range(3):
            wide[:, tile * 256:tile * 256 + 256] = dot_nt(
                d_up, wu[tile * 256:tile * 256 + 256, :]
            )

    def norm_mid_back(cell):
        for part in range(4):
            rows = pl.ds(part * 64, 64)
            total = upstream[cell, rows, :].astype(F32) + norm_back(
                wide[rows, :], gains_ref[1:2, :], cell, rows, normed_2, scale_2, 1
            )
            d_mid[rows, :] = total
            deltas_ref[some(cell, part), 3840:4608] = total.astype(BF16)

    def back_out(cell):
        d_branch = deltas_ref[whole(cell), 3840:4608]
        for tile in range(3):
            d_mixed[:, tile * 256:tile * 256 + 256] = dot_nt(
                d_branch, wo[tile * 256:tile * 256 + 256, :]
            ).astype(BF16)

    def attention_back(cell):
        def attend_back(pair, carry):
            start = pair * 128
            queries = stacked(deltas_ref[whole(cell), columns(start + 4608)])
            key_rows = deltas_ref[whole(cell), columns(start + 5376)]
            d_out = stacked(d_mixed[:, columns(start)])
            soft = probs[cell, pair]
            d_values = dot_tn(soft, d_out)
            d_soft = dot_nt(d_out, deltas_ref[whole(cell), columns(start + 6144)])
            soft = soft.astype(F32)
            inner = jnp.sum(soft * d_soft, axis=-1, keepdims=True)
            d_scores = (soft * (d_soft - inner)).astype(BF16)
            d_queries = unstacked(dot(d_scores, key_rows)) * HD ** -0.5
            d_keys = dot_tn(d_scores, queries)
            deltas_ref[whole(cell), columns(start + 4608)] = d_queries.astype(BF16)
            deltas_ref[whole(cell), columns(start + 5376)] = d_keys.astype(BF16)
            deltas_ref[whole(cell), columns(start + 6144)] = d_values.astype(BF16)
            return carry

        lax.fori_loop(0, pairs, attend_back, 0, unroll=True)

    def back_qkv(cell):
        d_qkv = deltas_ref[whole(cell), 4608:6912]
        for tile in range(3):
            wide[:, tile * 256:tile * 256 + 256] = dot_nt(
                d_qkv, wq[tile * 256:tile * 256 + 256, :]
            )

    def norm_source_back(cell):
        for part in range(4):
            rows = pl.ds(part * 64, 64)
            total = d_mid[rows, :] + norm_back(
                wide[rows, :], gains_ref[0:1, :], cell, rows, normed_1, scale_1, 0
            )

            relayed[cell, rows, :] = total.astype(BF16)

            @pl.when(on_first)
            def _():
                ends_out[cell, rows, :] = total

    def weights_here(t, at):
        @pl.when(t == 0)
        def _():
            loads[at].wait()

    def forward(t, cell):
        @pl.when(on_second)
        def _():
            relay_copy(cell, source).wait_recv()

        norm_source(cell)

        @pl.when(t == 0)
        def _():
            loads[0].wait()
            for load in loads[1:]:
                load.start()

        project_qkv(cell)
        attention(cell)
        weights_here(t, 1)
        project_out(cell)
        norm_mid(cell)
        weights_here(t, 2)
        go_up(cell)
        weights_here(t, 3)
        go_down(cell)

        @pl.when(on_second)
        def _():
            ends_copy(cell).start()

        @pl.when(on_first)
        def _():
            @pl.when(t == 0)
            def _():
                pl.semaphore_wait(barrier, len(met))

            relay_copy(cell, source).start()

    def nothing(at):
        del at

    def backward(cell, between=nothing):
        back_down(cell)
        between(0)
        back_up(cell)
        between(1)
        norm_mid_back(cell)
        back_out(cell)
        between(2)
        attention_back(cell)
        between(3)
        back_qkv(cell)
        norm_source_back(cell)

        @pl.when(on_second)
        def _():
            relay_copy(cell, upstream).start()

        @pl.when(on_first)
        def _():
            ends_copy(cell).start()

        between(4)

    def receive_gradient(cell):
        @pl.when(on_first)
        def _():
            relay_copy(cell, source).wait_send()
            relay_copy(cell, upstream).wait_recv()

        deltas_ref[whole(cell), 0:768] = upstream[cell]

    def step(t, carry):
        backwards = (1 - section) * (t // 2) + section * (t % 2)
        cell = (1 - section) * (t % 2) + section * (t // 2)

        @pl.when(backwards == 0)
        def _():
            forward(t, cell)

        @pl.when(backwards == 1)
        def _():
            receive_gradient(cell)
            backward(cell)

        return carry

    lax.fori_loop(0, 3 if scattering else 4, step, 0)

    if scattering:
        def gain_copy(at, device):
            return pltpu.make_async_remote_copy(
                src_ref=gain_held.at[min(at, 2)],
                dst_ref=gain_in.at[at],
                send_sem=gain_send.at[at],
                recv_sem=gain_recv.at[at],
                device_id=device,
                device_id_type=MESH,
            )

        inner = jnp.logical_or(z == 1, z == 2)
        outer = jnp.logical_or(z == 0, z == 3)
        near_device, far_device, mirror_device = z_devices
        leaving = (3 - z) // 3 * 48
        crossing = (2 - z) * 96
        crossing_in = (2 - z) * 48
        own_in = (z // 2) * (1 - z // 3) * 96

        def block(start, count=48):
            return pl.ds(pl.multiple_of(start, 16), count)

        def z_unit(i):
            return i * (EVERY + 1)

        def x_unit(j):
            return j + j // EVERY + 1

        def core_copy(k, room):
            return pltpu.make_async_remote_copy(
                src_ref=core_out.at[room], dst_ref=core_in.at[k],
                send_sem=core_send.at[k], recv_sem=core_recv.at[k],
                device_id=core_device, device_id_type=MESH,
            )

        def x_copy(j):
            return pltpu.make_async_remote_copy(
                src_ref=core_in.at[x_unit(j), block((1 - x) * 192, 192)], dst_ref=x_in.at[j],
                send_sem=x_send.at[j], recv_sem=x_recv.at[j],
                device_id=x_device, device_id_type=MESH,
            )

        def last_copy(i):
            return pltpu.make_async_remote_copy(
                src_ref=core_in.at[z_unit(i), block((1 - x) * 192 + z * 48)], dst_ref=last_in.at[i],
                send_sem=x_send.at[X_FIRST + i], recv_sem=x_recv.at[X_FIRST + i],
                device_id=x_device, device_id_type=MESH,
            )

        def x_line(j):
            return x_in.at[j], 0, j

        def z_lines(i):
            return [(core_in.at[z_unit(i)], side * 192, X_FIRST + 2 * i + side) for side in range(2)]

        def near_copy(line, from_outer):
            ref, base, slot = line
            if from_outer:
                source, target = ref.at[block(base + leaving, 144)], near_in.at[slot]
            else:
                source = ref.at[block(base + far_z[0] * 48)]
                target = near_in.at[slot, pl.ds(0, 48)]
            return pltpu.make_async_remote_copy(
                src_ref=source, dst_ref=target,
                send_sem=near_send.at[slot], recv_sem=near_recv.at[slot],
                device_id=near_device, device_id_type=MESH,
            )

        def far_copy(line, at):
            ref, base, slot = line
            target, device = ((far_z[2], mirror_device), (far_z[1], far_device))[at]
            return pltpu.make_async_remote_copy(
                src_ref=ref.at[block(base + target * 48)], dst_ref=far_in.at[slot],
                send_sem=far_send.at[slot, at], recv_sem=far_recv.at[slot],
                device_id=device, device_id_type=MESH,
            )

        def start_line(line):
            @pl.when(outer)
            def _():
                near_copy(line, True).start()

            @pl.when(inner)
            def _():
                near_copy(line, False).start()

        def pass_line(line):
            @pl.when(inner)
            def _():
                ref, base, slot = line
                near_copy(line, True).wait_recv()
                rows = block(base + crossing, 96)
                total = ref[rows, :].astype(F32) + near_in[slot, block(crossing_in, 96), :].astype(F32)
                ref[rows, :] = total.astype(BF16)
                far_copy(line, 0).start()
                far_copy(line, 1).start()

        def end_line(line):
            ref, base, slot = line

            @pl.when(outer)
            def _():
                near_copy(line, False).wait_recv()

            far_copy(line, 0).wait_recv()
            return (
                ref[block(base + z * 48), :].astype(F32)
                + near_in[slot, block(own_in), :].astype(F32)
                + far_in[slot].astype(F32)
            )

        def wait_line_sends(line):
            @pl.when(outer)
            def _():
                near_copy(line, True).wait_send()

            @pl.when(inner)
            def _():
                near_copy(line, False).wait_send()
                far_copy(line, 0).wait_send()
                far_copy(line, 1).wait_send()

        def form(k, room):
            down = (k < 12).astype(jnp.int32)
            left = down * (k // 3) + (1 - down) * (
                4 + (k >= 24).astype(jnp.int32) + (k >= 27).astype(jnp.int32)
            )
            right = down * (k % 3) + (1 - down) * (k - 9)
            delta = deltas_ref[:, columns(right * 256, 256)]
            away = turned[left, block((1 - core) * 384, 384), :]
            core_out[room] = dot(away, delta).astype(BF16)
            core_copy(k, room).start()
            own = turned[left, block(core * 384, 384), :]
            keep_core[room] = dot(own, delta)

        def form_z(i):
            @pl.when(i >= 1)
            def _():
                core_copy(z_unit(i - 1), HELD).wait_send()

            form(z_unit(i), HELD)

        def form_x(j):
            @pl.when(j >= HELD)
            def _():
                core_copy(x_unit(j - HELD), j % HELD).wait_send()

            form(x_unit(j), j % HELD)

        def over_core(k, room):
            core_copy(k, room).wait_recv()
            core_in[k] = (keep_core[room] + core_in[k].astype(F32)).astype(BF16)

        def over_core_z(i):
            over_core(z_unit(i), HELD)
            for line in z_lines(i):
                start_line(line)

        def over_core_x(j):
            over_core(x_unit(j), j % HELD)
            x_copy(j).start()

        def over_x(j):
            x_copy(j).wait_recv()
            own = core_in[x_unit(j), block(x * 192, 192), :].astype(F32)
            x_in[j] = (own + x_in[j].astype(F32)).astype(BF16)
            start_line(x_line(j))

        def pass_z(i):
            for line in z_lines(i):
                pass_line(line)

        def end_z(i):
            for ref, base, slot in z_lines(i):
                ref[block(base + z * 48), :] = end_line((ref, base, slot)).astype(BF16)
            last_copy(i).start()

        def store(k, total):
            @pl.when(k < 12)
            def _():
                rows = pl.ds(pl.multiple_of((k // 3) * 48, 8), 48)
                gd_out[rows, columns((k % 3) * 256, 256)] = total

            @pl.when(jnp.logical_and(k >= 12, k < 24))
            def _():
                gu_out[:, columns((k - 12) * 256, 256)] = total

            @pl.when(jnp.logical_and(k >= 24, k < 27))
            def _():
                go_out[:, columns((k - 24) * 256, 256)] = total

            @pl.when(k >= 27)
            def _():
                gq_out[:, columns((k - 27) * 256, 256)] = total

        def over_last(i):
            last_copy(i).wait_recv()
            own = core_in[z_unit(i), block(x * 192 + z * 48), :].astype(F32)
            store(z_unit(i), own + last_in[i].astype(F32))

        def end_x(j):
            store(x_unit(j), end_line(x_line(j)))

        share_copies = [
            pltpu.make_async_copy(vmem, hbm, out_sem.at[at])
            for at, (vmem, hbm) in enumerate(
                ((gd_out, gd_ref), (gu_out, gu_ref), (go_out, go_ref), (gq_out, gq_ref))
            )
        ]

        receive_gradient(1)

        @pl.when(on_first)
        def _():
            def early(t, carry):
                @pl.when(jnp.logical_and(t < EARLY, t % EVERY == 0))
                def _():
                    form_z(t // EVERY)

                @pl.when(t < EARLY)
                def _():
                    form_x(t)

                @pl.when(jnp.logical_and(t >= LAG_CORE, t % EVERY == LAG_CORE))
                def _():
                    over_core_z(t // EVERY)

                @pl.when(t >= LAG_CORE)
                def _():
                    over_core_x(t - LAG_CORE)

                return carry

            lax.fori_loop(0, EARLY + LAG_CORE, early, 0)

        def between(at):
            @pl.when(on_first)
            def _():
                for j in ((0, 1, 2), (3,), (4,), (5,), ())[at]:
                    over_x(j)
                if at == 1:
                    pass_z(0)
                for j in ((), (), (0,), (1,), (2,))[at]:
                    pass_line(x_line(j))
                if at == 3:
                    end_z(0)

        backward(1, between)

        gain_held[0] = gain_ref[...]
        gain_copy(0, core_device).start()

        def later(t, carry):
            def at(lag, low, high, work):
                @pl.when(jnp.logical_and(t >= lag + low, t < lag + high))
                def _():
                    work(t - lag)

            def at_z(lag, work):
                @pl.when(jnp.logical_and(
                    (t - lag) % EVERY == 0, jnp.logical_and(t >= lag, t < lag + X_FIRST)
                ))
                def _():
                    work((t - lag) // EVERY)

            at_z(0, form_z)
            at(0, 0, X_FIRST, form_x)

            @pl.when(jnp.logical_or(on_second, t >= EARLY + LAG_CORE))
            def _():
                at_z(LAG_CORE, over_core_z)
                at(LAG_CORE, 0, X_FIRST, over_core_x)

            at(LAG_X, 0, X_FIRST, over_x)
            at_z(LAG_Z_NEAR, pass_z)
            at(LAG_NEAR, 0, X_FIRST, lambda j: pass_line(x_line(j)))
            at_z(LAG_Z_FAR, end_z)
            at_z(LAG_Z_X, over_last)
            at(LAG_FAR, 0, X_FIRST, end_x)
            for copy, last in zip(share_copies, SHARE_ENDS):
                @pl.when(t == last)
                def _():
                    copy.start()

            @pl.when(t == 16)
            def _():
                gain_copy(0, core_device).wait()
                gain_held[1] = gain_held[0] + gain_in[0]
                gain_copy(1, x_device).start()

            @pl.when(t == 22)
            def _():
                gain_copy(1, x_device).wait()
                gain_held[2] = gain_held[1] + gain_in[1]
                for j in range(3):
                    gain_copy(2 + j, z_devices[j]).start()

            return carry

        lax.fori_loop((1 - section) * EARLY, X_FIRST + LAG_FAR, later, 0)
        share_copies[3].start()

        for j in range(3):
            gain_copy(2 + j, z_devices[j]).wait()
        total_gains = gain_held[2] + gain_in[2] + gain_in[3] + gain_in[4]
        chosen = (
            lax.broadcasted_iota(jnp.int32, (768, 48), 0)
            == lax.broadcasted_iota(jnp.int32, (768, 48), 1) + place * 48
        ).astype(F32)
        own_gains = jnp.dot(
            total_gains, chosen, precision=lax.Precision.HIGHEST, preferred_element_type=F32
        )
        gg_ref[...] = own_gains[:2]

        def finish_x(j, carry):
            @pl.when(j >= X_FIRST - HELD)
            def _():
                core_copy(x_unit(j), j % HELD).wait_send()

            x_copy(j).wait_send()
            wait_line_sends(x_line(j))
            return carry

        def finish_z(i, carry):
            for line in z_lines(i):
                wait_line_sends(line)
            last_copy(i).wait_send()
            return carry

        core_copy(z_unit(Z_FIRST - 1), HELD).wait_send()
        lax.fori_loop(0, X_FIRST, finish_x, 0)
        lax.fori_loop(0, Z_FIRST, finish_z, 0)
        for copy in share_copies:
            copy.wait()

    for cell in range(2):
        ends_copy(cell).wait()

    @pl.when(on_second)
    def _():
        for cell in range(2):
            relay_copy(cell, upstream).wait_send()


def run_kernel(scattering, acts, counts, cotangent, gains, weights):
    cells, length, width = acts.shape
    vmem = pl.BlockSpec(memory_space=pltpu.VMEM)
    anywhere = pl.BlockSpec(memory_space=pl.ANY)
    dma = pltpu.SemaphoreType.DMA
    held = (
        ((7, 768, cells * length), BF16),
        ((cells * length, 6912), BF16),
        ((8, 768), F32),
    )
    shares = (((48, 2304), F32), ((48, 768), F32), ((48, 3072), F32), ((192, 768), F32), ((2, 48), F32))
    outs = (((cells, length, width), F32),) + (shares if scattering else held)
    first = [pltpu.VMEM(shape, kind) for shape, kind in held + shares[:4]] + [dma((4,))]
    scratch = (
        ((768, 2304), BF16),
        ((768, 768), BF16),
        ((768, 3072), BF16),
        ((3072, 768), BF16),
        ((cells, length, width), BF16),
        ((cells, length, width), BF16),
        ((cells, length, width), BF16),
        ((length, width), BF16),
        ((length, width), BF16),
        ((length, width), BF16),
        ((length, 3072), BF16),
        ((cells, HEADS // 2, 2 * length, length), BF16),
        ((cells, length, width), F32),
        ((cells, length, width), F32),
        ((cells, length, 128), F32),
        ((cells, length, 128), F32),
        ((length, width), F32),
        ((length, width), F32),
        ((cells, length, width), F32),
    )
    semaphores = [dma((4,)), dma(()), dma((2,)), dma((2,)), dma((2,))]
    travel = ()
    if scattering:
        travel = (
            ((HELD + 1, 384, 256), BF16),
            ((HELD + 1, 384, 256), F32),
            ((UNITS, 384, 256), BF16),
            ((X_FIRST, 192, 256), BF16),
            ((Z_FIRST, 48, 256), BF16),
            ((LINES, 144, 256), BF16),
            ((LINES, 48, 256), BF16),
            ((3, 8, 768), F32),
            ((5, 8, 768), F32),
        )
    travel_semaphores = [
        dma((UNITS,)), dma((UNITS,)), dma((UNITS,)), dma((UNITS,)),
        dma((LINES,)), dma((LINES,)), dma((LINES, 2)), dma((LINES,)),
        dma((5,)), dma((5,)),
    ] if scattering else []
    return pl.pallas_call(
        functools.partial(kernel, scattering),
        out_shape=tuple(jax.ShapeDtypeStruct(shape, kind) for shape, kind in outs),
        in_specs=[pl.BlockSpec(memory_space=pltpu.SMEM), vmem] + [anywhere] * 6,
        out_specs=(anywhere,) + ((anywhere,) * 4 + (vmem,) if scattering else (vmem,) * 3),
        scratch_shapes=(first if scattering else [])
        + [pltpu.VMEM(shape, kind) for shape, kind in scratch]
        + semaphores
        + [pltpu.VMEM(shape, kind) for shape, kind in travel]
        + travel_semaphores,
        compiler_params=pltpu.CompilerParams(
            collective_id=1 if scattering else 2,
            has_side_effects=True,
            vmem_limit_bytes=VMEM_BYTES,
        ),
        name="relay_layers",
    )(counts, gains, acts, cotangent, *weights)


def hand_over_kernel(*refs):
    count = (len(refs) - 2) // 3
    sources, targets, rooms = (refs[at * count:(at + 1) * count] for at in range(3))
    read_sem, write_sem = refs[-2:]
    pieces = []
    for source, target, room in zip(sources, targets, rooms):
        if len(source.shape) == 3:
            for cell in range(source.shape[0]):
                pieces.append((source.at[cell], room.at[cell], target.at[cell]))
        else:
            pieces.append((source, room, target))
    reads, writes = [], []
    for at, (source, room, target) in enumerate(pieces):
        reads.append(pltpu.make_async_copy(source, room, read_sem.at[at]))
        writes.append(pltpu.make_async_copy(room, target, write_sem.at[at]))
    for read in reads:
        read.start()
    for read, write in zip(reads, writes):
        read.wait()
        write.start()
    for write in writes:
        write.wait()


def hand_over(*arrays):
    anywhere = pl.BlockSpec(memory_space=pl.ANY)
    sem = pltpu.SemaphoreType.DMA((len(arrays) + 1,))
    return pl.pallas_call(
        hand_over_kernel,
        out_shape=tuple(jax.ShapeDtypeStruct(array.shape, array.dtype) for array in arrays),
        in_specs=[anywhere] * len(arrays),
        out_specs=(anywhere,) * len(arrays),
        scratch_shapes=[pltpu.VMEM(array.shape, array.dtype) for array in arrays] + [sem, sem],
        name="hand_over",
    )(*arrays)


def plain_scattered(turned, deltas, d_gains):
    d_low, d_up = deltas[:, :768], deltas[:, 768:3840]
    d_branch, d_qkv = deltas[:, 3840:4608], deltas[:, 4608:]
    rows = turned.shape[2]
    shares = turned.reshape(7, 2, 2, 4, 48, rows).transpose(3, 2, 1, 0, 4, 5).reshape(16, 7, 48, rows)
    scatter = functools.partial(lax.psum_scatter, axis_name="dp", scatter_dimension=0, tiled=True)
    return (
        lax.psum_scatter(d_gains[:2], "dp", scatter_dimension=1, tiled=True),
        scatter(dot(shares[:, 6].reshape(768, rows), d_qkv)),
        scatter(dot(shares[:, 5].reshape(768, rows), d_branch)),
        scatter(dot(shares[:, 4].reshape(768, rows), d_up)),
        scatter(dot(shares[:, :4].reshape(3072, rows), d_low)),
    )


def body(acts, counts, cotangent, norm_gains, w_qkv, w_out, w_up, w_down):
    weights = (w_qkv[0], w_out[0], w_up[0], w_down[0])
    if lax.axis_size("dp") == 16:
        ends, *shares, d_gains = hand_over(
            *run_kernel(True, acts, counts, cotangent, norm_gains[0], weights)
        )
        shares = [d_gains] + shares
    else:
        ends, *held = run_kernel(False, acts, counts, cotangent, norm_gains[0], weights)
        shares = plain_scattered(*held)
    return (ends[None],) + tuple(share[None] for share in shares)


def solution(mesh):
    placed = (
        P("dp", None, None),
        P("dp"),
        P("dp", None, None),
        P("section", None, None),
        P("section", None, None),
        P("section", None, None),
        P("section", None, None),
        P("section", None, None),
    )
    return jax.shard_map(
        body,
        mesh=mesh,
        in_specs=placed,
        out_specs=(
            P("section", "dp", None, None),
            P("section", None, "dp"),
            P("section", "dp", None),
            P("section", "dp", None),
            P("section", "dp", None),
            P("section", "dp", None),
        ),
        check_vma=False,
    )
```

```python
import functools

import jax
import jax.numpy as jnp
from jax import lax
from jax.experimental import pallas as pl
from jax.experimental.pallas import tpu as pltpu
from jax.sharding import PartitionSpec as P

HEADS = 12
HD = 64
EPSILON = 1e-05
MESH = pl.DeviceIdType.MESH
F32 = jnp.float32
BF16 = jnp.bfloat16

UNITS = 36
Z_FIRST = 6
X_FIRST = UNITS - Z_FIRST
EVERY = 5
EARLY = 10
LAG_CORE = 2
LAG_X = 4
LAG_NEAR = 6
LAG_FAR = 10
LAG_Z_NEAR = 6
LAG_Z_FAR = 9
LAG_Z_X = 12
LAG_SENT = 14
HELD = 3
SHARE_ENDS = (20, 30, 33)
LINES = X_FIRST + 2 * Z_FIRST
VMEM_BYTES = 63 << 20


NT = (((1,), (1,)), ((), ()))
TN = (((0,), (0,)), ((), ()))


def dot(left, right):
    return jnp.dot(left, right, preferred_element_type=F32)


def dot_nt(left, right):
    return lax.dot_general(left, right, NT, preferred_element_type=F32)


def dot_tn(left, right):
    return lax.dot_general(left, right, TN, preferred_element_type=F32)


def gelu_and_slope(u):
    share = 0.5 + 0.5 * lax.erf(u * 0.5 ** 0.5)
    bell = jnp.exp(-0.5 * (u * u))
    return u * share, share + u * (bell * 0.3989422804014327)


def kernel(
    scattering, counts_ref, gains_ref, acts_ref, cotangent_ref, wq_hbm, wo_hbm, wu_hbm, wd_hbm,
    ends_ref, *rest,
):
    if scattering:
        gq_ref, go_ref, gu_ref, gd_ref, gg_ref, turned, deltas_ref, gain_ref = rest[:8]
        gq_out, go_out, gu_out, gd_out, out_sem = rest[8:13]
        (core_out, keep_core, core_in, x_in, last_in, near_in, far_in, gain_held, gain_in,
         core_send, core_recv, x_send, x_recv, near_send, near_recv, far_send, far_recv,
         gain_send, gain_recv) = rest[-19:]
        rest = rest[13:-19]
    else:
        turned, deltas_ref, gain_ref = rest[:3]
        rest = rest[3:]
    (wq, wo, wu, wd, source, upstream, relayed, a_ref, o_ref, b_ref, f_ref, probs,
     normed_1, normed_2, scale_1, scale_2, mid, wide, ends_out,
     weight_sem, input_sem, send_sem, recv_sem, ends_sem) = rest
    d_mid, d_mixed = mid, a_ref

    section = lax.axis_index("section")
    place = lax.axis_index("dp")
    partner = (1 - section, place)
    on_first = section == 0
    on_second = section == 1
    rows_in = source.shape[1]
    pairs = HEADS // 2

    z = place // 4
    x = (place // 2) % 2
    core = place % 2
    far_z = (z + 1 - 2 * (z % 2), (z + 2) % 4, 3 - z)
    core_device = (section, z * 4 + x * 2 + 1 - core)
    x_device = (section, z * 4 + (1 - x) * 2 + core)
    z_devices = [(section, other * 4 + x * 2 + core) for other in far_z]
    met = [partner] + ([core_device, x_device] + z_devices if scattering else [])

    barrier = pltpu.get_barrier_semaphore()
    for device in met:
        pl.semaphore_signal(barrier, inc=1, device_id=device, device_id_type=MESH)

    loads = [
        pltpu.make_async_copy(hbm, vmem, weight_sem.at[at])
        for at, (hbm, vmem) in enumerate(((wq_hbm, wq), (wo_hbm, wo), (wu_hbm, wu), (wd_hbm, wd)))
    ]
    acts_in = pltpu.make_async_copy(acts_ref, source, input_sem)
    cotangent_in = pltpu.make_async_copy(cotangent_ref, upstream, input_sem)

    @pl.when(on_first)
    def _():
        acts_in.start()

    loads[0].start()

    @pl.when(on_second)
    def _():
        cotangent_in.start()

    gain_ref[...] = jnp.zeros_like(gain_ref)

    @pl.when(on_first)
    def _():
        acts_in.wait()

    @pl.when(on_second)
    def _():
        cotangent_in.wait()
        pl.semaphore_wait(barrier, len(met))

    low_lanes = lax.broadcasted_iota(jnp.int32, (rows_in, 128), 1) < HD

    def relay_copy(cell, target):
        return pltpu.make_async_remote_copy(
            src_ref=relayed.at[cell],
            dst_ref=target.at[cell],
            send_sem=send_sem.at[cell],
            recv_sem=recv_sem.at[cell],
            device_id=partner,
            device_id_type=MESH,
        )

    def ends_copy(cell):
        return pltpu.make_async_copy(ends_out.at[cell], ends_ref.at[cell], ends_sem.at[cell])

    def place_of(share):
        return (share % 2) * 384 + ((share // 2) % 2) * 192 + (share // 4) * 48

    def turn(cell, ref, left):
        lanes = pl.ds(pl.multiple_of(cell * rows_in, 256), rows_in)
        for part in range(2):
            block = ref[:, part * 384:part * 384 + 384].T
            for at in range(8):
                start = place_of(part * 8 + at)
                turned[left, start:start + 48, lanes] = block[at * 48:at * 48 + 48]

    def turn_wide(cell):
        lanes = pl.ds(pl.multiple_of(cell * rows_in, 256), rows_in)
        for part in range(8):
            block = f_ref[:, part * 384:part * 384 + 384].T
            for at in range(8):
                start = place_of(part * 2 + at // 4)
                turned[at % 4, start:start + 48, lanes] = block[at * 48:at * 48 + 48]

    def stacked(pair_block):
        none = jnp.zeros_like(pair_block)
        return jnp.concatenate(
            [jnp.where(low_lanes, pair_block, none), jnp.where(low_lanes, none, pair_block)], axis=0
        )

    def unstacked(block):
        return jnp.where(low_lanes, block[:rows_in], block[rows_in:])

    def columns(start, width=128):
        return pl.ds(pl.multiple_of(start, 128), width)

    def norm_rows(values, row_gain, at, rows, normed, scale):
        centred = values - jnp.mean(values, axis=-1, keepdims=True)
        spread = jnp.mean(centred * centred, axis=-1, keepdims=True)
        factor = lax.rsqrt(spread + EPSILON)
        unit = centred * factor
        normed[at, rows, :] = unit
        scale[at, rows, :] = jnp.broadcast_to(factor, (values.shape[0], 128))
        return (unit * row_gain).astype(BF16)

    def norm_back(d_normed, row_gain, at, rows, normed, scale, gain_row):
        unit = normed[at, rows, :]
        product = d_normed * unit
        gain_ref[gain_row:gain_row + 1, :] += jnp.sum(product, axis=0, keepdims=True)
        e = d_normed * row_gain
        mean_e = jnp.mean(e, axis=-1, keepdims=True)
        mean_en = jnp.mean(product * row_gain, axis=-1, keepdims=True)
        return scale[at, rows, :1] * (e - mean_e - unit * mean_en)

    def whole(cell):
        return pl.ds(pl.multiple_of(cell * rows_in, 256), rows_in)

    def some(cell, part):
        return pl.ds(pl.multiple_of(cell * rows_in + part * 64, 64), 64)

    def norm_source(cell):
        for part in range(4):
            a_ref[part * 64:part * 64 + 64, :] = norm_rows(
                source[cell, pl.ds(part * 64, 64), :].astype(F32),
                gains_ref[0:1, :], cell, pl.ds(part * 64, 64), normed_1, scale_1,
            )

    def project_qkv(cell):
        a = a_ref[...]
        turn(cell, a_ref, 6)
        for tile in range(9):
            cols = slice(tile * 256, tile * 256 + 256)
            block = dot(a, wq[:, cols])
            if tile < 3:
                block = block.astype(BF16).astype(F32) * HD ** -0.5
            deltas_ref[whole(cell), tile * 256 + 4608:tile * 256 + 4864] = block.astype(BF16)

    def attention(cell):
        valid = lax.broadcasted_iota(jnp.int32, (1, rows_in), 1) < counts_ref[cell]

        def attend(pair, carry):
            start = pair * 128
            queries = stacked(deltas_ref[whole(cell), columns(start + 4608)])
            scores = dot_nt(queries, deltas_ref[whole(cell), columns(start + 5376)])
            scores = jnp.where(valid, scores, -1e30)
            raised = jnp.exp(scores - jnp.max(scores, axis=-1, keepdims=True))
            soft = raised * (1.0 / jnp.sum(raised, axis=-1, keepdims=True))
            soft = soft.astype(BF16)
            probs[cell, pair] = soft
            mixed = dot(soft, deltas_ref[whole(cell), columns(start + 6144)])
            o_ref[:, columns(start)] = unstacked(mixed).astype(BF16)
            return carry

        lax.fori_loop(0, pairs, attend, 0, unroll=True)

    def project_out(cell):
        o = o_ref[...]
        turn(cell, o_ref, 5)
        for tile in range(3):
            cols = slice(tile * 256, tile * 256 + 256)
            mid[:, cols] = source[cell, :, cols].astype(F32) + dot(o, wo[:, cols])

    def norm_mid(cell):
        for part in range(4):
            rows = pl.ds(part * 64, 64)
            b_ref[rows, :] = norm_rows(
                mid[rows, :], gains_ref[1:2, :], cell, rows, normed_2, scale_2
            )

    def go_up(cell):
        turn(cell, b_ref, 4)

        def rise(tile, carry):
            cols = columns(tile * 256, 256)
            u = dot(b_ref[...], wu[:, cols])
            value, steep = gelu_and_slope(u)
            f_ref[:, cols] = value.astype(BF16)
            deltas_ref[whole(cell), columns(tile * 256 + 768, 256)] = steep.astype(BF16)
            return carry

        lax.fori_loop(0, 12, rise, 0, unroll=6)

    def go_down(cell):
        f = f_ref[...]
        turn_wide(cell)
        for tile in range(3):
            cols = slice(tile * 256, tile * 256 + 256)
            result = mid[:, cols] + dot(f, wd[:, cols])
            ends_out[cell, :, cols] = result
            relayed[cell, :, cols] = result.astype(BF16)

    def back_down(cell):
        deltas_ref[whole(cell), 0:768] = upstream[cell]

        def fall(tile, carry):
            start = pl.multiple_of(tile * 256, 256)
            d_active = dot_nt(upstream[cell], wd[pl.ds(start, 256), :])
            d_up = d_active * deltas_ref[whole(cell), columns(start + 768, 256)].astype(F32)
            deltas_ref[whole(cell), columns(start + 768, 256)] = d_up.astype(BF16)
            return carry

        lax.fori_loop(0, 12, fall, 0, unroll=6)

    def back_up(cell):
        d_up = deltas_ref[whole(cell), 768:3840]
        for tile in range(3):
            wide[:, tile * 256:tile * 256 + 256] = dot_nt(
                d_up, wu[tile * 256:tile * 256 + 256, :]
            )

    def norm_mid_back(cell):
        for part in range(4):
            rows = pl.ds(part * 64, 64)
            total = upstream[cell, rows, :].astype(F32) + norm_back(
                wide[rows, :], gains_ref[1:2, :], cell, rows, normed_2, scale_2, 1
            )
            d_mid[rows, :] = total
            deltas_ref[some(cell, part), 3840:4608] = total.astype(BF16)

    def back_out(cell):
        d_branch = deltas_ref[whole(cell), 3840:4608]
        for tile in range(3):
            d_mixed[:, tile * 256:tile * 256 + 256] = dot_nt(
                d_branch, wo[tile * 256:tile * 256 + 256, :]
            ).astype(BF16)

    def attention_back(cell):
        def attend_back(pair, carry):
            start = pair * 128
            queries = stacked(deltas_ref[whole(cell), columns(start + 4608)])
            key_rows = deltas_ref[whole(cell), columns(start + 5376)]
            d_out = stacked(d_mixed[:, columns(start)])
            soft = probs[cell, pair]
            d_values = dot_tn(soft, d_out)
            d_soft = dot_nt(d_out, deltas_ref[whole(cell), columns(start + 6144)])
            soft = soft.astype(F32)
            inner = jnp.sum(soft * d_soft, axis=-1, keepdims=True)
            d_scores = (soft * (d_soft - inner)).astype(BF16)
            d_queries = unstacked(dot(d_scores, key_rows)) * HD ** -0.5
            d_keys = dot_tn(d_scores, queries)
            deltas_ref[whole(cell), columns(start + 4608)] = d_queries.astype(BF16)
            deltas_ref[whole(cell), columns(start + 5376)] = d_keys.astype(BF16)
            deltas_ref[whole(cell), columns(start + 6144)] = d_values.astype(BF16)
            return carry

        lax.fori_loop(0, pairs, attend_back, 0, unroll=True)

    def back_qkv(cell):
        d_qkv = deltas_ref[whole(cell), 4608:6912]
        for tile in range(3):
            wide[:, tile * 256:tile * 256 + 256] = dot_nt(
                d_qkv, wq[tile * 256:tile * 256 + 256, :]
            )

    def norm_source_back(cell):
        for part in range(4):
            rows = pl.ds(part * 64, 64)
            total = d_mid[rows, :] + norm_back(
                wide[rows, :], gains_ref[0:1, :], cell, rows, normed_1, scale_1, 0
            )

            relayed[cell, rows, :] = total.astype(BF16)

            @pl.when(on_first)
            def _():
                ends_out[cell, rows, :] = total

    def weights_here(t, at):
        @pl.when(t == 0)
        def _():
            loads[at].wait()

    def forward(t, cell):
        @pl.when(on_second)
        def _():
            relay_copy(cell, source).wait_recv()

        norm_source(cell)

        @pl.when(t == 0)
        def _():
            loads[0].wait()
            for load in loads[1:]:
                load.start()

        project_qkv(cell)
        attention(cell)
        weights_here(t, 1)
        project_out(cell)
        norm_mid(cell)
        weights_here(t, 2)
        go_up(cell)
        weights_here(t, 3)
        go_down(cell)

        @pl.when(on_second)
        def _():
            ends_copy(cell).start()

        @pl.when(on_first)
        def _():
            @pl.when(t == 0)
            def _():
                pl.semaphore_wait(barrier, len(met))

            relay_copy(cell, source).start()

    def nothing(at):
        del at

    def backward(cell, between=nothing):
        back_down(cell)
        between(0)
        back_up(cell)
        between(1)
        norm_mid_back(cell)
        back_out(cell)
        between(2)
        attention_back(cell)
        between(3)
        back_qkv(cell)
        norm_source_back(cell)

        @pl.when(on_second)
        def _():
            relay_copy(cell, upstream).start()

        @pl.when(on_first)
        def _():
            ends_copy(cell).start()

        between(4)

    def receive_gradient(cell):
        @pl.when(on_first)
        def _():
            relay_copy(cell, source).wait_send()
            relay_copy(cell, upstream).wait_recv()

        deltas_ref[whole(cell), 0:768] = upstream[cell]

    def step(t, carry):
        backwards = (1 - section) * (t // 2) + section * (t % 2)
        cell = (1 - section) * (t % 2) + section * (t // 2)

        @pl.when(backwards == 0)
        def _():
            forward(t, cell)

        @pl.when(backwards == 1)
        def _():
            receive_gradient(cell)
            backward(cell)

        return carry

    lax.fori_loop(0, 3 if scattering else 4, step, 0)

    if scattering:
        def gain_copy(at, device):
            return pltpu.make_async_remote_copy(
                src_ref=gain_held.at[min(at, 2)],
                dst_ref=gain_in.at[at],
                send_sem=gain_send.at[at],
                recv_sem=gain_recv.at[at],
                device_id=device,
                device_id_type=MESH,
            )

        inner = jnp.logical_or(z == 1, z == 2)
        outer = jnp.logical_or(z == 0, z == 3)
        near_device, far_device, mirror_device = z_devices
        leaving = (3 - z) // 3 * 48
        crossing = (2 - z) * 96
        crossing_in = (2 - z) * 48
        own_in = (z // 2) * (1 - z // 3) * 96

        def block(start, count=48):
            return pl.ds(pl.multiple_of(start, 16), count)

        def z_unit(i):
            return i * (EVERY + 1)

        def x_unit(j):
            return j + j // EVERY + 1

        def core_copy(k, room):
            return pltpu.make_async_remote_copy(
                src_ref=core_out.at[room], dst_ref=core_in.at[k],
                send_sem=core_send.at[k], recv_sem=core_recv.at[k],
                device_id=core_device, device_id_type=MESH,
            )

        def x_copy(j):
            return pltpu.make_async_remote_copy(
                src_ref=core_in.at[x_unit(j), block((1 - x) * 192, 192)], dst_ref=x_in.at[j],
                send_sem=x_send.at[j], recv_sem=x_recv.at[j],
                device_id=x_device, device_id_type=MESH,
            )

        def last_copy(i):
            return pltpu.make_async_remote_copy(
                src_ref=core_in.at[z_unit(i), block((1 - x) * 192 + z * 48)], dst_ref=last_in.at[i],
                send_sem=x_send.at[X_FIRST + i], recv_sem=x_recv.at[X_FIRST + i],
                device_id=x_device, device_id_type=MESH,
            )

        def x_line(j):
            return x_in.at[j], 0, j

        def z_lines(i):
            return [(core_in.at[z_unit(i)], side * 192, X_FIRST + 2 * i + side) for side in range(2)]

        def near_copy(line, from_outer):
            ref, base, slot = line
            if from_outer:
                source, target = ref.at[block(base + leaving, 144)], near_in.at[slot]
            else:
                source = ref.at[block(base + far_z[0] * 48)]
                target = near_in.at[slot, pl.ds(0, 48)]
            return pltpu.make_async_remote_copy(
                src_ref=source, dst_ref=target,
                send_sem=near_send.at[slot], recv_sem=near_recv.at[slot],
                device_id=near_device, device_id_type=MESH,
            )

        def far_copy(line, at):
            ref, base, slot = line
            target, device = ((far_z[2], mirror_device), (far_z[1], far_device))[at]
            return pltpu.make_async_remote_copy(
                src_ref=ref.at[block(base + target * 48)], dst_ref=far_in.at[slot],
                send_sem=far_send.at[slot, at], recv_sem=far_recv.at[slot],
                device_id=device, device_id_type=MESH,
            )

        def start_line(line):
            @pl.when(outer)
            def _():
                near_copy(line, True).start()

            @pl.when(inner)
            def _():
                near_copy(line, False).start()

        def pass_line(line):
            @pl.when(inner)
            def _():
                ref, base, slot = line
                near_copy(line, True).wait_recv()
                rows = block(base + crossing, 96)
                total = ref[rows, :].astype(F32) + near_in[slot, block(crossing_in, 96), :].astype(F32)
                ref[rows, :] = total.astype(BF16)
                far_copy(line, 0).start()
                far_copy(line, 1).start()

        def end_line(line):
            ref, base, slot = line

            @pl.when(outer)
            def _():
                near_copy(line, False).wait_recv()

            far_copy(line, 0).wait_recv()
            return (
                ref[block(base + z * 48), :].astype(F32)
                + near_in[slot, block(own_in), :].astype(F32)
                + far_in[slot].astype(F32)
            )

        def wait_line_sends(line):
            @pl.when(outer)
            def _():
                near_copy(line, True).wait_send()

            @pl.when(inner)
            def _():
                near_copy(line, False).wait_send()
                far_copy(line, 0).wait_send()
                far_copy(line, 1).wait_send()

        def form(k, room):
            down = (k < 12).astype(jnp.int32)
            left = down * (k // 3) + (1 - down) * (
                4 + (k >= 24).astype(jnp.int32) + (k >= 27).astype(jnp.int32)
            )
            right = down * (k % 3) + (1 - down) * (k - 9)
            delta = deltas_ref[:, columns(right * 256, 256)]
            away = turned[left, block((1 - core) * 384, 384), :]
            core_out[room] = dot(away, delta).astype(BF16)
            core_copy(k, room).start()
            own = turned[left, block(core * 384, 384), :]
            keep_core[room] = dot(own, delta)

        def form_z(i):
            @pl.when(i >= 1)
            def _():
                core_copy(z_unit(i - 1), HELD).wait_send()

            form(z_unit(i), HELD)

        def form_x(j):
            @pl.when(j >= HELD)
            def _():
                core_copy(x_unit(j - HELD), j % HELD).wait_send()

            form(x_unit(j), j % HELD)

        def over_core(k, room):
            core_copy(k, room).wait_recv()
            core_in[k] = (keep_core[room] + core_in[k].astype(F32)).astype(BF16)

        def over_core_z(i):
            over_core(z_unit(i), HELD)
            for line in z_lines(i):
                start_line(line)

        def over_core_x(j):
            over_core(x_unit(j), j % HELD)
            x_copy(j).start()

        def over_x(j):
            x_copy(j).wait_recv()
            own = core_in[x_unit(j), block(x * 192, 192), :].astype(F32)
            x_in[j] = (own + x_in[j].astype(F32)).astype(BF16)
            start_line(x_line(j))

        def pass_z(i):
            for line in z_lines(i):
                pass_line(line)

        def end_z(i):
            for ref, base, slot in z_lines(i):
                ref[block(base + z * 48), :] = end_line((ref, base, slot)).astype(BF16)
            last_copy(i).start()

        def store(k, total):
            @pl.when(k < 12)
            def _():
                rows = pl.ds(pl.multiple_of((k // 3) * 48, 8), 48)
                gd_out[rows, columns((k % 3) * 256, 256)] = total

            @pl.when(jnp.logical_and(k >= 12, k < 24))
            def _():
                gu_out[:, columns((k - 12) * 256, 256)] = total

            @pl.when(jnp.logical_and(k >= 24, k < 27))
            def _():
                go_out[:, columns((k - 24) * 256, 256)] = total

            @pl.when(k >= 27)
            def _():
                gq_out[:, columns((k - 27) * 256, 256)] = total

        def over_last(i):
            last_copy(i).wait_recv()
            own = core_in[z_unit(i), block(x * 192 + z * 48), :].astype(F32)
            store(z_unit(i), own + last_in[i].astype(F32))

        def end_x(j):
            store(x_unit(j), end_line(x_line(j)))

        def sent_x(j):
            x_copy(j).wait_send()
            wait_line_sends(x_line(j))

        def sent_z(i):
            for line in z_lines(i):
                wait_line_sends(line)
            last_copy(i).wait_send()

        share_copies = [
            pltpu.make_async_copy(vmem, hbm, out_sem.at[at])
            for at, (vmem, hbm) in enumerate(
                ((gd_out, gd_ref), (gu_out, gu_ref), (go_out, go_ref), (gq_out, gq_ref))
            )
        ]

        receive_gradient(1)

        @pl.when(on_first)
        def _():
            def early(t, carry):
                @pl.when(jnp.logical_and(t < EARLY, t % EVERY == 0))
                def _():
                    form_z(t // EVERY)

                @pl.when(t < EARLY)
                def _():
                    form_x(t)

                @pl.when(jnp.logical_and(t >= LAG_CORE, t % EVERY == LAG_CORE))
                def _():
                    over_core_z(t // EVERY)

                @pl.when(t >= LAG_CORE)
                def _():
                    over_core_x(t - LAG_CORE)

                return carry

            lax.fori_loop(0, EARLY + LAG_CORE, early, 0)

        def between(at):
            @pl.when(on_first)
            def _():
                for j in ((0, 1, 2), (3,), (4,), (5,), ())[at]:
                    over_x(j)
                if at == 1:
                    pass_z(0)
                for j in ((), (0,), (1,), (2,), (3,))[at]:
                    pass_line(x_line(j))
                if at == 3:
                    end_z(0)

        backward(1, between)

        gain_held[0] = gain_ref[...]
        gain_copy(0, core_device).start()

        def later(t, carry):
            def at(lag, low, high, work):
                @pl.when(jnp.logical_and(t >= lag + low, t < lag + high))
                def _():
                    work(t - lag)

            def at_z(lag, work):
                @pl.when(jnp.logical_and(
                    (t - lag) % EVERY == 0, jnp.logical_and(t >= lag, t < lag + X_FIRST)
                ))
                def _():
                    work((t - lag) // EVERY)

            at_z(0, form_z)
            at(0, 0, X_FIRST, form_x)

            @pl.when(jnp.logical_or(on_second, t >= EARLY + LAG_CORE))
            def _():
                at_z(LAG_CORE, over_core_z)
                at(LAG_CORE, 0, X_FIRST, over_core_x)

            at(LAG_X, 0, X_FIRST, over_x)
            at_z(LAG_Z_NEAR, pass_z)
            at(LAG_NEAR, 0, X_FIRST, lambda j: pass_line(x_line(j)))
            at_z(LAG_Z_FAR, end_z)
            at_z(LAG_Z_X, over_last)
            at(LAG_FAR, 0, X_FIRST, end_x)
            at(LAG_SENT, 0, X_FIRST, sent_x)
            at_z(LAG_SENT, sent_z)
            for copy, last in zip(share_copies, SHARE_ENDS):
                @pl.when(t == last)
                def _():
                    copy.start()

            @pl.when(t == 16)
            def _():
                gain_copy(0, core_device).wait()
                gain_held[1] = gain_held[0] + gain_in[0]
                gain_copy(1, x_device).start()

            @pl.when(t == 22)
            def _():
                gain_copy(1, x_device).wait()
                gain_held[2] = gain_held[1] + gain_in[1]
                for j in range(3):
                    gain_copy(2 + j, z_devices[j]).start()

            @pl.when(t == 28)
            def _():
                for j in range(3):
                    gain_copy(2 + j, z_devices[j]).wait()
                total_gains = gain_held[2] + gain_in[2] + gain_in[3] + gain_in[4]
                chosen = (
                    lax.broadcasted_iota(jnp.int32, (768, 48), 0)
                    == lax.broadcasted_iota(jnp.int32, (768, 48), 1) + place * 48
                ).astype(F32)
                own_gains = jnp.dot(
                    total_gains, chosen, precision=lax.Precision.HIGHEST, preferred_element_type=F32
                )
                gg_ref[...] = own_gains[:2]

            return carry

        lax.fori_loop((1 - section) * EARLY, X_FIRST + LAG_FAR, later, 0)
        share_copies[3].start()

        core_copy(z_unit(Z_FIRST - 1), HELD).wait_send()
        for j in range(X_FIRST - HELD, X_FIRST):
            core_copy(x_unit(j), j % HELD).wait_send()
        for j in range(X_FIRST + LAG_FAR - LAG_SENT, X_FIRST):
            sent_x(j)
        for i in range((X_FIRST + LAG_FAR - 1 - LAG_SENT) // EVERY + 1, Z_FIRST):
            sent_z(i)
        for copy in share_copies:
            copy.wait()

    for cell in range(2):
        ends_copy(cell).wait()

    @pl.when(on_second)
    def _():
        for cell in range(2):
            relay_copy(cell, upstream).wait_send()


def run_kernel(scattering, acts, counts, cotangent, gains, weights):
    cells, length, width = acts.shape
    vmem = pl.BlockSpec(memory_space=pltpu.VMEM)
    anywhere = pl.BlockSpec(memory_space=pl.ANY)
    dma = pltpu.SemaphoreType.DMA
    held = (
        ((7, 768, cells * length), BF16),
        ((cells * length, 6912), BF16),
        ((8, 768), F32),
    )
    shares = (((48, 2304), F32), ((48, 768), F32), ((48, 3072), F32), ((192, 768), F32), ((2, 48), F32))
    outs = (((cells, length, width), F32),) + (shares if scattering else held)
    first = [pltpu.VMEM(shape, kind) for shape, kind in held + shares[:4]] + [dma((4,))]
    scratch = (
        ((768, 2304), BF16),
        ((768, 768), BF16),
        ((768, 3072), BF16),
        ((3072, 768), BF16),
        ((cells, length, width), BF16),
        ((cells, length, width), BF16),
        ((cells, length, width), BF16),
        ((length, width), BF16),
        ((length, width), BF16),
        ((length, width), BF16),
        ((length, 3072), BF16),
        ((cells, HEADS // 2, 2 * length, length), BF16),
        ((cells, length, width), F32),
        ((cells, length, width), F32),
        ((cells, length, 128), F32),
        ((cells, length, 128), F32),
        ((length, width), F32),
        ((length, width), F32),
        ((cells, length, width), F32),
    )
    semaphores = [dma((4,)), dma(()), dma((2,)), dma((2,)), dma((2,))]
    travel = ()
    if scattering:
        travel = (
            ((HELD + 1, 384, 256), BF16),
            ((HELD + 1, 384, 256), F32),
            ((UNITS, 384, 256), BF16),
            ((X_FIRST, 192, 256), BF16),
            ((Z_FIRST, 48, 256), BF16),
            ((LINES, 144, 256), BF16),
            ((LINES, 48, 256), BF16),
            ((3, 8, 768), F32),
            ((5, 8, 768), F32),
        )
    travel_semaphores = [
        dma((UNITS,)), dma((UNITS,)), dma((UNITS,)), dma((UNITS,)),
        dma((LINES,)), dma((LINES,)), dma((LINES, 2)), dma((LINES,)),
        dma((5,)), dma((5,)),
    ] if scattering else []
    return pl.pallas_call(
        functools.partial(kernel, scattering),
        out_shape=tuple(jax.ShapeDtypeStruct(shape, kind) for shape, kind in outs),
        in_specs=[pl.BlockSpec(memory_space=pltpu.SMEM), vmem] + [anywhere] * 6,
        out_specs=(anywhere,) + ((anywhere,) * 4 + (vmem,) if scattering else (vmem,) * 3),
        scratch_shapes=(first if scattering else [])
        + [pltpu.VMEM(shape, kind) for shape, kind in scratch]
        + semaphores
        + [pltpu.VMEM(shape, kind) for shape, kind in travel]
        + travel_semaphores,
        compiler_params=pltpu.CompilerParams(
            collective_id=1 if scattering else 2,
            has_side_effects=True,
            vmem_limit_bytes=VMEM_BYTES,
        ),
        name="relay_layers",
    )(counts, gains, acts, cotangent, *weights)


def hand_over_kernel(*refs):
    count = (len(refs) - 2) // 3
    sources, targets, rooms = (refs[at * count:(at + 1) * count] for at in range(3))
    read_sem, write_sem = refs[-2:]
    pieces = []
    for source, target, room in zip(sources, targets, rooms):
        if len(source.shape) == 3:
            for cell in range(source.shape[0]):
                pieces.append((source.at[cell], room.at[cell], target.at[cell]))
        else:
            pieces.append((source, room, target))
    reads, writes = [], []
    for at, (source, room, target) in enumerate(pieces):
        reads.append(pltpu.make_async_copy(source, room, read_sem.at[at]))
        writes.append(pltpu.make_async_copy(room, target, write_sem.at[at]))
    for read in reads:
        read.start()
    for read, write in zip(reads, writes):
        read.wait()
        write.start()
    for write in writes:
        write.wait()


def hand_over(*arrays):
    anywhere = pl.BlockSpec(memory_space=pl.ANY)
    sem = pltpu.SemaphoreType.DMA((len(arrays) + 1,))
    return pl.pallas_call(
        hand_over_kernel,
        out_shape=tuple(jax.ShapeDtypeStruct(array.shape, array.dtype) for array in arrays),
        in_specs=[anywhere] * len(arrays),
        out_specs=(anywhere,) * len(arrays),
        scratch_shapes=[pltpu.VMEM(array.shape, array.dtype) for array in arrays] + [sem, sem],
        name="hand_over",
    )(*arrays)


def plain_scattered(turned, deltas, d_gains):
    d_low, d_up = deltas[:, :768], deltas[:, 768:3840]
    d_branch, d_qkv = deltas[:, 3840:4608], deltas[:, 4608:]
    rows = turned.shape[2]
    shares = turned.reshape(7, 2, 2, 4, 48, rows).transpose(3, 2, 1, 0, 4, 5).reshape(16, 7, 48, rows)
    scatter = functools.partial(lax.psum_scatter, axis_name="dp", scatter_dimension=0, tiled=True)
    return (
        lax.psum_scatter(d_gains[:2], "dp", scatter_dimension=1, tiled=True),
        scatter(dot(shares[:, 6].reshape(768, rows), d_qkv)),
        scatter(dot(shares[:, 5].reshape(768, rows), d_branch)),
        scatter(dot(shares[:, 4].reshape(768, rows), d_up)),
        scatter(dot(shares[:, :4].reshape(3072, rows), d_low)),
    )


def body(acts, counts, cotangent, norm_gains, w_qkv, w_out, w_up, w_down):
    weights = (w_qkv[0], w_out[0], w_up[0], w_down[0])
    if lax.axis_size("dp") == 16:
        ends, *shares, d_gains = hand_over(
            *run_kernel(True, acts, counts, cotangent, norm_gains[0], weights)
        )
        shares = [d_gains] + shares
    else:
        ends, *held = run_kernel(False, acts, counts, cotangent, norm_gains[0], weights)
        shares = plain_scattered(*held)
    return (ends[None],) + tuple(share[None] for share in shares)


def solution(mesh):
    placed = (
        P("dp", None, None),
        P("dp"),
        P("dp", None, None),
        P("section", None, None),
        P("section", None, None),
        P("section", None, None),
        P("section", None, None),
        P("section", None, None),
    )
    return jax.shard_map(
        body,
        mesh=mesh,
        in_specs=placed,
        out_specs=(
            P("section", "dp", None, None),
            P("section", None, "dp"),
            P("section", "dp", None),
            P("section", "dp", None),
            P("section", "dp", None),
            P("section", "dp", None),
        ),
        check_vma=False,
    )
```

```python
import functools

import jax
import jax.numpy as jnp
from jax import lax
from jax.experimental import pallas as pl
from jax.experimental.pallas import tpu as pltpu
from jax.sharding import PartitionSpec as P

HEADS = 12
HD = 64
EPSILON = 1e-05
MESH = pl.DeviceIdType.MESH
F32 = jnp.float32
BF16 = jnp.bfloat16

UNITS = 36
Z_FIRST = 6
X_FIRST = UNITS - Z_FIRST
EVERY = 5
EARLY = 10
LAG_CORE = 2
LAG_X = 4
LAG_NEAR = 6
LAG_FAR = 10
LAG_Z_NEAR = 6
LAG_Z_FAR = 9
LAG_Z_X = 12
LAG_SENT = 14
HELD = 3
SHARE_ENDS = (20, 30, 33)
LINES = X_FIRST + 2 * Z_FIRST
VMEM_BYTES = 63 << 20


NT = (((1,), (1,)), ((), ()))
TN = (((0,), (0,)), ((), ()))


def dot(left, right):
    return jnp.dot(left, right, preferred_element_type=F32)


def dot_nt(left, right):
    return lax.dot_general(left, right, NT, preferred_element_type=F32)


def dot_tn(left, right):
    return lax.dot_general(left, right, TN, preferred_element_type=F32)


def gelu_and_slope(u):
    share = 0.5 + 0.5 * lax.erf(u * 0.5 ** 0.5)
    bell = jnp.exp(-0.5 * (u * u))
    return u * share, share + u * (bell * 0.3989422804014327)


def kernel(
    scattering, counts_ref, gains_ref, acts_ref, cotangent_ref, wq_hbm, wo_hbm, wu_hbm, wd_hbm,
    ends_ref, *rest,
):
    if scattering:
        gq_ref, go_ref, gu_ref, gd_ref, gg_ref, turned, deltas_ref, gain_ref = rest[:8]
        gq_out, go_out, gu_out, gd_out, out_sem = rest[8:13]
        (core_out, keep_core, core_in, x_in, last_in, near_in, far_in, gain_held, gain_in,
         core_send, core_recv, x_send, x_recv, near_send, near_recv, far_send, far_recv,
         gain_send, gain_recv) = rest[-19:]
        rest = rest[13:-19]
    else:
        turned, deltas_ref, gain_ref = rest[:3]
        rest = rest[3:]
    (wq, wo, wu, wd, source, upstream, relayed, a_ref, o_ref, b_ref, f_ref, probs,
     normed_1, normed_2, scale_1, scale_2, mid, wide, ends_out,
     weight_sem, input_sem, send_sem, recv_sem, ends_sem) = rest
    d_mid, d_mixed = mid, a_ref

    section = lax.axis_index("section")
    place = lax.axis_index("dp")
    partner = (1 - section, place)
    on_first = section == 0
    on_second = section == 1
    rows_in = source.shape[1]
    pairs = HEADS // 2

    z = place // 4
    x = (place // 2) % 2
    core = place % 2
    far_z = (z + 1 - 2 * (z % 2), (z + 2) % 4, 3 - z)
    core_device = (section, z * 4 + x * 2 + 1 - core)
    x_device = (section, z * 4 + (1 - x) * 2 + core)
    z_devices = [(section, other * 4 + x * 2 + core) for other in far_z]
    met = [partner] + ([core_device, x_device] + z_devices if scattering else [])

    barrier = pltpu.get_barrier_semaphore()
    for device in met:
        pl.semaphore_signal(barrier, inc=1, device_id=device, device_id_type=MESH)

    loads = [
        pltpu.make_async_copy(hbm, vmem, weight_sem.at[at])
        for at, (hbm, vmem) in enumerate(((wq_hbm, wq), (wo_hbm, wo), (wu_hbm, wu), (wd_hbm, wd)))
    ]
    acts_in = pltpu.make_async_copy(acts_ref, source, input_sem)
    cotangent_in = pltpu.make_async_copy(cotangent_ref, upstream, input_sem)

    @pl.when(on_first)
    def _():
        acts_in.start()

    loads[0].start()

    @pl.when(on_second)
    def _():
        cotangent_in.start()

    gain_ref[...] = jnp.zeros_like(gain_ref)

    @pl.when(on_first)
    def _():
        acts_in.wait()

    @pl.when(on_second)
    def _():
        cotangent_in.wait()
        pl.semaphore_wait(barrier, len(met))

    low_lanes = lax.broadcasted_iota(jnp.int32, (rows_in, 128), 1) < HD

    def relay_copy(cell, target):
        return pltpu.make_async_remote_copy(
            src_ref=relayed.at[cell],
            dst_ref=target.at[cell],
            send_sem=send_sem.at[cell],
            recv_sem=recv_sem.at[cell],
            device_id=partner,
            device_id_type=MESH,
        )

    def ends_copy(cell):
        return pltpu.make_async_copy(ends_out.at[cell], ends_ref.at[cell], ends_sem.at[cell])

    def place_of(share):
        return (share % 2) * 384 + ((share // 2) % 2) * 192 + (share // 4) * 48

    def turn(cell, ref, left):
        lanes = pl.ds(pl.multiple_of(cell * rows_in, 256), rows_in)
        for part in range(2):
            block = ref[:, part * 384:part * 384 + 384].T
            for at in range(8):
                start = place_of(part * 8 + at)
                turned[left, start:start + 48, lanes] = block[at * 48:at * 48 + 48]

    def turn_wide(cell):
        lanes = pl.ds(pl.multiple_of(cell * rows_in, 256), rows_in)
        for part in range(8):
            block = f_ref[:, part * 384:part * 384 + 384].T
            for at in range(8):
                start = place_of(part * 2 + at // 4)
                turned[at % 4, start:start + 48, lanes] = block[at * 48:at * 48 + 48]

    def stacked(pair_block):
        none = jnp.zeros_like(pair_block)
        return jnp.concatenate(
            [jnp.where(low_lanes, pair_block, none), jnp.where(low_lanes, none, pair_block)], axis=0
        )

    def unstacked(block):
        return jnp.where(low_lanes, block[:rows_in], block[rows_in:])

    def columns(start, width=128):
        return pl.ds(pl.multiple_of(start, 128), width)

    def norm_rows(values, row_gain, at, rows, normed, scale):
        centred = values - jnp.mean(values, axis=-1, keepdims=True)
        spread = jnp.mean(centred * centred, axis=-1, keepdims=True)
        factor = lax.rsqrt(spread + EPSILON)
        unit = centred * factor
        normed[at, rows, :] = unit
        scale[at, rows, :] = jnp.broadcast_to(factor, (values.shape[0], 128))
        return (unit * row_gain).astype(BF16)

    def norm_back(d_normed, row_gain, at, rows, normed, scale, gain_row):
        unit = normed[at, rows, :]
        product = d_normed * unit
        gain_ref[gain_row:gain_row + 1, :] += jnp.sum(product, axis=0, keepdims=True)
        e = d_normed * row_gain
        mean_e = jnp.mean(e, axis=-1, keepdims=True)
        mean_en = jnp.mean(product * row_gain, axis=-1, keepdims=True)
        return scale[at, rows, :1] * (e - mean_e - unit * mean_en)

    def whole(cell):
        return pl.ds(pl.multiple_of(cell * rows_in, 256), rows_in)

    def some(cell, part):
        return pl.ds(pl.multiple_of(cell * rows_in + part * 64, 64), 64)

    def norm_source(cell):
        for part in range(4):
            a_ref[part * 64:part * 64 + 64, :] = norm_rows(
                source[cell, pl.ds(part * 64, 64), :].astype(F32),
                gains_ref[0:1, :], cell, pl.ds(part * 64, 64), normed_1, scale_1,
            )

    def project_qkv(cell):
        a = a_ref[...]
        turn(cell, a_ref, 6)
        for tile in range(9):
            cols = slice(tile * 256, tile * 256 + 256)
            block = dot(a, wq[:, cols])
            if tile < 3:
                block = block.astype(BF16).astype(F32) * HD ** -0.5
            deltas_ref[whole(cell), tile * 256 + 4608:tile * 256 + 4864] = block.astype(BF16)

    def attention(cell):
        valid = lax.broadcasted_iota(jnp.int32, (1, rows_in), 1) < counts_ref[cell]

        def attend(pair, carry):
            start = pair * 128
            queries = stacked(deltas_ref[whole(cell), columns(start + 4608)])
            scores = dot_nt(queries, deltas_ref[whole(cell), columns(start + 5376)])
            scores = jnp.where(valid, scores, -1e30)
            raised = jnp.exp(scores - jnp.max(scores, axis=-1, keepdims=True))
            soft = raised * (1.0 / jnp.sum(raised, axis=-1, keepdims=True))
            soft = soft.astype(BF16)
            probs[cell, pair] = soft
            mixed = dot(soft, deltas_ref[whole(cell), columns(start + 6144)])
            o_ref[:, columns(start)] = unstacked(mixed).astype(BF16)
            return carry

        lax.fori_loop(0, pairs, attend, 0, unroll=True)

    def project_out(cell):
        o = o_ref[...]
        turn(cell, o_ref, 5)
        for tile in range(3):
            cols = slice(tile * 256, tile * 256 + 256)
            mid[:, cols] = source[cell, :, cols].astype(F32) + dot(o, wo[:, cols])

    def norm_mid(cell):
        for part in range(4):
            rows = pl.ds(part * 64, 64)
            b_ref[rows, :] = norm_rows(
                mid[rows, :], gains_ref[1:2, :], cell, rows, normed_2, scale_2
            )

    def go_up(cell):
        turn(cell, b_ref, 4)

        def rise(tile, carry):
            cols = columns(tile * 256, 256)
            u = dot(b_ref[...], wu[:, cols])
            value, steep = gelu_and_slope(u)
            f_ref[:, cols] = value.astype(BF16)
            deltas_ref[whole(cell), columns(tile * 256 + 768, 256)] = steep.astype(BF16)
            return carry

        lax.fori_loop(0, 12, rise, 0, unroll=6)

    def go_down(cell):
        f = f_ref[...]
        turn_wide(cell)
        for tile in range(3):
            cols = slice(tile * 256, tile * 256 + 256)
            result = mid[:, cols] + dot(f, wd[:, cols])
            ends_out[cell, :, cols] = result
            relayed[cell, :, cols] = result.astype(BF16)

    def back_down(cell):
        deltas_ref[whole(cell), 0:768] = upstream[cell]

        def fall(tile, carry):
            start = pl.multiple_of(tile * 256, 256)
            d_active = dot_nt(upstream[cell], wd[pl.ds(start, 256), :])
            d_up = d_active * deltas_ref[whole(cell), columns(start + 768, 256)].astype(F32)
            deltas_ref[whole(cell), columns(start + 768, 256)] = d_up.astype(BF16)
            return carry

        lax.fori_loop(0, 12, fall, 0, unroll=6)

    def back_up(cell):
        d_up = deltas_ref[whole(cell), 768:3840]
        for tile in range(3):
            wide[:, tile * 256:tile * 256 + 256] = dot_nt(
                d_up, wu[tile * 256:tile * 256 + 256, :]
            )

    def norm_mid_back(cell):
        for part in range(4):
            rows = pl.ds(part * 64, 64)
            total = upstream[cell, rows, :].astype(F32) + norm_back(
                wide[rows, :], gains_ref[1:2, :], cell, rows, normed_2, scale_2, 1
            )
            d_mid[rows, :] = total
            deltas_ref[some(cell, part), 3840:4608] = total.astype(BF16)

    def back_out(cell):
        d_branch = deltas_ref[whole(cell), 3840:4608]
        for tile in range(3):
            d_mixed[:, tile * 256:tile * 256 + 256] = dot_nt(
                d_branch, wo[tile * 256:tile * 256 + 256, :]
            ).astype(BF16)

    def attention_back(cell):
        def attend_back(pair, carry):
            start = pair * 128
            queries = stacked(deltas_ref[whole(cell), columns(start + 4608)])
            key_rows = deltas_ref[whole(cell), columns(start + 5376)]
            d_out = stacked(d_mixed[:, columns(start)])
            soft = probs[cell, pair]
            d_values = dot_tn(soft, d_out)
            d_soft = dot_nt(d_out, deltas_ref[whole(cell), columns(start + 6144)])
            soft = soft.astype(F32)
            inner = jnp.sum(soft * d_soft, axis=-1, keepdims=True)
            d_scores = (soft * (d_soft - inner)).astype(BF16)
            d_queries = unstacked(dot(d_scores, key_rows)) * HD ** -0.5
            d_keys = dot_tn(d_scores, queries)
            deltas_ref[whole(cell), columns(start + 4608)] = d_queries.astype(BF16)
            deltas_ref[whole(cell), columns(start + 5376)] = d_keys.astype(BF16)
            deltas_ref[whole(cell), columns(start + 6144)] = d_values.astype(BF16)
            return carry

        lax.fori_loop(0, pairs, attend_back, 0, unroll=True)

    def back_qkv(cell):
        d_qkv = deltas_ref[whole(cell), 4608:6912]
        for tile in range(3):
            wide[:, tile * 256:tile * 256 + 256] = dot_nt(
                d_qkv, wq[tile * 256:tile * 256 + 256, :]
            )

    def norm_source_back(cell):
        for part in range(4):
            rows = pl.ds(part * 64, 64)
            total = d_mid[rows, :] + norm_back(
                wide[rows, :], gains_ref[0:1, :], cell, rows, normed_1, scale_1, 0
            )

            relayed[cell, rows, :] = total.astype(BF16)

            @pl.when(on_first)
            def _():
                ends_out[cell, rows, :] = total

    def weights_here(t, at):
        @pl.when(t == 0)
        def _():
            loads[at].wait()

    def forward(t, cell):
        @pl.when(on_second)
        def _():
            relay_copy(cell, source).wait_recv()

        norm_source(cell)

        @pl.when(t == 0)
        def _():
            loads[0].wait()
            for load in loads[1:]:
                load.start()

        project_qkv(cell)
        attention(cell)
        weights_here(t, 1)
        project_out(cell)
        norm_mid(cell)
        weights_here(t, 2)
        go_up(cell)
        weights_here(t, 3)
        go_down(cell)

        @pl.when(on_second)
        def _():
            ends_copy(cell).start()

        @pl.when(on_first)
        def _():
            @pl.when(t == 0)
            def _():
                pl.semaphore_wait(barrier, len(met))

            relay_copy(cell, source).start()

    def nothing(at):
        del at

    def backward(cell, between=nothing):
        back_down(cell)
        between(0)
        back_up(cell)
        between(1)
        norm_mid_back(cell)
        back_out(cell)
        between(2)
        attention_back(cell)
        between(3)
        back_qkv(cell)
        norm_source_back(cell)

        @pl.when(on_second)
        def _():
            relay_copy(cell, upstream).start()

        @pl.when(on_first)
        def _():
            ends_copy(cell).start()

        between(4)

    def receive_gradient(cell):
        @pl.when(on_first)
        def _():
            relay_copy(cell, source).wait_send()
            relay_copy(cell, upstream).wait_recv()

        deltas_ref[whole(cell), 0:768] = upstream[cell]

    def step(t, carry):
        backwards = (1 - section) * (t // 2) + section * (t % 2)
        cell = (1 - section) * (t % 2) + section * (t // 2)

        @pl.when(backwards == 0)
        def _():
            forward(t, cell)

        @pl.when(backwards == 1)
        def _():
            receive_gradient(cell)
            backward(cell)

        return carry

    lax.fori_loop(0, 3 if scattering else 4, step, 0)

    if scattering:
        def gain_copy(at, device):
            return pltpu.make_async_remote_copy(
                src_ref=gain_held.at[min(at, 2)],
                dst_ref=gain_in.at[at],
                send_sem=gain_send.at[at],
                recv_sem=gain_recv.at[at],
                device_id=device,
                device_id_type=MESH,
            )

        inner = jnp.logical_or(z == 1, z == 2)
        outer = jnp.logical_or(z == 0, z == 3)
        near_device, far_device, mirror_device = z_devices
        leaving = (3 - z) // 3 * 48
        crossing = (2 - z) * 96
        crossing_in = (2 - z) * 48
        own_in = (z // 2) * (1 - z // 3) * 96

        def block(start, count=48):
            return pl.ds(pl.multiple_of(start, 16), count)

        def z_unit(i):
            return i * (EVERY + 1)

        def x_unit(j):
            return j + j // EVERY + 1

        def core_copy(k, room):
            return pltpu.make_async_remote_copy(
                src_ref=core_out.at[room], dst_ref=core_in.at[k],
                send_sem=core_send.at[k], recv_sem=core_recv.at[k],
                device_id=core_device, device_id_type=MESH,
            )

        def x_copy(j):
            return pltpu.make_async_remote_copy(
                src_ref=core_in.at[x_unit(j), block((1 - x) * 192, 192)], dst_ref=x_in.at[j],
                send_sem=x_send.at[j], recv_sem=x_recv.at[j],
                device_id=x_device, device_id_type=MESH,
            )

        def last_copy(i):
            return pltpu.make_async_remote_copy(
                src_ref=core_in.at[z_unit(i), block((1 - x) * 192 + z * 48)], dst_ref=last_in.at[i],
                send_sem=x_send.at[X_FIRST + i], recv_sem=x_recv.at[X_FIRST + i],
                device_id=x_device, device_id_type=MESH,
            )

        def x_line(j):
            return x_in.at[j], 0, j

        def z_lines(i):
            return [(core_in.at[z_unit(i)], side * 192, X_FIRST + 2 * i + side) for side in range(2)]

        def near_copy(line, from_outer):
            ref, base, slot = line
            if from_outer:
                source, target = ref.at[block(base + leaving, 144)], near_in.at[slot]
            else:
                source = ref.at[block(base + far_z[0] * 48)]
                target = near_in.at[slot, pl.ds(0, 48)]
            return pltpu.make_async_remote_copy(
                src_ref=source, dst_ref=target,
                send_sem=near_send.at[slot], recv_sem=near_recv.at[slot],
                device_id=near_device, device_id_type=MESH,
            )

        def far_copy(line, at):
            ref, base, slot = line
            target, device = ((far_z[2], mirror_device), (far_z[1], far_device))[at]
            return pltpu.make_async_remote_copy(
                src_ref=ref.at[block(base + target * 48)], dst_ref=far_in.at[slot],
                send_sem=far_send.at[slot, at], recv_sem=far_recv.at[slot],
                device_id=device, device_id_type=MESH,
            )

        def start_line(line):
            @pl.when(outer)
            def _():
                near_copy(line, True).start()

            @pl.when(inner)
            def _():
                near_copy(line, False).start()

        def pass_line(line):
            @pl.when(inner)
            def _():
                ref, base, slot = line
                near_copy(line, True).wait_recv()
                rows = block(base + crossing, 96)
                total = ref[rows, :].astype(F32) + near_in[slot, block(crossing_in, 96), :].astype(F32)
                ref[rows, :] = total.astype(BF16)
                far_copy(line, 0).start()
                far_copy(line, 1).start()

        def end_line(line):
            ref, base, slot = line

            @pl.when(outer)
            def _():
                near_copy(line, False).wait_recv()

            far_copy(line, 0).wait_recv()
            return (
                ref[block(base + z * 48), :].astype(F32)
                + near_in[slot, block(own_in), :].astype(F32)
                + far_in[slot].astype(F32)
            )

        def wait_line_sends(line):
            @pl.when(outer)
            def _():
                near_copy(line, True).wait_send()

            @pl.when(inner)
            def _():
                near_copy(line, False).wait_send()
                far_copy(line, 0).wait_send()
                far_copy(line, 1).wait_send()

        def form(k, room):
            down = (k < 12).astype(jnp.int32)
            left = down * (k // 3) + (1 - down) * (
                4 + (k >= 24).astype(jnp.int32) + (k >= 27).astype(jnp.int32)
            )
            right = down * (k % 3) + (1 - down) * (k - 9)
            delta = deltas_ref[:, columns(right * 256, 256)]
            away = turned[left, block((1 - core) * 384, 384), :]
            core_out[room] = dot(away, delta).astype(BF16)
            core_copy(k, room).start()
            own = turned[left, block(core * 384, 384), :]
            keep_core[room] = dot(own, delta)

        def form_z(i):
            @pl.when(i >= 1)
            def _():
                core_copy(z_unit(i - 1), HELD).wait_send()

            form(z_unit(i), HELD)

        def form_x(j):
            @pl.when(j >= HELD)
            def _():
                core_copy(x_unit(j - HELD), j % HELD).wait_send()

            form(x_unit(j), j % HELD)

        def over_core(k, room):
            core_copy(k, room).wait_recv()
            core_in[k] = (keep_core[room] + core_in[k].astype(F32)).astype(BF16)

        def over_core_z(i):
            over_core(z_unit(i), HELD)
            for line in z_lines(i):
                start_line(line)

        def over_core_x(j):
            over_core(x_unit(j), j % HELD)
            x_copy(j).start()

        def over_x(j):
            x_copy(j).wait_recv()
            own = core_in[x_unit(j), block(x * 192, 192), :].astype(F32)
            x_in[j] = (own + x_in[j].astype(F32)).astype(BF16)
            start_line(x_line(j))

        def pass_z(i):
            for line in z_lines(i):
                pass_line(line)

        def end_z(i):
            for ref, base, slot in z_lines(i):
                ref[block(base + z * 48), :] = end_line((ref, base, slot)).astype(BF16)
            last_copy(i).start()

        def store(k, total):
            @pl.when(k < 12)
            def _():
                rows = pl.ds(pl.multiple_of((k // 3) * 48, 8), 48)
                gd_out[rows, columns((k % 3) * 256, 256)] = total

            @pl.when(jnp.logical_and(k >= 12, k < 24))
            def _():
                gu_out[:, columns((k - 12) * 256, 256)] = total

            @pl.when(jnp.logical_and(k >= 24, k < 27))
            def _():
                go_out[:, columns((k - 24) * 256, 256)] = total

            @pl.when(k >= 27)
            def _():
                gq_out[:, columns((k - 27) * 256, 256)] = total

        def over_last(i):
            last_copy(i).wait_recv()
            own = core_in[z_unit(i), block(x * 192 + z * 48), :].astype(F32)
            store(z_unit(i), own + last_in[i].astype(F32))

        def end_x(j):
            store(x_unit(j), end_line(x_line(j)))

        def sent_x(j):
            x_copy(j).wait_send()
            wait_line_sends(x_line(j))

        def sent_z(i):
            for line in z_lines(i):
                wait_line_sends(line)
            last_copy(i).wait_send()

        share_copies = [
            pltpu.make_async_copy(vmem, hbm, out_sem.at[at])
            for at, (vmem, hbm) in enumerate(
                ((gd_out, gd_ref), (gu_out, gu_ref), (go_out, go_ref), (gq_out, gq_ref))
            )
        ]

        receive_gradient(1)

        @pl.when(on_first)
        def _():
            def early(t, carry):
                @pl.when(jnp.logical_and(t < EARLY, t % EVERY == 0))
                def _():
                    form_z(t // EVERY)

                @pl.when(t < EARLY)
                def _():
                    form_x(t)

                @pl.when(jnp.logical_and(t >= LAG_CORE, t % EVERY == LAG_CORE))
                def _():
                    over_core_z(t // EVERY)

                @pl.when(t >= LAG_CORE)
                def _():
                    over_core_x(t - LAG_CORE)

                return carry

            lax.fori_loop(0, EARLY + LAG_CORE, early, 0)

        def between(at):
            @pl.when(on_first)
            def _():
                for j in ((0, 1, 2), (3,), (4,), (5,), ())[at]:
                    over_x(j)
                if at == 1:
                    pass_z(0)
                for j in ((), (0,), (1,), (2,), (3,))[at]:
                    pass_line(x_line(j))
                if at == 3:
                    end_z(0)

        backward(1, between)

        gain_held[0] = gain_ref[...]
        gain_copy(0, core_device).start()

        def later(t, carry):
            def at(lag, low, high, work):
                @pl.when(jnp.logical_and(t >= lag + low, t < lag + high))
                def _():
                    work(t - lag)

            def at_z(lag, work):
                @pl.when(jnp.logical_and(
                    (t - lag) % EVERY == 0, jnp.logical_and(t >= lag, t < lag + X_FIRST)
                ))
                def _():
                    work((t - lag) // EVERY)

            at_z(0, form_z)
            at(0, 0, X_FIRST, form_x)

            @pl.when(jnp.logical_or(on_second, t >= EARLY + LAG_CORE))
            def _():
                at_z(LAG_CORE, over_core_z)
                at(LAG_CORE, 0, X_FIRST, over_core_x)

            at(LAG_X, 0, X_FIRST, over_x)
            at_z(LAG_Z_NEAR, pass_z)
            at(LAG_NEAR, 0, X_FIRST, lambda j: pass_line(x_line(j)))
            at_z(LAG_Z_FAR, end_z)
            at_z(LAG_Z_X, over_last)
            at(LAG_FAR, 0, X_FIRST, end_x)
            at(LAG_SENT, 0, X_FIRST, sent_x)
            at_z(LAG_SENT, sent_z)
            for copy, last in zip(share_copies, SHARE_ENDS):
                @pl.when(t == last)
                def _():
                    copy.start()

            @pl.when(t == 16)
            def _():
                gain_copy(0, core_device).wait()
                gain_held[1] = gain_held[0] + gain_in[0]
                gain_copy(1, x_device).start()

            @pl.when(t == 22)
            def _():
                gain_copy(1, x_device).wait()
                gain_held[2] = gain_held[1] + gain_in[1]
                for j in range(3):
                    gain_copy(2 + j, z_devices[j]).start()

            @pl.when(t == 28)
            def _():
                for j in range(3):
                    gain_copy(2 + j, z_devices[j]).wait()
                total_gains = gain_held[2] + gain_in[2] + gain_in[3] + gain_in[4]
                chosen = (
                    lax.broadcasted_iota(jnp.int32, (768, 48), 0)
                    == lax.broadcasted_iota(jnp.int32, (768, 48), 1) + place * 48
                ).astype(F32)
                own_gains = jnp.dot(
                    total_gains, chosen, precision=lax.Precision.HIGHEST, preferred_element_type=F32
                )
                gg_ref[...] = own_gains[:2]

            return carry

        lax.fori_loop((1 - section) * EARLY, X_FIRST + LAG_FAR, later, 0)
        share_copies[3].start()

        core_copy(z_unit(Z_FIRST - 1), HELD).wait_send()
        for j in range(X_FIRST - HELD, X_FIRST):
            core_copy(x_unit(j), j % HELD).wait_send()
        for j in range(X_FIRST + LAG_FAR - LAG_SENT, X_FIRST):
            sent_x(j)
        for i in range((X_FIRST + LAG_FAR - 1 - LAG_SENT) // EVERY + 1, Z_FIRST):
            sent_z(i)
        for copy in share_copies:
            copy.wait()

    for cell in range(2):
        ends_copy(cell).wait()

    @pl.when(on_second)
    def _():
        for cell in range(2):
            relay_copy(cell, upstream).wait_send()


def run_kernel(scattering, acts, counts, cotangent, gains, weights):
    cells, length, width = acts.shape
    vmem = pl.BlockSpec(memory_space=pltpu.VMEM)
    anywhere = pl.BlockSpec(memory_space=pl.ANY)
    dma = pltpu.SemaphoreType.DMA
    held = (
        ((7, 768, cells * length), BF16),
        ((cells * length, 6912), BF16),
        ((8, 768), F32),
    )
    shares = (((48, 2304), F32), ((48, 768), F32), ((48, 3072), F32), ((192, 768), F32), ((2, 48), F32))
    outs = (((cells, length, width), F32),) + (shares if scattering else held)
    first = [pltpu.VMEM(shape, kind) for shape, kind in held + shares[:4]] + [dma((4,))]
    scratch = (
        ((768, 2304), BF16),
        ((768, 768), BF16),
        ((768, 3072), BF16),
        ((3072, 768), BF16),
        ((cells, length, width), BF16),
        ((cells, length, width), BF16),
        ((cells, length, width), BF16),
        ((length, width), BF16),
        ((length, width), BF16),
        ((length, width), BF16),
        ((length, 3072), BF16),
        ((cells, HEADS // 2, 2 * length, length), BF16),
        ((cells, length, width), F32),
        ((cells, length, width), F32),
        ((cells, length, 128), F32),
        ((cells, length, 128), F32),
        ((length, width), F32),
        ((length, width), F32),
        ((cells, length, width), F32),
    )
    semaphores = [dma((4,)), dma(()), dma((2,)), dma((2,)), dma((2,))]
    travel = ()
    if scattering:
        travel = (
            ((HELD + 1, 384, 256), BF16),
            ((HELD + 1, 384, 256), F32),
            ((UNITS, 384, 256), BF16),
            ((X_FIRST, 192, 256), BF16),
            ((Z_FIRST, 48, 256), BF16),
            ((LINES, 144, 256), BF16),
            ((LINES, 48, 256), BF16),
            ((3, 8, 768), F32),
            ((5, 8, 768), F32),
        )
    travel_semaphores = [
        dma((UNITS,)), dma((UNITS,)), dma((UNITS,)), dma((UNITS,)),
        dma((LINES,)), dma((LINES,)), dma((LINES, 2)), dma((LINES,)),
        dma((5,)), dma((5,)),
    ] if scattering else []
    return pl.pallas_call(
        functools.partial(kernel, scattering),
        out_shape=tuple(jax.ShapeDtypeStruct(shape, kind) for shape, kind in outs),
        in_specs=[pl.BlockSpec(memory_space=pltpu.SMEM), vmem] + [anywhere] * 6,
        out_specs=(anywhere,) + ((anywhere,) * 4 + (vmem,) if scattering else (vmem,) * 3),
        scratch_shapes=(first if scattering else [])
        + [pltpu.VMEM(shape, kind) for shape, kind in scratch]
        + semaphores
        + [pltpu.VMEM(shape, kind) for shape, kind in travel]
        + travel_semaphores,
        compiler_params=pltpu.CompilerParams(
            collective_id=1 if scattering else 2,
            has_side_effects=True,
            vmem_limit_bytes=VMEM_BYTES,
        ),
        name="relay_layers",
    )(counts, gains, acts, cotangent, *weights)


def hand_over_kernel(*refs):
    count = (len(refs) - 2) // 3
    sources, targets, rooms = (refs[at * count:(at + 1) * count] for at in range(3))
    read_sem, write_sem = refs[-2:]
    pieces = []
    for source, target, room in zip(sources, targets, rooms):
        if len(source.shape) == 3:
            half = source.shape[1] // 2
            for cell in range(source.shape[0]):
                for side in range(2):
                    rows = pl.ds(side * half, half)
                    pieces.append(tuple(ref.at[cell, rows] for ref in (source, room, target)))
        else:
            pieces.append((source, room, target))
    reads, writes = [], []
    for at, (source, room, target) in enumerate(pieces):
        reads.append(pltpu.make_async_copy(source, room, read_sem.at[at]))
        writes.append(pltpu.make_async_copy(room, target, write_sem.at[at]))
    for read in reads:
        read.start()
    for read, write in zip(reads, writes):
        read.wait()
        write.start()
    for write in writes:
        write.wait()


def hand_over(*arrays):
    anywhere = pl.BlockSpec(memory_space=pl.ANY)
    sem = pltpu.SemaphoreType.DMA((len(arrays) + 3,))
    return pl.pallas_call(
        hand_over_kernel,
        out_shape=tuple(jax.ShapeDtypeStruct(array.shape, array.dtype) for array in arrays),
        in_specs=[anywhere] * len(arrays),
        out_specs=(anywhere,) * len(arrays),
        scratch_shapes=[pltpu.VMEM(array.shape, array.dtype) for array in arrays] + [sem, sem],
        name="hand_over",
    )(*arrays)


def plain_scattered(turned, deltas, d_gains):
    d_low, d_up = deltas[:, :768], deltas[:, 768:3840]
    d_branch, d_qkv = deltas[:, 3840:4608], deltas[:, 4608:]
    rows = turned.shape[2]
    shares = turned.reshape(7, 2, 2, 4, 48, rows).transpose(3, 2, 1, 0, 4, 5).reshape(16, 7, 48, rows)
    scatter = functools.partial(lax.psum_scatter, axis_name="dp", scatter_dimension=0, tiled=True)
    return (
        lax.psum_scatter(d_gains[:2], "dp", scatter_dimension=1, tiled=True),
        scatter(dot(shares[:, 6].reshape(768, rows), d_qkv)),
        scatter(dot(shares[:, 5].reshape(768, rows), d_branch)),
        scatter(dot(shares[:, 4].reshape(768, rows), d_up)),
        scatter(dot(shares[:, :4].reshape(3072, rows), d_low)),
    )


def body(acts, counts, cotangent, norm_gains, w_qkv, w_out, w_up, w_down):
    weights = (w_qkv[0], w_out[0], w_up[0], w_down[0])
    if lax.axis_size("dp") == 16:
        ends, *shares, d_gains = hand_over(
            *run_kernel(True, acts, counts, cotangent, norm_gains[0], weights)
        )
        shares = [d_gains] + shares
    else:
        ends, *held = run_kernel(False, acts, counts, cotangent, norm_gains[0], weights)
        shares = plain_scattered(*held)
    return (ends[None],) + tuple(share[None] for share in shares)


def solution(mesh):
    placed = (
        P("dp", None, None),
        P("dp"),
        P("dp", None, None),
        P("section", None, None),
        P("section", None, None),
        P("section", None, None),
        P("section", None, None),
        P("section", None, None),
    )
    return jax.shard_map(
        body,
        mesh=mesh,
        in_specs=placed,
        out_specs=(
            P("section", "dp", None, None),
            P("section", None, "dp"),
            P("section", "dp", None),
            P("section", "dp", None),
            P("section", "dp", None),
            P("section", "dp", None),
        ),
        check_vma=False,
    )
```

```python
import functools

import jax
import jax.numpy as jnp
from jax import lax
from jax.experimental import pallas as pl
from jax.experimental.pallas import tpu as pltpu
from jax.sharding import PartitionSpec as P

HEADS = 12
HD = 64
EPSILON = 1e-05
MESH = pl.DeviceIdType.MESH
F32 = jnp.float32
BF16 = jnp.bfloat16

UNITS = 36
Z_FIRST = 6
X_FIRST = UNITS - Z_FIRST
EVERY = 5
EARLY = 10
LAG_CORE = 2
LAG_X = 4
LAG_NEAR = 6
LAG_FAR = 10
LAG_Z_NEAR = 6
LAG_Z_FAR = 9
LAG_Z_X = 12
LAG_SENT = 14
HELD = 3
SHARE_ENDS = (20, 30, 33)
LINES = X_FIRST + 2 * Z_FIRST
VMEM_BYTES = 63 << 20


NT = (((1,), (1,)), ((), ()))
TN = (((0,), (0,)), ((), ()))


def dot(left, right):
    return jnp.dot(left, right, preferred_element_type=F32)


def dot_nt(left, right):
    return lax.dot_general(left, right, NT, preferred_element_type=F32)


def dot_tn(left, right):
    return lax.dot_general(left, right, TN, preferred_element_type=F32)


def gelu_and_slope(u):
    share = 0.5 + 0.5 * lax.erf(u * 0.5 ** 0.5)
    bell = jnp.exp(-0.5 * (u * u))
    return u * share, share + u * (bell * 0.3989422804014327)


def kernel(
    scattering, counts_ref, gains_ref, acts_ref, cotangent_ref, wq_hbm, wo_hbm, wu_hbm, wd_hbm,
    ends_ref, *rest,
):
    if scattering:
        gq_ref, go_ref, gu_ref, gd_ref, gg_ref, turned, deltas_ref, gain_ref = rest[:8]
        gq_out, go_out, gu_out, gd_out, out_sem = rest[8:13]
        (core_out, keep_core, core_in, x_in, last_in, near_in, far_in, gain_held, gain_in,
         core_send, core_recv, x_send, x_recv, near_send, near_recv, far_send, far_recv,
         gain_send, gain_recv) = rest[-19:]
        rest = rest[13:-19]
    else:
        turned, deltas_ref, gain_ref = rest[:3]
        rest = rest[3:]
    (wq, wo, wu, wd, source, upstream, relayed, a_ref, o_ref, b_ref, f_ref, probs,
     normed_1, normed_2, scale_1, scale_2, mid, wide, ends_out,
     weight_sem, input_sem, send_sem, recv_sem, ends_sem) = rest
    d_mid, d_mixed = mid, a_ref

    section = lax.axis_index("section")
    place = lax.axis_index("dp")
    partner = (1 - section, place)
    on_first = section == 0
    on_second = section == 1
    rows_in = source.shape[1]
    pairs = HEADS // 2

    z = place // 4
    x = (place // 2) % 2
    core = place % 2
    far_z = (z + 1 - 2 * (z % 2), (z + 2) % 4, 3 - z)
    core_device = (section, z * 4 + x * 2 + 1 - core)
    x_device = (section, z * 4 + (1 - x) * 2 + core)
    z_devices = [(section, other * 4 + x * 2 + core) for other in far_z]
    met = [partner] + ([core_device, x_device] + z_devices if scattering else [])

    barrier = pltpu.get_barrier_semaphore()
    for device in met:
        pl.semaphore_signal(barrier, inc=1, device_id=device, device_id_type=MESH)

    loads = [
        pltpu.make_async_copy(hbm, vmem, weight_sem.at[at])
        for at, (hbm, vmem) in enumerate(((wq_hbm, wq), (wo_hbm, wo), (wu_hbm, wu), (wd_hbm, wd)))
    ]
    acts_in = pltpu.make_async_copy(acts_ref, source, input_sem)
    cotangent_in = pltpu.make_async_copy(cotangent_ref, upstream, input_sem)

    @pl.when(on_first)
    def _():
        acts_in.start()

    loads[0].start()

    @pl.when(on_second)
    def _():
        cotangent_in.start()

    gain_ref[...] = jnp.zeros_like(gain_ref)

    @pl.when(on_first)
    def _():
        acts_in.wait()

    @pl.when(on_second)
    def _():
        cotangent_in.wait()
        pl.semaphore_wait(barrier, len(met))

    low_lanes = lax.broadcasted_iota(jnp.int32, (rows_in, 128), 1) < HD

    def relay_copy(cell, target):
        return pltpu.make_async_remote_copy(
            src_ref=relayed.at[cell],
            dst_ref=target.at[cell],
            send_sem=send_sem.at[cell],
            recv_sem=recv_sem.at[cell],
            device_id=partner,
            device_id_type=MESH,
        )

    def ends_copy(cell):
        return pltpu.make_async_copy(ends_out.at[cell], ends_ref.at[cell], ends_sem.at[cell])

    def place_of(share):
        return (share % 2) * 384 + ((share // 2) % 2) * 192 + (share // 4) * 48

    def turn(cell, ref, left):
        lanes = pl.ds(pl.multiple_of(cell * rows_in, 256), rows_in)
        for part in range(2):
            block = ref[:, part * 384:part * 384 + 384].T
            for at in range(8):
                start = place_of(part * 8 + at)
                turned[left, start:start + 48, lanes] = block[at * 48:at * 48 + 48]

    def turn_wide(cell):
        lanes = pl.ds(pl.multiple_of(cell * rows_in, 256), rows_in)
        for part in range(8):
            block = f_ref[:, part * 384:part * 384 + 384].T
            for at in range(8):
                start = place_of(part * 2 + at // 4)
                turned[at % 4, start:start + 48, lanes] = block[at * 48:at * 48 + 48]

    def stacked(pair_block):
        none = jnp.zeros_like(pair_block)
        return jnp.concatenate(
            [jnp.where(low_lanes, pair_block, none), jnp.where(low_lanes, none, pair_block)], axis=0
        )

    def unstacked(block):
        return jnp.where(low_lanes, block[:rows_in], block[rows_in:])

    def columns(start, width=128):
        return pl.ds(pl.multiple_of(start, 128), width)

    def norm_rows(values, row_gain, at, rows, normed, scale):
        centred = values - jnp.mean(values, axis=-1, keepdims=True)
        spread = jnp.mean(centred * centred, axis=-1, keepdims=True)
        factor = lax.rsqrt(spread + EPSILON)
        unit = centred * factor
        normed[at, rows, :] = unit
        scale[at, rows, :] = jnp.broadcast_to(factor, (values.shape[0], 128))
        return (unit * row_gain).astype(BF16)

    def norm_back(d_normed, row_gain, at, rows, normed, scale, gain_row):
        unit = normed[at, rows, :]
        product = d_normed * unit
        gain_ref[gain_row:gain_row + 1, :] += jnp.sum(product, axis=0, keepdims=True)
        e = d_normed * row_gain
        mean_e = jnp.mean(e, axis=-1, keepdims=True)
        mean_en = jnp.mean(product * row_gain, axis=-1, keepdims=True)
        return scale[at, rows, :1] * (e - mean_e - unit * mean_en)

    def whole(cell):
        return pl.ds(pl.multiple_of(cell * rows_in, 256), rows_in)

    def some(cell, part):
        return pl.ds(pl.multiple_of(cell * rows_in + part * 64, 64), 64)

    def norm_source(cell):
        for part in range(4):
            a_ref[part * 64:part * 64 + 64, :] = norm_rows(
                source[cell, pl.ds(part * 64, 64), :].astype(F32),
                gains_ref[0:1, :], cell, pl.ds(part * 64, 64), normed_1, scale_1,
            )

    def project_qkv(cell):
        a = a_ref[...]
        turn(cell, a_ref, 6)
        for tile in range(9):
            cols = slice(tile * 256, tile * 256 + 256)
            block = dot(a, wq[:, cols])
            if tile < 3:
                block = block.astype(BF16).astype(F32) * HD ** -0.5
            deltas_ref[whole(cell), tile * 256 + 4608:tile * 256 + 4864] = block.astype(BF16)

    def attention(cell):
        valid = lax.broadcasted_iota(jnp.int32, (1, rows_in), 1) < counts_ref[cell]

        def attend(pair, carry):
            start = pair * 128
            queries = stacked(deltas_ref[whole(cell), columns(start + 4608)])
            scores = dot_nt(queries, deltas_ref[whole(cell), columns(start + 5376)])
            scores = jnp.where(valid, scores, -1e30)
            raised = jnp.exp(scores - jnp.max(scores, axis=-1, keepdims=True))
            soft = raised * (1.0 / jnp.sum(raised, axis=-1, keepdims=True))
            soft = soft.astype(BF16)
            probs[cell, pair] = soft
            mixed = dot(soft, deltas_ref[whole(cell), columns(start + 6144)])
            o_ref[:, columns(start)] = unstacked(mixed).astype(BF16)
            return carry

        lax.fori_loop(0, pairs, attend, 0, unroll=True)

    def project_out(cell):
        o = o_ref[...]
        turn(cell, o_ref, 5)
        for tile in range(3):
            cols = slice(tile * 256, tile * 256 + 256)
            mid[:, cols] = source[cell, :, cols].astype(F32) + dot(o, wo[:, cols])

    def norm_mid(cell):
        for part in range(4):
            rows = pl.ds(part * 64, 64)
            b_ref[rows, :] = norm_rows(
                mid[rows, :], gains_ref[1:2, :], cell, rows, normed_2, scale_2
            )

    def go_up(cell):
        turn(cell, b_ref, 4)

        def rise(tile, carry):
            cols = columns(tile * 256, 256)
            u = dot(b_ref[...], wu[:, cols])
            value, steep = gelu_and_slope(u)
            f_ref[:, cols] = value.astype(BF16)
            deltas_ref[whole(cell), columns(tile * 256 + 768, 256)] = steep.astype(BF16)
            return carry

        lax.fori_loop(0, 12, rise, 0, unroll=6)

    def go_down(cell):
        f = f_ref[...]
        turn_wide(cell)
        for tile in range(3):
            cols = slice(tile * 256, tile * 256 + 256)
            result = mid[:, cols] + dot(f, wd[:, cols])
            ends_out[cell, :, cols] = result
            relayed[cell, :, cols] = result.astype(BF16)

    def back_down(cell):
        deltas_ref[whole(cell), 0:768] = upstream[cell]

        def fall(tile, carry):
            start = pl.multiple_of(tile * 256, 256)
            d_active = dot_nt(upstream[cell], wd[pl.ds(start, 256), :])
            d_up = d_active * deltas_ref[whole(cell), columns(start + 768, 256)].astype(F32)
            deltas_ref[whole(cell), columns(start + 768, 256)] = d_up.astype(BF16)
            return carry

        lax.fori_loop(0, 12, fall, 0, unroll=6)

    def back_up(cell):
        d_up = deltas_ref[whole(cell), 768:3840]
        for tile in range(3):
            wide[:, tile * 256:tile * 256 + 256] = dot_nt(
                d_up, wu[tile * 256:tile * 256 + 256, :]
            )

    def norm_mid_back(cell):
        for part in range(4):
            rows = pl.ds(part * 64, 64)
            total = upstream[cell, rows, :].astype(F32) + norm_back(
                wide[rows, :], gains_ref[1:2, :], cell, rows, normed_2, scale_2, 1
            )
            d_mid[rows, :] = total
            deltas_ref[some(cell, part), 3840:4608] = total.astype(BF16)

    def back_out(cell):
        d_branch = deltas_ref[whole(cell), 3840:4608]
        for tile in range(3):
            d_mixed[:, tile * 256:tile * 256 + 256] = dot_nt(
                d_branch, wo[tile * 256:tile * 256 + 256, :]
            ).astype(BF16)

    def attention_back(cell):
        def attend_back(pair, carry):
            start = pair * 128
            queries = stacked(deltas_ref[whole(cell), columns(start + 4608)])
            key_rows = deltas_ref[whole(cell), columns(start + 5376)]
            d_out = stacked(d_mixed[:, columns(start)])
            soft = probs[cell, pair]
            d_values = dot_tn(soft, d_out)
            d_soft = dot_nt(d_out, deltas_ref[whole(cell), columns(start + 6144)])
            soft = soft.astype(F32)
            inner = jnp.sum(soft * d_soft, axis=-1, keepdims=True)
            d_scores = (soft * (d_soft - inner)).astype(BF16)
            d_queries = unstacked(dot(d_scores, key_rows)) * HD ** -0.5
            d_keys = dot_tn(d_scores, queries)
            deltas_ref[whole(cell), columns(start + 4608)] = d_queries.astype(BF16)
            deltas_ref[whole(cell), columns(start + 5376)] = d_keys.astype(BF16)
            deltas_ref[whole(cell), columns(start + 6144)] = d_values.astype(BF16)
            return carry

        lax.fori_loop(0, pairs, attend_back, 0, unroll=True)

    def back_qkv(cell):
        d_qkv = deltas_ref[whole(cell), 4608:6912]
        for tile in range(3):
            wide[:, tile * 256:tile * 256 + 256] = dot_nt(
                d_qkv, wq[tile * 256:tile * 256 + 256, :]
            )

    def norm_source_back(cell):
        for part in range(4):
            rows = pl.ds(part * 64, 64)
            total = d_mid[rows, :] + norm_back(
                wide[rows, :], gains_ref[0:1, :], cell, rows, normed_1, scale_1, 0
            )

            relayed[cell, rows, :] = total.astype(BF16)

            @pl.when(on_first)
            def _():
                ends_out[cell, rows, :] = total

    def weights_here(t, at):
        @pl.when(t == 0)
        def _():
            loads[at].wait()

    def forward(t, cell):
        @pl.when(on_second)
        def _():
            relay_copy(cell, source).wait_recv()

        norm_source(cell)

        @pl.when(t == 0)
        def _():
            loads[0].wait()
            for load in loads[1:]:
                load.start()

        project_qkv(cell)
        attention(cell)
        weights_here(t, 1)
        project_out(cell)
        norm_mid(cell)
        weights_here(t, 2)
        go_up(cell)
        weights_here(t, 3)
        go_down(cell)

        @pl.when(on_second)
        def _():
            ends_copy(cell).start()

        @pl.when(on_first)
        def _():
            @pl.when(t == 0)
            def _():
                pl.semaphore_wait(barrier, len(met))

            relay_copy(cell, source).start()

    def nothing(at):
        del at

    def backward(cell, between=nothing):
        back_down(cell)
        between(0)
        back_up(cell)
        between(1)
        norm_mid_back(cell)
        back_out(cell)
        between(2)
        attention_back(cell)
        between(3)
        back_qkv(cell)
        norm_source_back(cell)

        @pl.when(on_second)
        def _():
            relay_copy(cell, upstream).start()

        @pl.when(on_first)
        def _():
            ends_copy(cell).start()

        between(4)

    def receive_gradient(cell):
        @pl.when(on_first)
        def _():
            relay_copy(cell, source).wait_send()
            relay_copy(cell, upstream).wait_recv()

        deltas_ref[whole(cell), 0:768] = upstream[cell]

    def step(t, carry):
        backwards = (1 - section) * (t // 2) + section * (t % 2)
        cell = (1 - section) * (t % 2) + section * (t // 2)

        @pl.when(backwards == 0)
        def _():
            forward(t, cell)

        @pl.when(backwards == 1)
        def _():
            receive_gradient(cell)
            backward(cell)

        return carry

    lax.fori_loop(0, 3 if scattering else 4, step, 0)

    if scattering:
        def gain_copy(at, device):
            return pltpu.make_async_remote_copy(
                src_ref=gain_held.at[min(at, 2)],
                dst_ref=gain_in.at[at],
                send_sem=gain_send.at[at],
                recv_sem=gain_recv.at[at],
                device_id=device,
                device_id_type=MESH,
            )

        inner = jnp.logical_or(z == 1, z == 2)
        outer = jnp.logical_or(z == 0, z == 3)
        near_device, far_device, mirror_device = z_devices
        leaving = (3 - z) // 3 * 48
        crossing = (2 - z) * 96
        crossing_in = (2 - z) * 48
        own_in = (z // 2) * (1 - z // 3) * 96

        def block(start, count=48):
            return pl.ds(pl.multiple_of(start, 16), count)

        def z_unit(i):
            return i * (EVERY + 1)

        def x_unit(j):
            return j + j // EVERY + 1

        def core_copy(k, room):
            return pltpu.make_async_remote_copy(
                src_ref=core_out.at[room], dst_ref=core_in.at[k],
                send_sem=core_send.at[k], recv_sem=core_recv.at[k],
                device_id=core_device, device_id_type=MESH,
            )

        def x_copy(j):
            return pltpu.make_async_remote_copy(
                src_ref=core_in.at[x_unit(j), block((1 - x) * 192, 192)], dst_ref=x_in.at[j],
                send_sem=x_send.at[j], recv_sem=x_recv.at[j],
                device_id=x_device, device_id_type=MESH,
            )

        def last_copy(i):
            return pltpu.make_async_remote_copy(
                src_ref=core_in.at[z_unit(i), block((1 - x) * 192 + z * 48)], dst_ref=last_in.at[i],
                send_sem=x_send.at[X_FIRST + i], recv_sem=x_recv.at[X_FIRST + i],
                device_id=x_device, device_id_type=MESH,
            )

        def x_line(j):
            return x_in.at[j], 0, j

        def z_lines(i):
            return [(core_in.at[z_unit(i)], side * 192, X_FIRST + 2 * i + side) for side in range(2)]

        def near_copy(line, from_outer):
            ref, base, slot = line
            if from_outer:
                source, target = ref.at[block(base + leaving, 144)], near_in.at[slot]
            else:
                source = ref.at[block(base + far_z[0] * 48)]
                target = near_in.at[slot, pl.ds(0, 48)]
            return pltpu.make_async_remote_copy(
                src_ref=source, dst_ref=target,
                send_sem=near_send.at[slot], recv_sem=near_recv.at[slot],
                device_id=near_device, device_id_type=MESH,
            )

        def far_copy(line, at):
            ref, base, slot = line
            target, device = ((far_z[2], mirror_device), (far_z[1], far_device))[at]
            return pltpu.make_async_remote_copy(
                src_ref=ref.at[block(base + target * 48)], dst_ref=far_in.at[slot],
                send_sem=far_send.at[slot, at], recv_sem=far_recv.at[slot],
                device_id=device, device_id_type=MESH,
            )

        def start_line(line):
            @pl.when(outer)
            def _():
                near_copy(line, True).start()

            @pl.when(inner)
            def _():
                near_copy(line, False).start()

        def pass_line(line):
            @pl.when(inner)
            def _():
                ref, base, slot = line
                near_copy(line, True).wait_recv()
                rows = block(base + crossing, 96)
                total = ref[rows, :].astype(F32) + near_in[slot, block(crossing_in, 96), :].astype(F32)
                ref[rows, :] = total.astype(BF16)
                far_copy(line, 0).start()
                far_copy(line, 1).start()

        def end_line(line):
            ref, base, slot = line

            @pl.when(outer)
            def _():
                near_copy(line, False).wait_recv()

            far_copy(line, 0).wait_recv()
            return (
                ref[block(base + z * 48), :].astype(F32)
                + near_in[slot, block(own_in), :].astype(F32)
                + far_in[slot].astype(F32)
            )

        def wait_line_sends(line):
            @pl.when(outer)
            def _():
                near_copy(line, True).wait_send()

            @pl.when(inner)
            def _():
                near_copy(line, False).wait_send()
                far_copy(line, 0).wait_send()
                far_copy(line, 1).wait_send()

        def form(k, room):
            down = (k < 12).astype(jnp.int32)
            left = down * (k // 3) + (1 - down) * (
                4 + (k >= 24).astype(jnp.int32) + (k >= 27).astype(jnp.int32)
            )
            right = down * (k % 3) + (1 - down) * (k - 9)
            delta = deltas_ref[:, columns(right * 256, 256)]
            away = turned[left, block((1 - core) * 384, 384), :]
            core_out[room] = dot(away, delta).astype(BF16)
            core_copy(k, room).start()
            own = turned[left, block(core * 384, 384), :]
            keep_core[room] = dot(own, delta)

        def form_z(i):
            @pl.when(i >= 1)
            def _():
                core_copy(z_unit(i - 1), HELD).wait_send()

            form(z_unit(i), HELD)

        def form_x(j):
            @pl.when(j >= HELD)
            def _():
                core_copy(x_unit(j - HELD), j % HELD).wait_send()

            form(x_unit(j), j % HELD)

        def over_core(k, room):
            core_copy(k, room).wait_recv()
            core_in[k] = (keep_core[room] + core_in[k].astype(F32)).astype(BF16)

        def over_core_z(i):
            over_core(z_unit(i), HELD)
            for line in z_lines(i):
                start_line(line)

        def over_core_x(j):
            over_core(x_unit(j), j % HELD)
            x_copy(j).start()

        def over_x(j):
            x_copy(j).wait_recv()
            own = core_in[x_unit(j), block(x * 192, 192), :].astype(F32)
            x_in[j] = (own + x_in[j].astype(F32)).astype(BF16)
            start_line(x_line(j))

        def pass_z(i):
            for line in z_lines(i):
                pass_line(line)

        def end_z(i):
            for ref, base, slot in z_lines(i):
                ref[block(base + z * 48), :] = end_line((ref, base, slot)).astype(BF16)
            last_copy(i).start()

        def store(k, total):
            @pl.when(k < 12)
            def _():
                rows = pl.ds(pl.multiple_of((k // 3) * 48, 8), 48)
                gd_out[rows, columns((k % 3) * 256, 256)] = total

            @pl.when(jnp.logical_and(k >= 12, k < 24))
            def _():
                gu_out[:, columns((k - 12) * 256, 256)] = total

            @pl.when(jnp.logical_and(k >= 24, k < 27))
            def _():
                go_out[:, columns((k - 24) * 256, 256)] = total

            @pl.when(k >= 27)
            def _():
                gq_out[:, columns((k - 27) * 256, 256)] = total

        def over_last(i):
            last_copy(i).wait_recv()
            own = core_in[z_unit(i), block(x * 192 + z * 48), :].astype(F32)
            store(z_unit(i), own + last_in[i].astype(F32))

        def end_x(j):
            store(x_unit(j), end_line(x_line(j)))

        def sent_x(j):
            x_copy(j).wait_send()
            wait_line_sends(x_line(j))

        def sent_z(i):
            for line in z_lines(i):
                wait_line_sends(line)
            last_copy(i).wait_send()

        share_copies = [
            pltpu.make_async_copy(vmem, hbm, out_sem.at[at])
            for at, (vmem, hbm) in enumerate(
                ((gd_out, gd_ref), (gu_out, gu_ref), (go_out, go_ref), (gq_out, gq_ref))
            )
        ]

        receive_gradient(1)

        @pl.when(on_first)
        def _():
            def early(t, carry):
                @pl.when(jnp.logical_and(t < EARLY, t % EVERY == 0))
                def _():
                    form_z(t // EVERY)

                @pl.when(t < EARLY)
                def _():
                    form_x(t)

                @pl.when(jnp.logical_and(t >= LAG_CORE, t % EVERY == LAG_CORE))
                def _():
                    over_core_z(t // EVERY)

                @pl.when(t >= LAG_CORE)
                def _():
                    over_core_x(t - LAG_CORE)

                return carry

            lax.fori_loop(0, EARLY + LAG_CORE, early, 0)

        def between(at):
            @pl.when(on_first)
            def _():
                for j in ((0,), (1, 2), (3,), (4,), (5,))[at]:
                    over_x(j)
                if at == 1:
                    pass_z(0)
                for j in ((), (), (0,), (1, 2), (3,))[at]:
                    pass_line(x_line(j))
                if at == 3:
                    end_z(0)

        backward(1, between)

        gain_held[0] = gain_ref[...]
        gain_copy(0, core_device).start()

        def later(t, carry):
            def at(lag, low, high, work):
                @pl.when(jnp.logical_and(t >= lag + low, t < lag + high))
                def _():
                    work(t - lag)

            def at_z(lag, work):
                @pl.when(jnp.logical_and(
                    (t - lag) % EVERY == 0, jnp.logical_and(t >= lag, t < lag + X_FIRST)
                ))
                def _():
                    work((t - lag) // EVERY)

            at_z(0, form_z)
            at(0, 0, X_FIRST, form_x)

            @pl.when(jnp.logical_or(on_second, t >= EARLY + LAG_CORE))
            def _():
                at_z(LAG_CORE, over_core_z)
                at(LAG_CORE, 0, X_FIRST, over_core_x)

            at(LAG_X, 0, X_FIRST, over_x)
            at_z(LAG_Z_NEAR, pass_z)
            at(LAG_NEAR, 0, X_FIRST, lambda j: pass_line(x_line(j)))
            at_z(LAG_Z_FAR, end_z)
            at_z(LAG_Z_X, over_last)
            at(LAG_FAR, 0, X_FIRST, end_x)
            at(LAG_SENT, 0, X_FIRST, sent_x)
            at_z(LAG_SENT, sent_z)
            for copy, last in zip(share_copies, SHARE_ENDS):
                @pl.when(t == last)
                def _():
                    copy.start()

            @pl.when(t == 16)
            def _():
                gain_copy(0, core_device).wait()
                gain_held[1] = gain_held[0] + gain_in[0]
                gain_copy(1, x_device).start()

            @pl.when(t == 22)
            def _():
                gain_copy(1, x_device).wait()
                gain_held[2] = gain_held[1] + gain_in[1]
                for j in range(3):
                    gain_copy(2 + j, z_devices[j]).start()

            @pl.when(t == 28)
            def _():
                for j in range(3):
                    gain_copy(2 + j, z_devices[j]).wait()
                total_gains = gain_held[2] + gain_in[2] + gain_in[3] + gain_in[4]
                chosen = (
                    lax.broadcasted_iota(jnp.int32, (768, 48), 0)
                    == lax.broadcasted_iota(jnp.int32, (768, 48), 1) + place * 48
                ).astype(F32)
                own_gains = jnp.dot(
                    total_gains, chosen, precision=lax.Precision.HIGHEST, preferred_element_type=F32
                )
                gg_ref[...] = own_gains[:2]

            return carry

        lax.fori_loop((1 - section) * EARLY, X_FIRST + LAG_FAR, later, 0)
        share_copies[3].start()

        core_copy(z_unit(Z_FIRST - 1), HELD).wait_send()
        for j in range(X_FIRST - HELD, X_FIRST):
            core_copy(x_unit(j), j % HELD).wait_send()
        for j in range(X_FIRST + LAG_FAR - LAG_SENT, X_FIRST):
            sent_x(j)
        for i in range((X_FIRST + LAG_FAR - 1 - LAG_SENT) // EVERY + 1, Z_FIRST):
            sent_z(i)
        for copy in share_copies:
            copy.wait()

    for cell in range(2):
        ends_copy(cell).wait()

    @pl.when(on_second)
    def _():
        for cell in range(2):
            relay_copy(cell, upstream).wait_send()


def run_kernel(scattering, acts, counts, cotangent, gains, weights):
    cells, length, width = acts.shape
    vmem = pl.BlockSpec(memory_space=pltpu.VMEM)
    anywhere = pl.BlockSpec(memory_space=pl.ANY)
    dma = pltpu.SemaphoreType.DMA
    held = (
        ((7, 768, cells * length), BF16),
        ((cells * length, 6912), BF16),
        ((8, 768), F32),
    )
    shares = (((48, 2304), F32), ((48, 768), F32), ((48, 3072), F32), ((192, 768), F32), ((2, 48), F32))
    outs = (((cells, length, width), F32),) + (shares if scattering else held)
    first = [pltpu.VMEM(shape, kind) for shape, kind in held + shares[:4]] + [dma((4,))]
    scratch = (
        ((768, 2304), BF16),
        ((768, 768), BF16),
        ((768, 3072), BF16),
        ((3072, 768), BF16),
        ((cells, length, width), BF16),
        ((cells, length, width), BF16),
        ((cells, length, width), BF16),
        ((length, width), BF16),
        ((length, width), BF16),
        ((length, width), BF16),
        ((length, 3072), BF16),
        ((cells, HEADS // 2, 2 * length, length), BF16),
        ((cells, length, width), F32),
        ((cells, length, width), F32),
        ((cells, length, 128), F32),
        ((cells, length, 128), F32),
        ((length, width), F32),
        ((length, width), F32),
        ((cells, length, width), F32),
    )
    semaphores = [dma((4,)), dma(()), dma((2,)), dma((2,)), dma((2,))]
    travel = ()
    if scattering:
        travel = (
            ((HELD + 1, 384, 256), BF16),
            ((HELD + 1, 384, 256), F32),
            ((UNITS, 384, 256), BF16),
            ((X_FIRST, 192, 256), BF16),
            ((Z_FIRST, 48, 256), BF16),
            ((LINES, 144, 256), BF16),
            ((LINES, 48, 256), BF16),
            ((3, 8, 768), F32),
            ((5, 8, 768), F32),
        )
    travel_semaphores = [
        dma((UNITS,)), dma((UNITS,)), dma((UNITS,)), dma((UNITS,)),
        dma((LINES,)), dma((LINES,)), dma((LINES, 2)), dma((LINES,)),
        dma((5,)), dma((5,)),
    ] if scattering else []
    return pl.pallas_call(
        functools.partial(kernel, scattering),
        out_shape=tuple(jax.ShapeDtypeStruct(shape, kind) for shape, kind in outs),
        in_specs=[pl.BlockSpec(memory_space=pltpu.SMEM), vmem] + [anywhere] * 6,
        out_specs=(anywhere,) + ((anywhere,) * 4 + (vmem,) if scattering else (vmem,) * 3),
        scratch_shapes=(first if scattering else [])
        + [pltpu.VMEM(shape, kind) for shape, kind in scratch]
        + semaphores
        + [pltpu.VMEM(shape, kind) for shape, kind in travel]
        + travel_semaphores,
        compiler_params=pltpu.CompilerParams(
            collective_id=1 if scattering else 2,
            has_side_effects=True,
            vmem_limit_bytes=VMEM_BYTES,
        ),
        name="relay_layers",
    )(counts, gains, acts, cotangent, *weights)


def hand_over_kernel(*refs):
    count = (len(refs) - 2) // 3
    sources, targets, rooms = (refs[at * count:(at + 1) * count] for at in range(3))
    read_sem, write_sem = refs[-2:]
    pieces = []
    for source, target, room in zip(sources, targets, rooms):
        if len(source.shape) == 3:
            for cell in range(source.shape[0]):
                pieces.append((source.at[cell], room.at[cell], target.at[cell]))
        else:
            pieces.append((source, room, target))
    reads, writes = [], []
    for at, (source, room, target) in enumerate(pieces):
        reads.append(pltpu.make_async_copy(source, room, read_sem.at[at]))
        writes.append(pltpu.make_async_copy(room, target, write_sem.at[at]))
    for read in reads:
        read.start()
    for read, write in zip(reads, writes):
        read.wait()
        write.start()
    for write in writes:
        write.wait()


def hand_over(*arrays):
    anywhere = pl.BlockSpec(memory_space=pl.ANY)
    sem = pltpu.SemaphoreType.DMA((len(arrays) + 1,))
    return pl.pallas_call(
        hand_over_kernel,
        out_shape=tuple(jax.ShapeDtypeStruct(array.shape, array.dtype) for array in arrays),
        in_specs=[anywhere] * len(arrays),
        out_specs=(anywhere,) * len(arrays),
        scratch_shapes=[pltpu.VMEM(array.shape, array.dtype) for array in arrays] + [sem, sem],
        name="hand_over",
    )(*arrays)


def plain_scattered(turned, deltas, d_gains):
    d_low, d_up = deltas[:, :768], deltas[:, 768:3840]
    d_branch, d_qkv = deltas[:, 3840:4608], deltas[:, 4608:]
    rows = turned.shape[2]
    shares = turned.reshape(7, 2, 2, 4, 48, rows).transpose(3, 2, 1, 0, 4, 5).reshape(16, 7, 48, rows)
    scatter = functools.partial(lax.psum_scatter, axis_name="dp", scatter_dimension=0, tiled=True)
    return (
        lax.psum_scatter(d_gains[:2], "dp", scatter_dimension=1, tiled=True),
        scatter(dot(shares[:, 6].reshape(768, rows), d_qkv)),
        scatter(dot(shares[:, 5].reshape(768, rows), d_branch)),
        scatter(dot(shares[:, 4].reshape(768, rows), d_up)),
        scatter(dot(shares[:, :4].reshape(3072, rows), d_low)),
    )


def body(acts, counts, cotangent, norm_gains, w_qkv, w_out, w_up, w_down):
    weights = (w_qkv[0], w_out[0], w_up[0], w_down[0])
    if lax.axis_size("dp") == 16:
        ends, *shares, d_gains = hand_over(
            *run_kernel(True, acts, counts, cotangent, norm_gains[0], weights)
        )
        shares = [d_gains] + shares
    else:
        ends, *held = run_kernel(False, acts, counts, cotangent, norm_gains[0], weights)
        shares = plain_scattered(*held)
    return (ends[None],) + tuple(share[None] for share in shares)


def solution(mesh):
    placed = (
        P("dp", None, None),
        P("dp"),
        P("dp", None, None),
        P("section", None, None),
        P("section", None, None),
        P("section", None, None),
        P("section", None, None),
        P("section", None, None),
    )
    return jax.shard_map(
        body,
        mesh=mesh,
        in_specs=placed,
        out_specs=(
            P("section", "dp", None, None),
            P("section", None, "dp"),
            P("section", "dp", None),
            P("section", "dp", None),
            P("section", "dp", None),
            P("section", "dp", None),
        ),
        check_vma=False,
    )
```
